512 devices in a mesh: inl: 16 (over z_hi, y, core), xl: 8 (over z_lo), gz: 4 (over x).
Axes of the slice: x: 4, y: 4, z: 16 (z_hi: 2, z_lo: 8; z = z_hi * 8 + z_lo), core: 2. Of those that a mesh axis runs over, the one named last changes fastest.
Arguments:
- wave_p: float32 [32, 128, 1024], P('gz', 'inl', 'xl'), may hold values from -6 to 6
- wave_p_old: float32 [32, 128, 1024], P('gz', 'inl', 'xl'), may hold values from -6 to 6
- wave_q: float32 [32, 128, 1024], P('gz', 'inl', 'xl'), may hold values from -6 to 6
- wave_q_old: float32 [32, 128, 1024], P('gz', 'inl', 'xl'), may hold values from -6 to 6
- courant_square: float32 [32, 128, 1024], P('gz', 'inl', 'xl'), may hold values from 0.05 to 0.11
- thomsen_epsilon: float32 [32, 128, 1024], P('gz', 'inl', 'xl'), may hold values from 0.1 to 0.35
- thomsen_delta: float32 [32, 128, 1024], P('gz', 'inl', 'xl'), may hold values from 0.02 to 0.2
- tilt_angle: float32 [32, 128, 1024], P('gz', 'inl', 'xl'), may hold values from -3.140625 to 3.140625
- azimuth: float32 [32, 128, 1024], P('gz', 'inl', 'xl'), may hold values from -3.140625 to 3.140625
- shear_ratio: float32 [32, 128, 1024], P('gz', 'inl', 'xl'), may hold values from 0.1 to 0.6
- damping: float32 [32, 128, 1024], P('gz', 'inl', 'xl'), may hold values from 0 to 0.3
- trace_samples: float32 [131072, 256], P(('inl', 'xl', 'gz')), may hold values from -6 to 6
- resample_filter: float32 [2, 256], replicated, may hold values from -0.375 to 0.375
- line_gain: float32 [64], replicated, may hold values from 0.5 to 4
- receiver_inline: int32 [131072], P(('inl', 'xl', 'gz')), may hold values from 0 to 127, as said below
- receiver_crossline: int32 [131072], P(('inl', 'xl', 'gz')), may hold values from 0 to 1023, as said below
- shot_line: int32 [131072], P(('inl', 'xl', 'gz')), may hold values from 0 to 63
Outputs:
- next_p: float32 [32, 128, 1024], P('gz', 'inl', 'xl')
- next_q: float32 [32, 128, 1024], P('gz', 'inl', 'xl')
- prior_p: float32 [32, 128, 1024], P('gz', 'inl', 'xl')
- prior_q: float32 [32, 128, 1024], P('gz', 'inl', 'xl')
The draws below stay inside these ranges and needn't reach their ends.
Inputs may be any that keep to these rules, and one draw needn't show every extreme that they name: In each aligned block of 256 traces (the traces of one device), at most 4 traces lie in one device column (equal receiver_inline // 8 and receiver_crossline // 128); in every block some column holds exactly 4. `receiver_crossline`: see receiver_inline.
All inputs are finite; a program needn't handle non-finite values.
Results may differ from the reference program's by a relative error of at most 0.000075.
Values sent between devices are 32-bit elements; how exact they have to be, the bound alone decides.
A program may use at most 64 MiB of HBM per device.

```python
import math
import jax
import jax.numpy as jnp
import numpy as np
from jax import lax

CX = 8
CY = 128
REC_DEV = 256
SAMPLES = 256
STEPS = 2
LINES = 64
NZ = 32
NX = 128
NY = 1024
COLUMNS = 128
CAP = 4
RECS = 131072


def receiver_cells(key):
    blocks = RECS // REC_DEV
    base = jax.random.fold_in(key, 11)
    keys = jax.random.split(base, 5)
    sizes = jax.random.randint(keys[0], (blocks, REC_DEV), (CAP + 1) // 2, CAP + 1)
    sizes = sizes.at[:, 0].set(CAP)
    ends = jnp.cumsum(sizes, axis=1)
    positions = jnp.arange(REC_DEV, dtype=jnp.int32)
    group = jax.vmap(lambda edge: jnp.searchsorted(edge, positions, side='right'))(ends).astype(jnp.int32)
    orders = jax.vmap(lambda sub: jax.random.permutation(sub, COLUMNS))(jax.random.split(keys[1], blocks)).astype(jnp.int32)
    column = jnp.take_along_axis(orders, group, axis=1)
    shuffles = jax.vmap(lambda sub: jax.random.permutation(sub, REC_DEV))(jax.random.split(keys[2], blocks)).astype(jnp.int32)
    column = jnp.take_along_axis(column, shuffles, axis=1)
    per_row = NY // CY
    inline_cell = column // per_row * CX + jax.random.randint(keys[3], (blocks, REC_DEV), 0, CX)
    cross_cell = column % per_row * CY + jax.random.randint(keys[4], (blocks, REC_DEV), 0, CY)
    return (inline_cell.reshape(-1).astype(jnp.int32), cross_cell.reshape(-1).astype(jnp.int32))


def draw_receiver_inline(key, part):
    return receiver_cells(key)[0]


def draw_receiver_crossline(key, part):
    return receiver_cells(key)[1]


def with_ends(result, stream_key, low, high):
    spot = [jax.random.randint(jax.random.fold_in(stream_key, axis), (), 0, length) for axis, length in enumerate(result.shape)]
    main_axis = result.shape.index(max(result.shape))
    beside = spot[:main_axis] + [(spot[main_axis] + 1) % result.shape[main_axis]] + spot[main_axis + 1:]
    return result.at[tuple(spot)].set(low).at[tuple(beside)].set(high)


def level_of(stream_key, dims, pieces, low, largest):
    factor_of = 1.0
    for dim, shards_of in pieces:
        steps = jax.random.uniform(jax.random.fold_in(jax.random.fold_in(stream_key, 6), dim), (shards_of,), jnp.float32, low / len(pieces), largest / len(pieces))
        factor_of = factor_of * jnp.repeat(jnp.exp(steps), dims[dim] // shards_of).reshape((-1,) + (1,) * (len(dims) - 1 - dim))
    return factor_of


def rank_bounds(count, lean):
    portions = [(1 << 20) // math.isqrt(standing ** lean) + 1 for standing in range(1, count + 1)]
    scale = 1 + sum(portions) // (1 << 30)
    return np.cumsum(np.array([max(1, weight // scale) for weight in portions]))


def ranked(key, shape, amount, skew):
    grid = rank_bounds(amount, skew)
    lot = jax.random.randint(jax.random.fold_in(key, 1), shape, 0, int(grid[amount - 1]))
    rank = jnp.searchsorted(jnp.asarray(grid, jnp.int32), lot, side="right")
    return jax.random.permutation(jax.random.fold_in(key, 2), amount)[rank].astype(jnp.int32)


def gaussian(key, extent, scale, bound, cuts=(), kind=jnp.bfloat16):
    entries = jax.random.normal(key, extent, jnp.float32) * scale
    if len(cuts) > 0:
        entries = level_of(key, extent, cuts, -0.22, 0.18) * entries
    return jnp.clip(entries, min=-bound, max=bound).astype(kind)


def setup_inputs(seed: int = 0) -> dict:
    key_list = jax.random.split(jax.random.key(seed), 18)
    wave_p = gaussian(key_list[0], (NZ, NX, NY), 1.0, 6.0, ((0, 4), (1, 16), (2, 8)), jnp.float32)
    wave_p_old = gaussian(key_list[1], (NZ, NX, NY), 1.0, 6.0, ((0, 4), (1, 16), (2, 8)), jnp.float32)
    wave_q = gaussian(key_list[2], (NZ, NX, NY), 1.0, 6.0, ((0, 4), (1, 16), (2, 8)), jnp.float32)
    wave_q_old = gaussian(key_list[3], (NZ, NX, NY), 1.0, 6.0, ((0, 4), (1, 16), (2, 8)), jnp.float32)
    courant_square = jnp.clip(0.05 + 0.06 * jax.random.uniform(key_list[4], (NZ, NX, NY), jnp.float32) ** level_of(key_list[4], (NZ, NX, NY), ((0, 4), (1, 16), (2, 8)), -0.2, 0.2), 0.05, 0.11)
    thomsen_epsilon = jnp.clip(0.1 + 0.25 * jax.random.uniform(key_list[5], (NZ, NX, NY), jnp.float32) ** level_of(key_list[5], (NZ, NX, NY), ((0, 4), (1, 16), (2, 8)), -0.2, 0.2), 0.1, 0.35)
    thomsen_delta = jnp.clip(0.02 + 0.18 * jax.random.uniform(key_list[6], (NZ, NX, NY), jnp.float32) ** level_of(key_list[6], (NZ, NX, NY), ((0, 4), (1, 16), (2, 8)), -0.2, 0.2), 0.02, 0.2)
    tilt_angle = jnp.clip(jax.random.uniform(key_list[7], (NZ, NX, NY), jnp.float32, -3.140625, 3.140625), -3.140625, 3.140625)
    azimuth = jnp.clip(jax.random.uniform(key_list[8], (NZ, NX, NY), jnp.float32, -3.140625, 3.140625), -3.140625, 3.140625)
    shear_ratio = jnp.clip(0.1 + 0.5 * jax.random.uniform(key_list[9], (NZ, NX, NY), jnp.float32) ** level_of(key_list[9], (NZ, NX, NY), ((0, 4), (1, 16), (2, 8)), -0.2, 0.2), 0.1, 0.6)
    damping = jnp.clip(0.3 * jax.random.uniform(key_list[10], (NZ, NX, NY), jnp.float32) ** level_of(key_list[10], (NZ, NX, NY), ((0, 4), (1, 16), (2, 8)), -0.2, 0.2), 0.0, 0.3)
    trace_samples = gaussian(key_list[11], (RECS, SAMPLES), 1.0, 6.0, ((0, 512),), jnp.float32)
    resample_filter = gaussian(key_list[12], (STEPS, SAMPLES), SAMPLES ** -0.5, 0.375, (), jnp.float32)
    line_gain = jnp.clip(jnp.exp(jax.random.uniform(key_list[13], (LINES,), jnp.float32, math.log(0.5), math.log(4.0))), 0.5, 4.0)
    receiver_inline = draw_receiver_inline(jax.random.fold_in(key_list[17], 71), 0)
    receiver_crossline = draw_receiver_crossline(jax.random.fold_in(key_list[17], 71), 0)
    shot_line = with_ends(ranked(key_list[16], (RECS,), LINES, 2), jax.random.fold_in(key_list[16], 3), 0, LINES - 1).astype(jnp.int32)
    return {"wave_p": wave_p, "wave_p_old": wave_p_old, "wave_q": wave_q, "wave_q_old": wave_q_old, "courant_square": courant_square, "thomsen_epsilon": thomsen_epsilon, "thomsen_delta": thomsen_delta, "tilt_angle": tilt_angle, "azimuth": azimuth, "shear_ratio": shear_ratio, "damping": damping, "trace_samples": trace_samples, "resample_filter": resample_filter, "line_gain": line_gain, "receiver_inline": receiver_inline, "receiver_crossline": receiver_crossline, "shot_line": shot_line}


second_coef = (-205.0 / 72.0, 8.0 / 5.0, -1.0 / 5.0, 8.0 / 315.0, -1.0 / 560.0)
first_coef = (0.0, 4.0 / 5.0, -1.0 / 5.0, 4.0 / 105.0, -1.0 / 280.0)


def derivatives(padded):
    depth = padded.shape[-3] - 8
    across = padded.shape[-2] - 8
    along = padded.shape[-1] - 8

    def piece(dz, dx, dy):
        return padded[..., 4 + dz:4 + dz + depth, 4 + dx:4 + dx + across, 4 + dy:4 + dy + along]

    center = piece(0, 0, 0)
    u_zz = second_coef[0] * center
    u_xx = second_coef[0] * center
    u_yy = second_coef[0] * center
    for k in range(1, 5):
        u_zz = u_zz + second_coef[k] * (piece(k, 0, 0) + piece(-k, 0, 0))
        u_xx = u_xx + second_coef[k] * (piece(0, k, 0) + piece(0, -k, 0))
        u_yy = u_yy + second_coef[k] * (piece(0, 0, k) + piece(0, 0, -k))
    grad_x = first_coef[1] * (padded[..., :, 5:5 + across, :] - padded[..., :, 3:3 + across, :])
    grad_y = first_coef[1] * (padded[..., :, 4:4 + across, 5:5 + along] - padded[..., :, 4:4 + across, 3:3 + along])
    for k in range(2, 5):
        grad_x = grad_x + first_coef[k] * (padded[..., :, 4 + k:4 + k + across, :] - padded[..., :, 4 - k:4 - k + across, :])
        grad_y = grad_y + first_coef[k] * (padded[..., :, 4:4 + across, 4 + k:4 + k + along] - padded[..., :, 4:4 + across, 4 - k:4 - k + along])
    u_xy = first_coef[1] * (grad_x[..., 4:4 + depth, :, 5:5 + along] - grad_x[..., 4:4 + depth, :, 3:3 + along])
    u_xz = first_coef[1] * (grad_x[..., 5:5 + depth, :, 4:4 + along] - grad_x[..., 3:3 + depth, :, 4:4 + along])
    u_yz = first_coef[1] * (grad_y[..., 5:5 + depth, :, :] - grad_y[..., 3:3 + depth, :, :])
    for k in range(2, 5):
        u_xy = u_xy + first_coef[k] * (grad_x[..., 4:4 + depth, :, 4 + k:4 + k + along] - grad_x[..., 4:4 + depth, :, 4 - k:4 - k + along])
        u_xz = u_xz + first_coef[k] * (grad_x[..., 4 + k:4 + k + depth, :, 4:4 + along] - grad_x[..., 4 - k:4 - k + depth, :, 4:4 + along])
        u_yz = u_yz + first_coef[k] * (grad_y[..., 4 + k:4 + k + depth, :, :] - grad_y[..., 4 - k:4 - k + depth, :, :])
    return u_zz, u_xx, u_yy, u_xy, u_xz, u_yz


def anisotropy(tilt_angle, azimuth):
    sin_t = jnp.sin(tilt_angle)
    cos_t = jnp.cos(tilt_angle)
    sin_f = jnp.sin(azimuth)
    cos_f = jnp.cos(azimuth)
    a_xx = sin_t * sin_t * cos_f * cos_f
    a_yy = sin_t * sin_t * sin_f * sin_f
    a_zz = cos_t * cos_t
    a_xy = 2.0 * sin_t * sin_t * sin_f * cos_f
    a_xz = 2.0 * sin_t * cos_t * cos_f
    a_yz = 2.0 * sin_t * cos_t * sin_f
    return a_xx, a_yy, a_zz, a_xy, a_xz, a_yz


def advance(padded, current, previous, fields, coefs, plane):
    courant, eps_field, delta_field, shear, damp = fields
    a_xx, a_yy, a_zz, a_xy, a_xz, a_yz = coefs
    u_zz, u_xx, u_yy, u_xy, u_xz, u_yz = derivatives(padded)
    h_one = a_xx * u_xx + a_yy * u_yy + a_zz * u_zz + a_xy * u_xy + a_xz * u_xz + a_yz * u_yz
    h_two = u_xx + u_yy + u_zz - h_one
    wave_a = current[0]
    wave_b = current[1]
    old_a = previous[0]
    old_b = previous[1]
    new_a = 2.0 * wave_a - old_a + courant * ((1.0 + 2.0 * eps_field) * h_two[0] + h_one[1] + shear * (h_one[0] - h_one[1])) - damp * (wave_a - old_a)
    new_b = 2.0 * wave_b - old_b + courant * ((1.0 + 2.0 * delta_field) * h_two[0] + h_one[1] + shear * (h_two[1] - h_two[0])) - damp * (wave_b - old_b)
    new_a = new_a.at[0].add(plane)
    new_b = new_b.at[0].add(plane)
    return jnp.stack([new_a, new_b])


def reference(wave_p, wave_p_old, wave_q, wave_q_old, courant_square, thomsen_epsilon, thomsen_delta, tilt_angle, azimuth, shear_ratio, damping, trace_samples, resample_filter, line_gain, receiver_inline, receiver_crossline, shot_line):
    gains = line_gain[shot_line.astype(jnp.int32)]
    amplitude = jnp.dot(trace_samples, resample_filter.T, precision=lax.Precision.HIGHEST) * gains[:, None]
    target = (receiver_inline * NY + receiver_crossline).astype(jnp.int32)
    planes = jnp.zeros((STEPS, NX * NY), jnp.float32).at[:, target].add(amplitude.T)
    planes = planes.reshape(STEPS, NX, NY)
    coefs = anisotropy(tilt_angle, azimuth)
    fields = (courant_square, thomsen_epsilon, thomsen_delta, shear_ratio, damping)
    current = jnp.stack([wave_p, wave_q])
    previous = jnp.stack([wave_p_old, wave_q_old])
    for step in range(STEPS):
        padded = jnp.pad(current, ((0, 0), (4, 4), (4, 4), (4, 4)))
        newer = advance(padded, current, previous, fields, coefs, planes[step])
        previous = current
        current = newer
    return current[0], current[1], previous[0], previous[1]
```

```python
import functools

import jax
import jax.numpy as jnp
from jax import lax
from jax.experimental import pallas as pl
from jax.experimental.pallas import tpu as pltpu
from jax.sharding import PartitionSpec as P

MESH = pl.DeviceIdType.MESH
second_coef = (-205.0 / 72.0, 8.0 / 5.0, -1.0 / 5.0, 8.0 / 315.0, -1.0 / 560.0)
first_coef = (0.0, 4.0 / 5.0, -1.0 / 5.0, 4.0 / 105.0, -1.0 / 280.0)

OFFSETS = (
    [(d, 0, 0) for d in (1, -1)]
    + [(d, 0, e) for d in (1, -1) for e in (1, -1)]
    + [(d, e, 0) for d in (1, -1) for e in (1, -1)]
    + [(0, d, e) for d in (1, -1) for e in (1, -1)]
    + [(0, d, 0) for d in (1, -1)]
    + [(0, 0, d) for d in (1, -1)]
)
RING = 16
GROUP = 8
SLOTS = 4
WORDS = 16


def iota(shape, axis):
    return lax.broadcasted_iota(jnp.int32, shape, axis)


def shifted(body, halo, axis):
    size = body.shape[axis]
    place = iota(body.shape, axis)
    above = [pltpu.roll(jnp.where(place < k, halo, body), size - k, axis) for k in range(1, 5)]
    below = [pltpu.roll(jnp.where(place >= size - k, halo, body), k, axis) for k in range(1, 5)]
    return above, below


def slope(above, below):
    total = first_coef[1] * (above[0] - below[0])
    for k in range(2, 5):
        total = total + first_coef[k] * (above[k - 1] - below[k - 1])
    return total


def bend(center, above, below):
    total = second_coef[0] * center
    for k in range(1, 5):
        total = total + second_coef[k] * (above[k - 1] + below[k - 1])
    return total


def kernel(sizes, *refs):
    n_inl, n_xl, n_gz = sizes
    (
        wave_p,
        wave_p_old,
        wave_q,
        wave_q_old,
        courant,
        epsilon,
        delta,
        tilt,
        azimuth,
        shear,
        damping,
        samples,
        weights,
        gain,
        inline,
        crossline,
        shot,
        next_p,
        next_q,
        prior_p,
        prior_q,
        body,
        side,
        packed,
        parcel,
        edge_y,
        edge_xy,
        old,
        field,
        coef,
        trace,
        small_w,
        small_g,
        small_r,
        letters,
        mail,
        bundle,
        heap,
        plane,
        result,
        load_sem,
        store_sem,
        send_sem,
        recv_sem,
        letter_send,
        letter_recv,
        bundle_send,
        bundle_recv,
    ) = refs
    i = lax.axis_index("inl")
    j = lax.axis_index("xl")
    g = lax.axis_index("gz")
    depth, across, along = 8, 8, 128
    half = n_inl // 2
    ring = 2 * n_xl
    high, low = i // half, i % half
    level = high * n_xl + j

    loads = [
        (wave_p, body.at[0, 0, pl.ds(4, depth)]),
        (wave_q, body.at[0, 1, pl.ds(4, depth)]),
        (wave_p_old, old.at[0]),
        (wave_q_old, old.at[1]),
        (courant, field.at[0]),
        (epsilon, field.at[1]),
        (delta, field.at[2]),
        (tilt, field.at[3]),
        (azimuth, field.at[4]),
        (shear, field.at[5]),
        (damping, field.at[6]),
        (samples, trace),
        (weights, small_w),
        (gain, small_g),
        (inline, small_r.at[0]),
        (crossline, small_r.at[1]),
        (shot, small_r.at[2]),
    ]
    loads = [pltpu.make_async_copy(a, b, load_sem.at[k]) for k, (a, b) in enumerate(loads)]
    for copy in loads:
        copy.start()

    nothing = jnp.zeros((2, 4, across, along), jnp.float32)
    for turn in range(2):
        body[turn, :, 0:4] = nothing
        body[turn, :, 12:16] = nothing
        for k in range(4):
            side[turn, :, 4 * k : 4 * k + 4] = nothing
        packed[turn] = jnp.zeros((5, 2, across, along), jnp.float32)
    mail[...] = jnp.zeros((RING, along), jnp.float32)
    heap[...] = jnp.zeros((4, 2, GROUP, along), jnp.float32)

    def there(offset):
        d, e, f = offset
        ok = []
        for step, place, count in ((d, i, n_inl), (e, j, n_xl), (f, g, n_gz)):
            if step == 1:
                ok.append(place < count - 1)
            if step == -1:
                ok.append(place > 0)
        return functools.reduce(jnp.logical_and, ok)

    def device(offset):
        d, e, f = offset
        return (
            jnp.clip(i + d, 0, n_inl - 1),
            jnp.clip(j + e, 0, n_xl - 1),
            jnp.clip(g + f, 0, n_gz - 1),
        )

    def on_ring(k):
        place = lax.rem(level + k, ring)
        return (place // n_xl * half + low, lax.rem(place, n_xl), g)

    def in_group(k, layer):
        return (high * half + lax.rem(low + k, half), j, layer)

    barrier = pltpu.get_barrier_semaphore()
    count = jnp.int32(ring - 1) + jnp.where(g == 0, half - 1, half)
    for offset in OFFSETS:

        @pl.when(there(offset))
        def _(offset=offset):
            pl.semaphore_signal(barrier, inc=1, device_id=device(offset), device_id_type=MESH)

        count = count + there(offset).astype(jnp.int32)
    for k in range(1, ring):
        pl.semaphore_signal(barrier, inc=1, device_id=on_ring(k), device_id_type=MESH)

    @pl.when(g == 0)
    def _():
        for layer in range(n_gz):
            for k in range(half):
                if layer > 0 or k > 0:
                    pl.semaphore_signal(
                        barrier, inc=1, device_id=in_group(k, layer), device_id_type=MESH
                    )

    for copy in loads:
        copy.wait()

    def prepare(z, _):
        sin_t, cos_t = jnp.sin(field[3, z]), jnp.cos(field[3, z])
        sin_f, cos_f = jnp.sin(field[4, z]), jnp.cos(field[4, z])
        coef[0, z] = sin_t * sin_t * cos_f * cos_f
        coef[1, z] = sin_t * sin_t * sin_f * sin_f
        coef[2, z] = cos_t * cos_t
        coef[3, z] = 2.0 * sin_t * sin_t * sin_f * cos_f
        coef[4, z] = 2.0 * sin_t * cos_t * cos_f
        coef[5, z] = 2.0 * sin_t * cos_t * sin_f
        c, s = field[0, z], field[5, z]
        grow, lean = 1.0 + 2.0 * field[1, z], 1.0 + 2.0 * field[2, z]
        coef[6, z] = c * grow
        coef[7, z] = c * (s - grow)
        coef[8, z] = c * (1.0 - s)
        coef[9, z] = c * (lean - s)
        coef[10, z] = c * s
        coef[11, z] = 1.0 - field[6, z]
        return 0

    lax.fori_loop(0, depth, prepare, 0)

    n_traces = trace.shape[0]
    row, column, line = small_r[0], small_r[1], small_r[2]
    lines = small_g.shape[1]
    picked = jnp.where(iota((lines, n_traces), 0) == line, 1.0, 0.0).astype(jnp.float32)
    gains = jnp.dot(
        small_g[...],
        picked,
        precision=lax.Precision.HIGHEST,
        preferred_element_type=jnp.float32,
    )
    amplitude = (
        lax.dot_general(
            small_w[...],
            trace[...],
            (((1,), (1,)), ((), ())),
            precision=lax.Precision.HIGHEST,
            preferred_element_type=jnp.float32,
        )
        * gains
    )
    to_inl, to_xl = row >> 3, column >> 7
    cell = ((row & 7) << 7) + (column & 127) + 1
    to_high = jnp.where(to_inl >= half, 1, 0)
    to_low = to_inl - to_high * half
    owner = to_inl * n_xl + to_xl
    columns = n_inl * n_xl
    member = jnp.where(iota((columns, n_traces), 0) == owner, 1.0, 0.0).astype(jnp.float32)
    earlier = jnp.where(
        iota((n_traces, n_traces), 0) < iota((n_traces, n_traces), 1), 1.0, 0.0
    ).astype(jnp.float32)
    before = jnp.dot(
        member.astype(jnp.bfloat16),
        earlier.astype(jnp.bfloat16),
        preferred_element_type=jnp.float32,
    )
    rank = jnp.sum(member * before, axis=0, keepdims=True).astype(jnp.int32)
    hop = to_high * n_xl + to_xl - level
    hop = jnp.where(hop < 0, hop + ring, hop)
    block = to_low - low
    block = jnp.where(block < 0, block + half, block)
    word = block * WORDS + rank
    spot = iota((along, n_traces), 0)
    content = (
        jnp.where(spot == word, amplitude[0:1, :], 0.0)
        + jnp.where(spot == word + SLOTS, amplitude[1:2, :], 0.0)
        + jnp.where(spot == word + 2 * SLOTS, cell.astype(jnp.float32), 0.0)
    )
    address = jnp.where(iota((RING, n_traces), 0) == hop, 1.0, 0.0).astype(jnp.float32)
    written = lax.dot_general(
        address,
        content,
        (((1,), (1,)), ((), ())),
        precision=lax.Precision.HIGHEST,
        preferred_element_type=jnp.float32,
    )
    letters[...] = written
    mail[0:1, :] = written[0:1, :]

    lane = iota((across, along), 1)
    sub = iota((across, along), 0)

    def pack(turn):
        total = jnp.zeros((across, along), jnp.float32)
        for f in range(2):
            for z in range(depth):
                tile = f * depth + z
                moved = pltpu.roll(body[turn, f, 4 + z], (8 * tile + 4) % along, 1)
                total = jnp.where(lane // 8 == tile, moved, total)
        parcel[turn] = total

    pack(0)

    def copies(turn):
        out = []
        mine = body.at[turn]
        beside = side.at[turn]
        for number, offset in enumerate(OFFSETS):
            d, e, f = offset
            if e != 0:
                kind = 0
                if f != 0:
                    kind = 1 if f == 1 else 2
                if d != 0:
                    kind = 3 if d == 1 else 4
                source = parcel.at[turn]
                target = packed.at[turn, kind, 0 if e == 1 else 1]
            else:
                deep = {0: (4, 8, 4), 1: (8, 4, 0), -1: (4, 4, 12)}[f]
                if d == 0:
                    source = mine.at[:, pl.ds(deep[0], deep[1])]
                    target = mine.at[:, pl.ds(deep[2], deep[1])]
                else:
                    wide = pl.ds(4 if d == 1 else 0, 4)
                    source = mine.at[:, pl.ds(deep[0], deep[1]), wide]
                    target = beside.at[:, pl.ds(deep[2], deep[1]), wide]
            out.append(
                pltpu.make_async_remote_copy(
                    src_ref=source,
                    dst_ref=target,
                    send_sem=send_sem.at[turn, number],
                    recv_sem=recv_sem.at[turn, number],
                    device_id=device(offset),
                    device_id_type=MESH,
                )
            )
        return out

    def begin(turn):
        for offset, copy in zip(OFFSETS, copies(turn)):

            @pl.when(there(offset))
            def _(copy=copy):
                copy.start()

    def arrive(turn):
        for offset, copy in zip(OFFSETS, copies(turn)):

            @pl.when(there(tuple(-d for d in offset)))
            def _(copy=copy):
                copy.wait_recv()

    def depart(turn):
        for offset, copy in zip(OFFSETS, copies(turn)):

            @pl.when(there(offset))
            def _(copy=copy):
                copy.wait_send()

    def letter(k):
        return pltpu.make_async_remote_copy(
            src_ref=letters.at[pl.ds(k, 1)],
            dst_ref=mail.at[pl.ds(k, 1)],
            send_sem=letter_send.at[k],
            recv_sem=letter_recv.at[k],
            device_id=on_ring(k),
            device_id_type=MESH,
        )

    def parcel_of(k, layer):
        return pltpu.make_async_remote_copy(
            src_ref=bundle.at[:, pl.ds(k, 1)],
            dst_ref=heap.at[layer, :, pl.ds(k, 1)],
            send_sem=bundle_send.at[k],
            recv_sem=bundle_recv.at[layer, k],
            device_id=in_group(k, 0),
            device_id_type=MESH,
        )

    pl.semaphore_wait(barrier, count)
    begin(0)
    for k in range(1, ring):
        letter(k).start()

    for k in range(1, ring):
        letter(k).wait_recv()
    for t in range(2):
        got = mail[8 * t : 8 * t + 8, :]
        turned = jnp.zeros((GROUP, along), jnp.float32)
        for d in range(GROUP):
            moved = got if d == 0 else pltpu.roll(pltpu.roll(got, d, 0), along - WORDS * d, 1)
            turned = jnp.where(((sub - lane // WORDS) & 7) == d, moved, turned)
        bundle[t] = turned

    for k in range(half):
        if k > 0:
            parcel_of(k, g).start()
        else:

            @pl.when(g > 0)
            def _():
                parcel_of(0, g).start()

            @pl.when(g == 0)
            def _():
                heap[0, :, 0:1] = bundle[:, 0:1]

    def unpack(turn):
        def pair(kind):
            return jnp.where(lane % 8 < 4, packed[turn, kind, 0], packed[turn, kind, 1])

        plain = pair(0)
        deep = jnp.where((lane // 8) % 8 >= 4, pair(1), pair(2))
        wide = jnp.where(sub < 4, pair(4), pair(3))
        for f in range(2):
            for z in range(depth):
                turnback = (along - 4 - 8 * (f * depth + z)) % along
                edge_y[f, 4 + z] = pltpu.roll(plain, turnback, 1)
                edge_y[f, z - 4 if z >= 4 else 12 + z] = pltpu.roll(deep, turnback, 1)
                edge_xy[f, z] = pltpu.roll(wide, turnback, 1)

    def advance(turn, store):
        def layer(z, _):
            first, whole = [], []
            for f in range(2):
                center = body[turn, f, z + 4]
                beside = side[turn, f, z + 4]
                edge = edge_y[f, z + 4]
                above = [body[turn, f, z + 4 + k] for k in range(1, 5)]
                below = [body[turn, f, z + 4 - k] for k in range(1, 5)]
                u_zz = bend(center, above, below)
                grad_z = slope(above, below)
                grad_z_side = slope(
                    [side[turn, f, z + 4 + k] for k in range(1, 5)],
                    [side[turn, f, z + 4 - k] for k in range(1, 5)],
                )
                grad_z_edge = slope(
                    [edge_y[f, z + 4 + k] for k in range(1, 5)],
                    [edge_y[f, z + 4 - k] for k in range(1, 5)],
                )
                x_moves = shifted(center, beside, 0)
                u_xx = bend(center, *x_moves)
                grad_x = slope(*x_moves)
                grad_x_edge = slope(*shifted(edge, edge_xy[f, z], 0))
                u_yy = bend(center, *shifted(center, edge, 1))
                u_xy = slope(*shifted(grad_x, grad_x_edge, 1))
                u_xz = slope(*shifted(grad_z, grad_z_side, 0))
                u_yz = slope(*shifted(grad_z, grad_z_edge, 1))
                first.append(
                    coef[0, z] * u_xx
                    + coef[1, z] * u_yy
                    + coef[2, z] * u_zz
                    + coef[3, z] * u_xy
                    + coef[4, z] * u_xz
                    + coef[5, z] * u_yz
                )
                whole.append(u_xx + u_yy + u_zz)
            stay = coef[11, z]
            now_p, now_q = body[turn, 0, z + 4], body[turn, 1, z + 4]
            if turn == 0:
                was_p, was_q = old[0, z], old[1, z]
            else:
                was_p, was_q = body[0, 0, z + 4], body[0, 1, z + 4]
            mixed = coef[8, z] * first[1]
            new_p = (
                now_p
                + stay * (now_p - was_p)
                + (coef[6, z] * whole[0] + coef[7, z] * first[0] + mixed)
            )
            new_q = (
                now_q
                + stay * (now_q - was_q)
                + (coef[9, z] * (whole[0] - first[0]) + coef[10, z] * whole[1] + mixed)
            )
            store(z, new_p, new_q)
            return 0

        lax.fori_loop(0, depth, layer, 0)

    def keep(z, new_p, new_q):
        body[1, 0, z + 4] = new_p
        body[1, 1, z + 4] = new_q

    def finish(z, new_p, new_q):
        result[0, z] = new_p
        result[1, z] = new_q

    arrive(0)
    unpack(0)
    advance(0, keep)

    @pl.when(g == 0)
    def _():
        for layer in range(n_gz):
            for k in range(half):
                if layer > 0 or k > 0:
                    parcel_of(k, layer).wait_recv()
        place = iota((2 * GROUP, along), 1) % WORDS // SLOTS
        parts = [heap[layer].reshape(2 * GROUP, along) for layer in range(4)]

        def gather(kind):
            total = jnp.zeros((2 * GROUP, along), jnp.float32)
            for layer in range(4):
                shift = SLOTS * (layer - kind) % along
                moved = parts[layer] if shift == 0 else pltpu.roll(parts[layer], shift, 1)
                total = jnp.where(place == layer, moved, total)
            return total

        label = gather(2).astype(jnp.int32) - 1
        label_x, label_y = label >> 7, label & 127
        pieces = []
        for kind in range(2):
            rest = gather(kind)
            for _ in range(3):
                rounded = rest.astype(jnp.bfloat16).astype(jnp.float32)
                pieces.append(rounded)
                rest = rest - rounded
        total = jnp.zeros((6 * across, along), jnp.float32)
        for r in range(0, 2 * GROUP, 2):

            def flat(array):
                return jnp.concatenate([array[r : r + 1], array[r + 1 : r + 2]], axis=1)

            at_x = iota((across, 2 * along), 0) == flat(label_x)
            left = jnp.concatenate(
                [jnp.where(at_x, flat(piece), 0.0) for piece in pieces], axis=0
            )
            right = jnp.where(iota((along, 2 * along), 0) == flat(label_y), 1.0, 0.0)
            total = total + lax.dot_general(
                left.astype(jnp.bfloat16),
                right.astype(jnp.bfloat16),
                (((1,), (1,)), ((), ())),
                preferred_element_type=jnp.float32,
            )
        for k in range(2):
            part = total[24 * k : 24 * k + 24]
            plane[k] = part[0:8] + part[8:16] + part[16:24]
        for f in range(2):
            body[1, f, 4] = body[1, f, 4] + plane[0]

    pack(1)
    begin(1)
    stores = [
        pltpu.make_async_copy(body.at[1, 0, pl.ds(4, depth)], prior_p, store_sem.at[0]),
        pltpu.make_async_copy(body.at[1, 1, pl.ds(4, depth)], prior_q, store_sem.at[1]),
        pltpu.make_async_copy(result.at[0], next_p, store_sem.at[2]),
        pltpu.make_async_copy(result.at[1], next_q, store_sem.at[3]),
    ]
    stores[0].start()
    stores[1].start()
    arrive(1)
    unpack(1)
    advance(1, finish)

    @pl.when(g == 0)
    def _():
        for f in range(2):
            result[f, 0] = result[f, 0] + plane[1]

    stores[2].start()
    stores[3].start()
    depart(0)
    depart(1)
    for k in range(1, ring):
        letter(k).wait_send()
    for k in range(half):
        if k > 0:
            parcel_of(k, g).wait_send()
        else:

            @pl.when(g > 0)
            def _():
                parcel_of(0, g).wait_send()

    for copy in stores:
        copy.wait()


def local(sizes, *args):
    fields = args[:11]
    samples, weights, gain, row, column, line = args[11:]
    block = fields[0].shape
    n_traces = samples.shape[0]
    receivers = [ids.reshape(1, -1) for ids in (row, column, line)]
    f32 = jnp.float32
    return pl.pallas_call(
        functools.partial(kernel, sizes),
        out_shape=[jax.ShapeDtypeStruct(block, f32)] * 4,
        in_specs=[pl.BlockSpec(memory_space=pltpu.HBM)] * 17,
        out_specs=[pl.BlockSpec(memory_space=pltpu.HBM)] * 4,
        scratch_shapes=[
            pltpu.VMEM((2, 2, 16, 8, 128), f32),
            pltpu.VMEM((2, 2, 16, 8, 128), f32),
            pltpu.VMEM((2, 5, 2, 8, 128), f32),
            pltpu.VMEM((2, 8, 128), f32),
            pltpu.VMEM((2, 16, 8, 128), f32),
            pltpu.VMEM((2, 8, 8, 128), f32),
            pltpu.VMEM((2, 8, 8, 128), f32),
            pltpu.VMEM((7, 8, 8, 128), f32),
            pltpu.VMEM((12, 8, 8, 128), f32),
            pltpu.VMEM(samples.shape, f32),
            pltpu.VMEM(weights.shape, f32),
            pltpu.VMEM((1, gain.shape[0]), f32),
            pltpu.VMEM((3, 1, n_traces), jnp.int32),
            pltpu.VMEM((RING, 128), f32),
            pltpu.VMEM((RING, 128), f32),
            pltpu.VMEM((2, GROUP, 128), f32),
            pltpu.VMEM((4, 2, GROUP, 128), f32),
            pltpu.VMEM((2, 8, 128), f32),
            pltpu.VMEM((2, 8, 8, 128), f32),
            pltpu.SemaphoreType.DMA((17,)),
            pltpu.SemaphoreType.DMA((4,)),
            pltpu.SemaphoreType.DMA((2, len(OFFSETS))),
            pltpu.SemaphoreType.DMA((2, len(OFFSETS))),
            pltpu.SemaphoreType.DMA((RING,)),
            pltpu.SemaphoreType.DMA((RING,)),
            pltpu.SemaphoreType.DMA((GROUP,)),
            pltpu.SemaphoreType.DMA((4, GROUP)),
        ],
        compiler_params=pltpu.CompilerParams(
            collective_id=0, has_side_effects=True, vmem_limit_bytes=60 * 2**20
        ),
        name="wave_steps",
    )(*fields, samples, weights, gain.reshape(1, -1), *receivers)


def solution(mesh):
    sizes = tuple(mesh.shape[axis] for axis in ("inl", "xl", "gz"))
    cells = P("gz", "inl", "xl")
    traces = P(("inl", "xl", "gz"))
    return jax.shard_map(
        functools.partial(local, sizes),
        mesh=mesh,
        in_specs=(cells,) * 11 + (P(("inl", "xl", "gz"), None), P(), P(), traces, traces, traces),
        out_specs=(cells,) * 4,
        check_vma=False,
    )
```

```python
import functools

import jax
import jax.numpy as jnp
from jax import lax
from jax.experimental import pallas as pl
from jax.experimental.pallas import tpu as pltpu
from jax.sharding import PartitionSpec as P

MESH = pl.DeviceIdType.MESH
second_coef = (-205.0 / 72.0, 8.0 / 5.0, -1.0 / 5.0, 8.0 / 315.0, -1.0 / 560.0)
first_coef = (0.0, 4.0 / 5.0, -1.0 / 5.0, 4.0 / 105.0, -1.0 / 280.0)

OFFSETS = (
    [(d, 0, 0) for d in (1, -1)]
    + [(d, 0, e) for d in (1, -1) for e in (1, -1)]
    + [(d, e, 0) for d in (1, -1) for e in (1, -1)]
    + [(0, d, e) for d in (1, -1) for e in (1, -1)]
    + [(0, d, 0) for d in (1, -1)]
    + [(0, 0, d) for d in (1, -1)]
)
RING = 16
GROUP = 8
SLOTS = 4
WORDS = 16
BESIDE = [(d, e) for d in (1, -1, 0) for e in (1, -1, 0) if d != 0 or e != 0]


def iota(shape, axis):
    return lax.broadcasted_iota(jnp.int32, shape, axis)


def shifted(body, halo, axis):
    size = body.shape[axis]
    place = iota(body.shape, axis)
    above = [pltpu.roll(jnp.where(place < k, halo, body), size - k, axis) for k in range(1, 5)]
    below = [pltpu.roll(jnp.where(place >= size - k, halo, body), k, axis) for k in range(1, 5)]
    return above, below


def slope(above, below):
    total = first_coef[1] * (above[0] - below[0])
    for k in range(2, 5):
        total = total + first_coef[k] * (above[k - 1] - below[k - 1])
    return total


def bend(center, above, below):
    total = second_coef[0] * center
    for k in range(1, 5):
        total = total + second_coef[k] * (above[k - 1] + below[k - 1])
    return total


def kernel(sizes, *refs):
    n_inl, n_xl, n_gz = sizes
    (
        wave_p,
        wave_p_old,
        wave_q,
        wave_q_old,
        courant,
        epsilon,
        delta,
        tilt,
        azimuth,
        shear,
        damping,
        samples,
        weights,
        gain,
        inline,
        crossline,
        shot,
        next_p,
        next_q,
        prior_p,
        prior_q,
        body,
        side,
        packed,
        parcel,
        edge_y,
        edge_xy,
        old,
        field,
        coef,
        trace,
        small_w,
        small_g,
        small_r,
        letters,
        transit,
        mail,
        bundle,
        bundle_far,
        heap,
        heap_far,
        plane,
        plane_far,
        plane_side,
        plane_parcel,
        plane_packed,
        result,
        load_sem,
        store_sem,
        send_sem,
        recv_sem,
        letter_send,
        letter_recv,
        relay_send,
        relay_recv,
        bundle_send,
        bundle_recv,
        far_send,
        far_recv,
        plane_send,
        plane_recv,
    ) = refs
    i = lax.axis_index("inl")
    j = lax.axis_index("xl")
    g = lax.axis_index("gz")
    depth, across, along = 8, 8, 128
    half = n_inl // 2
    ring = 2 * n_xl
    high, low = i // half, i % half
    level = high * n_xl + j
    quarter = ring // 4
    border = jnp.where(high == 0, half - 1, 0)
    on_border = low == border
    surface = g == 0

    loads = [
        (wave_p, body.at[0, 0, pl.ds(4, depth)]),
        (wave_q, body.at[0, 1, pl.ds(4, depth)]),
        (wave_p_old, old.at[0]),
        (wave_q_old, old.at[1]),
        (courant, field.at[0]),
        (epsilon, field.at[1]),
        (delta, field.at[2]),
        (tilt, field.at[3]),
        (azimuth, field.at[4]),
        (shear, field.at[5]),
        (damping, field.at[6]),
        (samples, trace),
        (weights, small_w),
        (gain, small_g),
        (inline, small_r.at[0]),
        (crossline, small_r.at[1]),
        (shot, small_r.at[2]),
    ]
    loads = [pltpu.make_async_copy(a, b, load_sem.at[k]) for k, (a, b) in enumerate(loads)]
    for copy in loads:
        copy.start()

    nothing = jnp.zeros((2, 4, across, along), jnp.float32)
    for turn in range(2):
        body[turn, :, 0:4] = nothing
        body[turn, :, 12:16] = nothing
        for k in range(4):
            side[turn, :, 4 * k : 4 * k + 4] = nothing
        packed[turn] = jnp.zeros((5, 2, across, along), jnp.float32)
    mail[...] = jnp.zeros((2, RING, along), jnp.float32)
    heap[...] = jnp.zeros((4, 2, GROUP, along), jnp.float32)
    for layer in range(4):
        heap_far[layer] = jnp.zeros((GROUP, across, along), jnp.float32)
    plane_far[...] = jnp.zeros((across, along), jnp.float32)
    plane_side[...] = jnp.zeros((across, along), jnp.float32)
    plane_packed[...] = jnp.zeros((3, 2, across, along), jnp.float32)

    def there(offset):
        d, e, f = offset
        ok = []
        for step, place, count in ((d, i, n_inl), (e, j, n_xl), (f, g, n_gz)):
            if step == 1:
                ok.append(place < count - 1)
            if step == -1:
                ok.append(place > 0)
        return functools.reduce(jnp.logical_and, ok)

    def device(offset):
        d, e, f = offset
        return (
            jnp.clip(i + d, 0, n_inl - 1),
            jnp.clip(j + e, 0, n_xl - 1),
            jnp.clip(g + f, 0, n_gz - 1),
        )

    def on_ring(k):
        place = lax.rem(level + k + ring, ring)
        return (place // n_xl * half + low, lax.rem(place, n_xl), g)

    def in_group(k, layer):
        return (high * half + lax.rem(low + k, half), j, layer)

    barrier = pltpu.get_barrier_semaphore()
    count = jnp.int32(2 * quarter) + jnp.where(surface, half - 1, half)
    for offset in OFFSETS:

        @pl.when(there(offset))
        def _(offset=offset):
            pl.semaphore_signal(barrier, inc=1, device_id=device(offset), device_id_type=MESH)

        count = count + there(offset).astype(jnp.int32)
    near_ring = [k for k in range(-quarter, quarter + 1) if k != 0]
    for k in near_ring:
        pl.semaphore_signal(barrier, inc=1, device_id=on_ring(k), device_id_type=MESH)

    @pl.when(surface)
    def _():
        for layer in range(n_gz):
            for k in range(half):
                if layer > 0 or k > 0:
                    pl.semaphore_signal(
                        barrier, inc=1, device_id=in_group(k, layer), device_id_type=MESH
                    )

    for copy in loads:
        copy.wait()

    def prepare(z, _):
        sin_t, cos_t = jnp.sin(field[3, z]), jnp.cos(field[3, z])
        sin_f, cos_f = jnp.sin(field[4, z]), jnp.cos(field[4, z])
        coef[0, z] = sin_t * sin_t * cos_f * cos_f
        coef[1, z] = sin_t * sin_t * sin_f * sin_f
        coef[2, z] = cos_t * cos_t
        coef[3, z] = 2.0 * sin_t * sin_t * sin_f * cos_f
        coef[4, z] = 2.0 * sin_t * cos_t * cos_f
        coef[5, z] = 2.0 * sin_t * cos_t * sin_f
        c, s = field[0, z], field[5, z]
        grow, lean = 1.0 + 2.0 * field[1, z], 1.0 + 2.0 * field[2, z]
        coef[6, z] = c * grow
        coef[7, z] = c * (s - grow)
        coef[8, z] = c * (1.0 - s)
        coef[9, z] = c * (lean - s)
        coef[10, z] = c * s
        coef[11, z] = 1.0 - field[6, z]
        return 0

    lax.fori_loop(0, depth, prepare, 0)

    n_traces = trace.shape[0]
    row, column, line = small_r[0], small_r[1], small_r[2]
    lines = small_g.shape[1]
    picked = jnp.where(iota((lines, n_traces), 0) == line, 1.0, 0.0).astype(jnp.float32)
    gains = jnp.dot(
        small_g[...],
        picked,
        precision=lax.Precision.HIGHEST,
        preferred_element_type=jnp.float32,
    )
    amplitude = (
        lax.dot_general(
            small_w[...],
            trace[...],
            (((1,), (1,)), ((), ())),
            precision=lax.Precision.HIGHEST,
            preferred_element_type=jnp.float32,
        )
        * gains
    )
    to_inl, to_xl = row >> 3, column >> 7
    cell = ((row & 7) << 7) + (column & 127) + 1
    to_high = jnp.where(to_inl >= half, 1, 0)
    to_low = to_inl - to_high * half
    owner = to_inl * n_xl + to_xl
    columns = n_inl * n_xl
    member = jnp.where(iota((columns, n_traces), 0) == owner, 1.0, 0.0).astype(jnp.float32)
    earlier = jnp.where(
        iota((n_traces, n_traces), 0) < iota((n_traces, n_traces), 1), 1.0, 0.0
    ).astype(jnp.float32)
    before = jnp.dot(
        member.astype(jnp.bfloat16),
        earlier.astype(jnp.bfloat16),
        preferred_element_type=jnp.float32,
    )
    rank = jnp.sum(member * before, axis=0, keepdims=True).astype(jnp.int32)
    to_level = to_high * n_xl + to_xl
    block = to_low - low
    block = jnp.where(block < 0, block + half, block)
    word = block * WORDS + rank
    spot = iota((along, n_traces), 0)
    content = (
        jnp.where(spot == word, amplitude[0:1, :], 0.0)
        + jnp.where(spot == word + SLOTS, amplitude[1:2, :], 0.0)
        + jnp.where(spot == word + 2 * SLOTS, cell.astype(jnp.float32), 0.0)
    )
    leaves = (to_inl == half - 1) & ((row & 7) >= 4)
    enters = (to_inl == half) & ((row & 7) < 4)
    far_level = jnp.where(leaves, n_xl + to_xl, to_xl)
    far_word = 2 * SLOTS * level + rank
    far_content = jnp.where(spot == far_word, amplitude[0:1, :], 0.0) + jnp.where(
        spot == far_word + SLOTS, cell.astype(jnp.float32), 0.0
    )

    def write(target, wanted, words):
        hop = target - level + ring // 2
        hop = jnp.where(hop < 0, hop + ring, jnp.where(hop >= ring, hop - ring, hop))
        address = (iota((RING, n_traces), 0) == hop) & wanted
        return lax.dot_general(
            jnp.where(address, 1.0, 0.0).astype(jnp.float32),
            words,
            (((1,), (1,)), ((), ())),
            precision=lax.Precision.HIGHEST,
            preferred_element_type=jnp.float32,
        )

    letters[0] = write(to_level, to_level >= 0, content)
    letters[1] = write(far_level, leaves | enters, far_content)

    lane = iota((across, along), 1)
    sub = iota((across, along), 0)

    def pack(turn):
        total = jnp.zeros((across, along), jnp.float32)
        for f in range(2):
            for z in range(depth):
                tile = f * depth + z
                moved = pltpu.roll(body[turn, f, 4 + z], (8 * tile + 4) % along, 1)
                total = jnp.where(lane // 8 == tile, moved, total)
        parcel[turn] = total

    pack(0)

    def copies(turn):
        out = []
        mine = body.at[turn]
        beside = side.at[turn]
        for number, offset in enumerate(OFFSETS):
            d, e, f = offset
            if e != 0:
                kind = 0
                if f != 0:
                    kind = 1 if f == 1 else 2
                if d != 0:
                    kind = 3 if d == 1 else 4
                source = parcel.at[turn]
                target = packed.at[turn, kind, 0 if e == 1 else 1]
            else:
                deep = {0: (4, 8, 4), 1: (8, 4, 0), -1: (4, 4, 12)}[f]
                if d == 0:
                    source = mine.at[:, pl.ds(deep[0], deep[1])]
                    target = mine.at[:, pl.ds(deep[2], deep[1])]
                else:
                    wide = pl.ds(4 if d == 1 else 0, 4)
                    source = mine.at[:, pl.ds(deep[0], deep[1]), wide]
                    target = beside.at[:, pl.ds(deep[2], deep[1]), wide]
            out.append(
                pltpu.make_async_remote_copy(
                    src_ref=source,
                    dst_ref=target,
                    send_sem=send_sem.at[turn, number],
                    recv_sem=recv_sem.at[turn, number],
                    device_id=device(offset),
                    device_id_type=MESH,
                )
            )
        return out

    def begin(turn):
        for offset, copy in zip(OFFSETS, copies(turn)):

            @pl.when(there(offset))
            def _(copy=copy):
                copy.start()

    def arrive(turn):
        for offset, copy in zip(OFFSETS, copies(turn)):

            @pl.when(there(tuple(-d for d in offset)))
            def _(copy=copy):
                copy.wait_recv()

    def depart(turn):
        for offset, copy in zip(OFFSETS, copies(turn)):

            @pl.when(there(offset))
            def _(copy=copy):
                copy.wait_send()

    def letter(k):
        rows = pl.ds(2 * (k + quarter), 2)
        return pltpu.make_async_remote_copy(
            src_ref=letters.at[:, rows],
            dst_ref=transit.at[:, rows],
            send_sem=letter_send.at[k + quarter],
            recv_sem=letter_recv.at[k + quarter],
            device_id=on_ring(k),
            device_id_type=MESH,
        )

    def relay_rows(k):
        first = max(2 * (k + quarter) - 1, 0)
        return first, min(2 * (k + quarter) + 1, ring) - first

    def relay(k):
        rows = pl.ds(*relay_rows(k))
        return pltpu.make_async_remote_copy(
            src_ref=transit.at[:, rows],
            dst_ref=mail.at[:, rows],
            send_sem=relay_send.at[k + quarter],
            recv_sem=relay_recv.at[k + quarter],
            device_id=on_ring(k),
            device_id_type=MESH,
        )

    def parcel_of(k, layer):
        return pltpu.make_async_remote_copy(
            src_ref=bundle.at[:, pl.ds(k, 1)],
            dst_ref=heap.at[layer, :, pl.ds(k, 1)],
            send_sem=bundle_send.at[k],
            recv_sem=bundle_recv.at[layer, k],
            device_id=in_group(k, 0),
            device_id_type=MESH,
        )

    def far_parcel(layer, place):
        return pltpu.make_async_remote_copy(
            src_ref=bundle_far,
            dst_ref=heap_far.at[layer, place],
            send_sem=far_send,
            recv_sem=far_recv.at[layer, place],
            device_id=(high * half + border, j, 0),
            device_id_type=MESH,
        )

    def post():
        for k in near_ring:
            relay(k).wait_recv()
        for t in range(2):
            got = mail[0, 8 * t : 8 * t + 8, :]
            turned = jnp.zeros((GROUP, along), jnp.float32)
            for d in range(GROUP):
                moved = got if d == 0 else pltpu.roll(pltpu.roll(got, d, 0), along - WORDS * d, 1)
                turned = jnp.where(((sub - lane // WORDS) & 7) == d, moved, turned)
            bundle[t] = turned
        far = jnp.sum(mail[1], axis=0, keepdims=True)
        bundle_far[...] = jnp.where(sub == low, far, 0.0)
        for k in range(1, half):
            parcel_of(k, g).start()

        @pl.when(jnp.logical_not(surface))
        def _():
            parcel_of(0, g).start()

        @pl.when(surface)
        def _():
            heap[0, :, 0:1] = bundle[:, 0:1]

        @pl.when(jnp.logical_not(surface & on_border))
        def _():
            far_parcel(g, low).start()

        @pl.when(surface & on_border)
        def _():
            heap_far[0, border] = bundle_far[...]

    pl.semaphore_wait(barrier, count)
    begin(0)
    for k in range(-quarter, quarter):
        if k != 0:
            letter(k).start()
    own = pl.ds(2 * quarter, 2)
    transit[:, own] = letters[:, own]
    for k in range(-quarter, quarter):
        if k != 0:
            letter(k).wait_recv()
    for k in near_ring:
        relay(k).start()
    kept = pl.ds(*relay_rows(0))
    mail[:, kept] = transit[:, kept]

    def unpack(turn):
        def pair(kind):
            return jnp.where(lane % 8 < 4, packed[turn, kind, 0], packed[turn, kind, 1])

        plain = pair(0)
        deep = jnp.where((lane // 8) % 8 >= 4, pair(1), pair(2))
        wide = jnp.where(sub < 4, pair(4), pair(3))
        for f in range(2):
            for z in range(depth):
                turnback = (along - 4 - 8 * (f * depth + z)) % along
                edge_y[f, 4 + z] = pltpu.roll(plain, turnback, 1)
                edge_y[f, z - 4 if z >= 4 else 12 + z] = pltpu.roll(deep, turnback, 1)
                edge_xy[f, z] = pltpu.roll(wide, turnback, 1)

    def advance(turn, store):
        def layer(z, _):
            first, whole = [], []
            for f in range(2):
                center = body[turn, f, z + 4]
                beside = side[turn, f, z + 4]
                edge = edge_y[f, z + 4]
                above = [body[turn, f, z + 4 + k] for k in range(1, 5)]
                below = [body[turn, f, z + 4 - k] for k in range(1, 5)]
                u_zz = bend(center, above, below)
                grad_z = slope(above, below)
                grad_z_side = slope(
                    [side[turn, f, z + 4 + k] for k in range(1, 5)],
                    [side[turn, f, z + 4 - k] for k in range(1, 5)],
                )
                grad_z_edge = slope(
                    [edge_y[f, z + 4 + k] for k in range(1, 5)],
                    [edge_y[f, z + 4 - k] for k in range(1, 5)],
                )
                x_moves = shifted(center, beside, 0)
                u_xx = bend(center, *x_moves)
                grad_x = slope(*x_moves)
                grad_x_edge = slope(*shifted(edge, edge_xy[f, z], 0))
                u_yy = bend(center, *shifted(center, edge, 1))
                u_xy = slope(*shifted(grad_x, grad_x_edge, 1))
                u_xz = slope(*shifted(grad_z, grad_z_side, 0))
                u_yz = slope(*shifted(grad_z, grad_z_edge, 1))
                first.append(
                    coef[0, z] * u_xx
                    + coef[1, z] * u_yy
                    + coef[2, z] * u_zz
                    + coef[3, z] * u_xy
                    + coef[4, z] * u_xz
                    + coef[5, z] * u_yz
                )
                whole.append(u_xx + u_yy + u_zz)
            stay = coef[11, z]
            now_p, now_q = body[turn, 0, z + 4], body[turn, 1, z + 4]
            if turn == 0:
                was_p, was_q = old[0, z], old[1, z]
            else:
                was_p, was_q = body[0, 0, z + 4], body[0, 1, z + 4]
            mixed = coef[8, z] * first[1]
            new_p = (
                now_p
                + stay * (now_p - was_p)
                + (coef[6, z] * whole[0] + coef[7, z] * first[0] + mixed)
            )
            new_q = (
                now_q
                + stay * (now_q - was_q)
                + (coef[9, z] * (whole[0] - first[0]) + coef[10, z] * whole[1] + mixed)
            )
            store(z, new_p, new_q)
            return 0

        lax.fori_loop(0, depth, layer, 0)

    def keep(z, new_p, new_q):
        body[1, 0, z + 4] = new_p
        body[1, 1, z + 4] = new_q

    def finish(z, new_p, new_q):
        result[0, z] = new_p
        result[1, z] = new_q

    late = (high == 0) & on_border

    @pl.when(late)
    def _():
        post()

    arrive(0)
    unpack(0)
    advance(0, keep)
    pack(1)
    begin(1)

    @pl.when(jnp.logical_not(late))
    def _():
        post()

    def add_up(label, values):
        label_x, label_y = label >> 7, label & 127
        pieces = []
        for rest in values:
            for _ in range(3):
                rounded = rest.astype(jnp.bfloat16).astype(jnp.float32)
                pieces.append(rounded)
                rest = rest - rounded
        total = jnp.zeros((len(pieces) * across, along), jnp.float32)
        for r in range(0, 2 * GROUP, 2):

            def flat(array):
                return jnp.concatenate([array[r : r + 1], array[r + 1 : r + 2]], axis=1)

            at_x = iota((across, 2 * along), 0) == flat(label_x)
            left = jnp.concatenate([jnp.where(at_x, flat(piece), 0.0) for piece in pieces], axis=0)
            right = jnp.where(iota((along, 2 * along), 0) == flat(label_y), 1.0, 0.0)
            total = total + lax.dot_general(
                left.astype(jnp.bfloat16),
                right.astype(jnp.bfloat16),
                (((1,), (1,)), ((), ())),
                preferred_element_type=jnp.float32,
            )
        return [
            total[24 * k : 24 * k + 8] + total[24 * k + 8 : 24 * k + 16] + total[24 * k + 16 : 24 * k + 24]
            for k in range(len(values))
        ]

    def plane_there(d, e):
        crosses = jnp.bool_(False)
        if d == 1:
            crosses = i == half - 1
        if d == -1:
            crosses = i == half
        return there((d, e, 0)) & jnp.logical_not(crosses)

    def plane_copy(number):
        d, e = BESIDE[number]
        if e == 0:
            rows = pl.ds(4 if d == 1 else 0, 4)
            source, target = plane.at[0, rows], plane_side.at[rows]
        else:
            source, target = plane_parcel, plane_packed.at[{0: 0, 1: 1, -1: 2}[d], 0 if e == 1 else 1]
        return pltpu.make_async_remote_copy(
            src_ref=source,
            dst_ref=target,
            send_sem=plane_send.at[number],
            recv_sem=plane_recv.at[number],
            device_id=device((d, e, 0)),
            device_id_type=MESH,
        )

    @pl.when(surface)
    def _():
        for layer in range(n_gz):
            for k in range(half):
                if layer > 0 or k > 0:
                    parcel_of(k, layer).wait_recv()
        place = iota((2 * GROUP, along), 1) % WORDS // SLOTS
        parts = [heap[layer].reshape(2 * GROUP, along) for layer in range(4)]

        def gather(kind):
            total = jnp.zeros((2 * GROUP, along), jnp.float32)
            for layer in range(4):
                shift = SLOTS * (layer - kind) % along
                moved = parts[layer] if shift == 0 else pltpu.roll(parts[layer], shift, 1)
                total = jnp.where(place == layer, moved, total)
            return total

        sums = add_up(gather(2).astype(jnp.int32) - 1, [gather(0), gather(1)])
        plane[0] = sums[0]
        plane[1] = sums[1]

    @pl.when(surface & on_border)
    def _():
        for layer in range(n_gz):
            for place in range(half):

                @pl.when((layer > 0) | (border != place))
                def _(layer=layer, place=place):
                    far_parcel(layer, place).wait_recv()

        parts = [jnp.sum(heap_far[layer], axis=0) for layer in range(4)]
        front = lane % 8 < 4
        values, labels = [], []
        for k in (0, 2):
            values.append(jnp.where(front, parts[k], pltpu.roll(parts[k + 1], SLOTS, 1)))
            labels.append(jnp.where(front, pltpu.roll(parts[k], along - SLOTS, 1), parts[k + 1]))
        label = jnp.concatenate(labels, axis=0).astype(jnp.int32) - 1
        [total] = add_up(label, [jnp.concatenate(values, axis=0)])
        plane_far[...] = total

        @pl.when(high == 0)
        def _():
            plane_side[0:4] = total[0:4]

        @pl.when(high != 0)
        def _():
            plane_side[4:8] = total[4:8]

    @pl.when(surface)
    def _():
        plane_parcel[...] = jnp.where(
            lane < 8, pltpu.roll(plane[0], 4, 1), pltpu.roll(plane_far[...], 12, 1)
        )
        for number, (d, e) in enumerate(BESIDE):

            @pl.when(plane_there(d, e))
            def _(number=number):
                plane_copy(number).start()

    depart(1)
    arrive(1)
    unpack(1)

    @pl.when(surface)
    def _():
        for number, (d, e) in enumerate(BESIDE):

            @pl.when(plane_there(-d, -e))
            def _(number=number):
                plane_copy(number).wait_recv()

        def pair(kind):
            return jnp.where(lane % 8 < 4, plane_packed[kind, 0], plane_packed[kind, 1])

        same = pair(0)
        edge = pltpu.roll(same, along - 4, 1)
        corner = pltpu.roll(jnp.where(sub < 4, pair(2), pair(1)), along - 4, 1) + pltpu.roll(
            same, along - 12, 1
        )
        for f in range(2):
            body[1, f, 4] = body[1, f, 4] + plane[0]
            side[1, f, 4] = side[1, f, 4] + plane_side[...]
            edge_y[f, 4] = edge_y[f, 4] + edge
            edge_xy[f, 0] = edge_xy[f, 0] + corner

    stores = [
        pltpu.make_async_copy(body.at[1, 0, pl.ds(4, depth)], prior_p, store_sem.at[0]),
        pltpu.make_async_copy(body.at[1, 1, pl.ds(4, depth)], prior_q, store_sem.at[1]),
        pltpu.make_async_copy(result.at[0], next_p, store_sem.at[2]),
        pltpu.make_async_copy(result.at[1], next_q, store_sem.at[3]),
    ]
    stores[0].start()
    stores[1].start()
    advance(1, finish)

    @pl.when(surface)
    def _():
        for f in range(2):
            result[f, 0] = result[f, 0] + plane[1]

    stores[2].start()
    stores[3].start()
    depart(0)
    for k in range(-quarter, quarter):
        if k != 0:
            letter(k).wait_send()
    for k in near_ring:
        relay(k).wait_send()
    for k in range(1, half):
        parcel_of(k, g).wait_send()

    @pl.when(jnp.logical_not(surface))
    def _():
        parcel_of(0, g).wait_send()

    @pl.when(jnp.logical_not(surface & on_border))
    def _():
        far_parcel(g, low).wait_send()

    @pl.when(surface)
    def _():
        for number, (d, e) in enumerate(BESIDE):

            @pl.when(plane_there(d, e))
            def _(number=number):
                plane_copy(number).wait_send()

    for copy in stores:
        copy.wait()


def hand_over(*refs):
    sources, targets, sem = refs[:4], refs[4:8], refs[8]
    copies = [pltpu.make_async_copy(a, b, sem.at[k]) for k, (a, b) in enumerate(zip(sources, targets))]
    for copy in copies:
        copy.start()
    for copy in copies:
        copy.wait()


def local(sizes, *args):
    fields = args[:11]
    samples, weights, gain, row, column, line = args[11:]
    block = fields[0].shape
    n_traces = samples.shape[0]
    receivers = [ids.reshape(1, -1) for ids in (row, column, line)]
    f32 = jnp.float32
    outs = pl.pallas_call(
        functools.partial(kernel, sizes),
        out_shape=[jax.ShapeDtypeStruct(block, f32)] * 4,
        in_specs=[pl.BlockSpec(memory_space=pltpu.HBM)] * 17,
        out_specs=[pl.BlockSpec(memory_space=pltpu.HBM)] * 4,
        scratch_shapes=[
            pltpu.VMEM((2, 2, 16, 8, 128), f32),
            pltpu.VMEM((2, 2, 16, 8, 128), f32),
            pltpu.VMEM((2, 5, 2, 8, 128), f32),
            pltpu.VMEM((2, 8, 128), f32),
            pltpu.VMEM((2, 16, 8, 128), f32),
            pltpu.VMEM((2, 8, 8, 128), f32),
            pltpu.VMEM((2, 8, 8, 128), f32),
            pltpu.VMEM((7, 8, 8, 128), f32),
            pltpu.VMEM((12, 8, 8, 128), f32),
            pltpu.VMEM(samples.shape, f32),
            pltpu.VMEM(weights.shape, f32),
            pltpu.VMEM((1, gain.shape[0]), f32),
            pltpu.VMEM((3, 1, n_traces), jnp.int32),
            pltpu.VMEM((2, RING, 128), f32),
            pltpu.VMEM((2, RING, 128), f32),
            pltpu.VMEM((2, RING, 128), f32),
            pltpu.VMEM((2, GROUP, 128), f32),
            pltpu.VMEM((8, 128), f32),
            pltpu.VMEM((4, 2, GROUP, 128), f32),
            pltpu.VMEM((4, GROUP, 8, 128), f32),
            pltpu.VMEM((2, 8, 128), f32),
            pltpu.VMEM((8, 128), f32),
            pltpu.VMEM((8, 128), f32),
            pltpu.VMEM((8, 128), f32),
            pltpu.VMEM((3, 2, 8, 128), f32),
            pltpu.VMEM((2, 8, 8, 128), f32),
            pltpu.SemaphoreType.DMA((17,)),
            pltpu.SemaphoreType.DMA((4,)),
            pltpu.SemaphoreType.DMA((2, len(OFFSETS))),
            pltpu.SemaphoreType.DMA((2, len(OFFSETS))),
            pltpu.SemaphoreType.DMA((9,)),
            pltpu.SemaphoreType.DMA((9,)),
            pltpu.SemaphoreType.DMA((9,)),
            pltpu.SemaphoreType.DMA((9,)),
            pltpu.SemaphoreType.DMA((GROUP,)),
            pltpu.SemaphoreType.DMA((4, GROUP)),
            pltpu.SemaphoreType.DMA,
            pltpu.SemaphoreType.DMA((4, GROUP)),
            pltpu.SemaphoreType.DMA((8,)),
            pltpu.SemaphoreType.DMA((8,)),
        ],
        compiler_params=pltpu.CompilerParams(
            collective_id=0, has_side_effects=True, vmem_limit_bytes=60 * 2**20
        ),
        name="wave_steps",
    )(*fields, samples, weights, gain.reshape(1, -1), *receivers)
    return pl.pallas_call(
        hand_over,
        out_shape=[jax.ShapeDtypeStruct(block, f32)] * 4,
        in_specs=[pl.BlockSpec(memory_space=pltpu.HBM)] * 4,
        out_specs=[pl.BlockSpec(memory_space=pltpu.HBM)] * 4,
        scratch_shapes=[pltpu.SemaphoreType.DMA((4,))],
        compiler_params=pltpu.CompilerParams(vmem_limit_bytes=60 * 2**20),
        name="hand_over",
    )(*outs)


def solution(mesh):
    sizes = tuple(mesh.shape[axis] for axis in ("inl", "xl", "gz"))
    cells = P("gz", "inl", "xl")
    traces = P(("inl", "xl", "gz"))
    return jax.shard_map(
        functools.partial(local, sizes),
        mesh=mesh,
        in_specs=(cells,) * 11 + (P(("inl", "xl", "gz"), None), P(), P(), traces, traces, traces),
        out_specs=(cells,) * 4,
        check_vma=False,
    )
```

```python
import functools

import jax
import jax.numpy as jnp
from jax import lax
from jax.experimental import pallas as pl
from jax.experimental.pallas import tpu as pltpu
from jax.sharding import PartitionSpec as P

MESH = pl.DeviceIdType.MESH
second_coef = (-205.0 / 72.0, 8.0 / 5.0, -1.0 / 5.0, 8.0 / 315.0, -1.0 / 560.0)
first_coef = (0.0, 4.0 / 5.0, -1.0 / 5.0, 4.0 / 105.0, -1.0 / 280.0)

OFFSETS = (
    [(d, 0, 0) for d in (1, -1)]
    + [(d, 0, e) for d in (1, -1) for e in (1, -1)]
    + [(d, e, 0) for d in (1, -1) for e in (1, -1)]
    + [(0, d, e) for d in (1, -1) for e in (1, -1)]
    + [(0, d, 0) for d in (1, -1)]
    + [(0, 0, d) for d in (1, -1)]
)
RING = 16
GROUP = 8
SLOTS = 4
WORDS = 16
BESIDE = [(d, e) for d in (1, -1, 0) for e in (1, -1, 0) if d != 0 or e != 0]


def iota(shape, axis):
    return lax.broadcasted_iota(jnp.int32, shape, axis)


def shifted(body, halo, axis):
    size = body.shape[axis]
    place = iota(body.shape, axis)
    above = [pltpu.roll(jnp.where(place < k, halo, body), size - k, axis) for k in range(1, 5)]
    below = [pltpu.roll(jnp.where(place >= size - k, halo, body), k, axis) for k in range(1, 5)]
    return above, below


def slope(above, below):
    total = first_coef[1] * (above[0] - below[0])
    for k in range(2, 5):
        total = total + first_coef[k] * (above[k - 1] - below[k - 1])
    return total


def bend(center, above, below):
    total = second_coef[0] * center
    for k in range(1, 5):
        total = total + second_coef[k] * (above[k - 1] + below[k - 1])
    return total


def kernel(sizes, *refs):
    n_inl, n_xl, n_gz = sizes
    (
        wave_p,
        wave_p_old,
        wave_q,
        wave_q_old,
        courant,
        epsilon,
        delta,
        tilt,
        azimuth,
        shear,
        damping,
        samples,
        weights,
        gain,
        inline,
        crossline,
        shot,
        next_p,
        next_q,
        prior_p,
        prior_q,
        body,
        side,
        packed,
        parcel,
        edge_y,
        edge_xy,
        old,
        field,
        coef,
        trace,
        small_w,
        small_g,
        small_r,
        letters,
        transit,
        mail,
        bundle,
        bundle_far,
        heap,
        heap_far,
        plane,
        plane_far,
        plane_side,
        plane_parcel,
        plane_packed,
        load_sem,
        send_sem,
        recv_sem,
        letter_send,
        letter_recv,
        relay_send,
        relay_recv,
        bundle_send,
        bundle_recv,
        far_send,
        far_recv,
        plane_send,
        plane_recv,
    ) = refs
    i = lax.axis_index("inl")
    j = lax.axis_index("xl")
    g = lax.axis_index("gz")
    depth, across, along = 8, 8, 128
    half = n_inl // 2
    ring = 2 * n_xl
    high, low = i // half, i % half
    level = high * n_xl + j
    quarter = ring // 4
    border = jnp.where(high == 0, half - 1, 0)
    on_border = low == border
    surface = g == 0

    loads = [
        (wave_p, body.at[0, 0, pl.ds(4, depth)]),
        (wave_q, body.at[0, 1, pl.ds(4, depth)]),
        (wave_p_old, old.at[0]),
        (wave_q_old, old.at[1]),
        (courant, field.at[0]),
        (epsilon, field.at[1]),
        (delta, field.at[2]),
        (tilt, field.at[3]),
        (azimuth, field.at[4]),
        (shear, field.at[5]),
        (damping, field.at[6]),
        (samples, trace),
        (weights, small_w),
        (gain, small_g),
        (inline, small_r.at[0]),
        (crossline, small_r.at[1]),
        (shot, small_r.at[2]),
    ]
    loads = [pltpu.make_async_copy(a, b, load_sem.at[k]) for k, (a, b) in enumerate(loads)]
    for copy in loads:
        copy.start()

    nothing = jnp.zeros((2, 4, across, along), jnp.float32)
    for turn in range(2):
        body[turn, :, 0:4] = nothing
        body[turn, :, 12:16] = nothing
        for k in range(4):
            side[turn, :, 4 * k : 4 * k + 4] = nothing
        packed[turn] = jnp.zeros((5, 2, across, along), jnp.float32)
    mail[...] = jnp.zeros((2, RING, along), jnp.float32)
    heap[...] = jnp.zeros((4, 2, GROUP, along), jnp.float32)
    for layer in range(4):
        heap_far[layer] = jnp.zeros((GROUP, across, along), jnp.float32)
    plane_far[...] = jnp.zeros((across, along), jnp.float32)
    plane_side[...] = jnp.zeros((across, along), jnp.float32)
    plane_packed[...] = jnp.zeros((3, 2, across, along), jnp.float32)

    def there(offset):
        d, e, f = offset
        ok = []
        for step, place, count in ((d, i, n_inl), (e, j, n_xl), (f, g, n_gz)):
            if step == 1:
                ok.append(place < count - 1)
            if step == -1:
                ok.append(place > 0)
        return functools.reduce(jnp.logical_and, ok)

    def device(offset):
        d, e, f = offset
        return (
            jnp.clip(i + d, 0, n_inl - 1),
            jnp.clip(j + e, 0, n_xl - 1),
            jnp.clip(g + f, 0, n_gz - 1),
        )

    def on_ring(k):
        place = lax.rem(level + k + ring, ring)
        return (place // n_xl * half + low, lax.rem(place, n_xl), g)

    def in_group(k, layer):
        return (high * half + lax.rem(low + k, half), j, layer)

    barrier = pltpu.get_barrier_semaphore()
    count = jnp.int32(2 * quarter) + jnp.where(surface, half - 1, half)
    for offset in OFFSETS:

        @pl.when(there(offset))
        def _(offset=offset):
            pl.semaphore_signal(barrier, inc=1, device_id=device(offset), device_id_type=MESH)

        count = count + there(offset).astype(jnp.int32)
    near_ring = [k for k in range(-quarter, quarter + 1) if k != 0]
    for k in near_ring:
        pl.semaphore_signal(barrier, inc=1, device_id=on_ring(k), device_id_type=MESH)

    @pl.when(surface)
    def _():
        for layer in range(n_gz):
            for k in range(half):
                if layer > 0 or k > 0:
                    pl.semaphore_signal(
                        barrier, inc=1, device_id=in_group(k, layer), device_id_type=MESH
                    )

    for copy in loads:
        copy.wait()

    def prepare(z, _):
        sin_t, cos_t = jnp.sin(field[3, z]), jnp.cos(field[3, z])
        sin_f, cos_f = jnp.sin(field[4, z]), jnp.cos(field[4, z])
        coef[0, z] = sin_t * sin_t * cos_f * cos_f
        coef[1, z] = sin_t * sin_t * sin_f * sin_f
        coef[2, z] = cos_t * cos_t
        coef[3, z] = 2.0 * sin_t * sin_t * sin_f * cos_f
        coef[4, z] = 2.0 * sin_t * cos_t * cos_f
        coef[5, z] = 2.0 * sin_t * cos_t * sin_f
        c, s = field[0, z], field[5, z]
        grow, lean = 1.0 + 2.0 * field[1, z], 1.0 + 2.0 * field[2, z]
        coef[6, z] = c * grow
        coef[7, z] = c * (s - grow)
        coef[8, z] = c * (1.0 - s)
        coef[9, z] = c * (lean - s)
        coef[10, z] = c * s
        coef[11, z] = 1.0 - field[6, z]
        return 0

    lax.fori_loop(0, depth, prepare, 0)

    n_traces = trace.shape[0]
    row, column, line = small_r[0], small_r[1], small_r[2]
    lines = small_g.shape[1]
    picked = jnp.where(iota((lines, n_traces), 0) == line, 1.0, 0.0).astype(jnp.float32)
    gains = jnp.dot(
        small_g[...],
        picked,
        precision=lax.Precision.HIGHEST,
        preferred_element_type=jnp.float32,
    )
    amplitude = (
        lax.dot_general(
            small_w[...],
            trace[...],
            (((1,), (1,)), ((), ())),
            precision=lax.Precision.HIGHEST,
            preferred_element_type=jnp.float32,
        )
        * gains
    )
    to_inl, to_xl = row >> 3, column >> 7
    cell = ((row & 7) << 7) + (column & 127) + 1
    to_high = jnp.where(to_inl >= half, 1, 0)
    to_low = to_inl - to_high * half
    owner = to_inl * n_xl + to_xl
    columns = n_inl * n_xl
    member = jnp.where(iota((columns, n_traces), 0) == owner, 1.0, 0.0).astype(jnp.float32)
    earlier = jnp.where(
        iota((n_traces, n_traces), 0) < iota((n_traces, n_traces), 1), 1.0, 0.0
    ).astype(jnp.float32)
    before = jnp.dot(
        member.astype(jnp.bfloat16),
        earlier.astype(jnp.bfloat16),
        preferred_element_type=jnp.float32,
    )
    rank = jnp.sum(member * before, axis=0, keepdims=True).astype(jnp.int32)
    to_level = to_high * n_xl + to_xl
    block = to_low - low
    block = jnp.where(block < 0, block + half, block)
    word = block * WORDS + rank
    spot = iota((along, n_traces), 0)
    content = (
        jnp.where(spot == word, amplitude[0:1, :], 0.0)
        + jnp.where(spot == word + SLOTS, amplitude[1:2, :], 0.0)
        + jnp.where(spot == word + 2 * SLOTS, cell.astype(jnp.float32), 0.0)
    )
    leaves = (to_inl == half - 1) & ((row & 7) >= 4)
    enters = (to_inl == half) & ((row & 7) < 4)
    far_level = jnp.where(leaves, n_xl + to_xl, to_xl)
    far_word = 2 * SLOTS * level + rank
    far_content = jnp.where(spot == far_word, amplitude[0:1, :], 0.0) + jnp.where(
        spot == far_word + SLOTS, cell.astype(jnp.float32), 0.0
    )

    def write(target, wanted, words):
        hop = target - level + ring // 2
        hop = jnp.where(hop < 0, hop + ring, jnp.where(hop >= ring, hop - ring, hop))
        address = (iota((RING, n_traces), 0) == hop) & wanted
        return lax.dot_general(
            jnp.where(address, 1.0, 0.0).astype(jnp.float32),
            words,
            (((1,), (1,)), ((), ())),
            precision=lax.Precision.HIGHEST,
            preferred_element_type=jnp.float32,
        )

    letters[0] = write(to_level, to_level >= 0, content)
    letters[1] = write(far_level, leaves | enters, far_content)

    lane = iota((across, along), 1)
    sub = iota((across, along), 0)

    def pack(turn):
        total = jnp.zeros((across, along), jnp.float32)
        for f in range(2):
            for z in range(depth):
                tile = f * depth + z
                moved = pltpu.roll(body[turn, f, 4 + z], (8 * tile + 4) % along, 1)
                total = jnp.where(lane // 8 == tile, moved, total)
        parcel[turn] = total

    pack(0)

    def copies(turn):
        out = []
        mine = body.at[turn]
        beside = side.at[turn]
        for number, offset in enumerate(OFFSETS):
            d, e, f = offset
            if e != 0:
                kind = 0
                if f != 0:
                    kind = 1 if f == 1 else 2
                if d != 0:
                    kind = 3 if d == 1 else 4
                source = parcel.at[turn]
                target = packed.at[turn, kind, 0 if e == 1 else 1]
            else:
                deep = {0: (4, 8, 4), 1: (8, 4, 0), -1: (4, 4, 12)}[f]
                if d == 0:
                    source = mine.at[:, pl.ds(deep[0], deep[1])]
                    target = mine.at[:, pl.ds(deep[2], deep[1])]
                else:
                    wide = pl.ds(4 if d == 1 else 0, 4)
                    source = mine.at[:, pl.ds(deep[0], deep[1]), wide]
                    target = beside.at[:, pl.ds(deep[2], deep[1]), wide]
            out.append(
                pltpu.make_async_remote_copy(
                    src_ref=source,
                    dst_ref=target,
                    send_sem=send_sem.at[turn, number],
                    recv_sem=recv_sem.at[turn, number],
                    device_id=device(offset),
                    device_id_type=MESH,
                )
            )
        return out

    def begin(turn):
        for offset, copy in zip(OFFSETS, copies(turn)):

            @pl.when(there(offset))
            def _(copy=copy):
                copy.start()

    def arrive(turn):
        for offset, copy in zip(OFFSETS, copies(turn)):

            @pl.when(there(tuple(-d for d in offset)))
            def _(copy=copy):
                copy.wait_recv()

    def depart(turn):
        for offset, copy in zip(OFFSETS, copies(turn)):

            @pl.when(there(offset))
            def _(copy=copy):
                copy.wait_send()

    def letter(k):
        rows = pl.ds(2 * (k + quarter), 2)
        return pltpu.make_async_remote_copy(
            src_ref=letters.at[:, rows],
            dst_ref=transit.at[:, rows],
            send_sem=letter_send.at[k + quarter],
            recv_sem=letter_recv.at[k + quarter],
            device_id=on_ring(k),
            device_id_type=MESH,
        )

    def relay_rows(k):
        first = max(2 * (k + quarter) - 1, 0)
        return first, min(2 * (k + quarter) + 1, ring) - first

    def relay(k):
        rows = pl.ds(*relay_rows(k))
        return pltpu.make_async_remote_copy(
            src_ref=transit.at[:, rows],
            dst_ref=mail.at[:, rows],
            send_sem=relay_send.at[k + quarter],
            recv_sem=relay_recv.at[k + quarter],
            device_id=on_ring(k),
            device_id_type=MESH,
        )

    def parcel_of(k, layer):
        return pltpu.make_async_remote_copy(
            src_ref=bundle.at[:, pl.ds(k, 1)],
            dst_ref=heap.at[layer, :, pl.ds(k, 1)],
            send_sem=bundle_send.at[k],
            recv_sem=bundle_recv.at[layer, k],
            device_id=in_group(k, 0),
            device_id_type=MESH,
        )

    def far_parcel(layer, place):
        return pltpu.make_async_remote_copy(
            src_ref=bundle_far,
            dst_ref=heap_far.at[layer, place],
            send_sem=far_send,
            recv_sem=far_recv.at[layer, place],
            device_id=(high * half + border, j, 0),
            device_id_type=MESH,
        )

    def post():
        for k in near_ring:
            relay(k).wait_recv()
        for t in range(2):
            got = mail[0, 8 * t : 8 * t + 8, :]
            turned = jnp.zeros((GROUP, along), jnp.float32)
            for d in range(GROUP):
                moved = got if d == 0 else pltpu.roll(pltpu.roll(got, d, 0), along - WORDS * d, 1)
                turned = jnp.where(((sub - lane // WORDS) & 7) == d, moved, turned)
            bundle[t] = turned
        far = jnp.sum(mail[1], axis=0, keepdims=True)
        bundle_far[...] = jnp.where(sub == low, far, 0.0)
        for k in range(1, half):
            parcel_of(k, g).start()

        @pl.when(jnp.logical_not(surface))
        def _():
            parcel_of(0, g).start()

        @pl.when(surface)
        def _():
            heap[0, :, 0:1] = bundle[:, 0:1]

        @pl.when(jnp.logical_not(surface & on_border))
        def _():
            far_parcel(g, low).start()

        @pl.when(surface & on_border)
        def _():
            heap_far[0, border] = bundle_far[...]

    pl.semaphore_wait(barrier, count)
    for k in range(-quarter, quarter):
        if k != 0:
            letter(k).start()
    begin(0)
    own = pl.ds(2 * quarter, 2)
    transit[:, own] = letters[:, own]
    for k in range(-quarter, quarter):
        if k != 0:
            letter(k).wait_recv()
    for k in near_ring:
        relay(k).start()
    kept = pl.ds(*relay_rows(0))
    mail[:, kept] = transit[:, kept]

    def unpack(turn):
        def pair(kind):
            return jnp.where(lane % 8 < 4, packed[turn, kind, 0], packed[turn, kind, 1])

        plain = pair(0)
        deep = jnp.where((lane // 8) % 8 >= 4, pair(1), pair(2))
        wide = jnp.where(sub < 4, pair(4), pair(3))
        for f in range(2):
            for z in range(depth):
                turnback = (along - 4 - 8 * (f * depth + z)) % along
                edge_y[f, 4 + z] = pltpu.roll(plain, turnback, 1)
                edge_y[f, z - 4 if z >= 4 else 12 + z] = pltpu.roll(deep, turnback, 1)
                edge_xy[f, z] = pltpu.roll(wide, turnback, 1)

    def advance(turn, store):
        def layer(z, _):
            first, whole = [], []
            for f in range(2):
                center = body[turn, f, z + 4]
                beside = side[turn, f, z + 4]
                edge = edge_y[f, z + 4]
                above = [body[turn, f, z + 4 + k] for k in range(1, 5)]
                below = [body[turn, f, z + 4 - k] for k in range(1, 5)]
                u_zz = bend(center, above, below)
                grad_z = slope(above, below)
                grad_z_side = slope(
                    [side[turn, f, z + 4 + k] for k in range(1, 5)],
                    [side[turn, f, z + 4 - k] for k in range(1, 5)],
                )
                grad_z_edge = slope(
                    [edge_y[f, z + 4 + k] for k in range(1, 5)],
                    [edge_y[f, z + 4 - k] for k in range(1, 5)],
                )
                x_moves = shifted(center, beside, 0)
                u_xx = bend(center, *x_moves)
                grad_x = slope(*x_moves)
                grad_x_edge = slope(*shifted(edge, edge_xy[f, z], 0))
                u_yy = bend(center, *shifted(center, edge, 1))
                u_xy = slope(*shifted(grad_x, grad_x_edge, 1))
                u_xz = slope(*shifted(grad_z, grad_z_side, 0))
                u_yz = slope(*shifted(grad_z, grad_z_edge, 1))
                first.append(
                    coef[0, z] * u_xx
                    + coef[1, z] * u_yy
                    + coef[2, z] * u_zz
                    + coef[3, z] * u_xy
                    + coef[4, z] * u_xz
                    + coef[5, z] * u_yz
                )
                whole.append(u_xx + u_yy + u_zz)
            stay = coef[11, z]
            now_p, now_q = body[turn, 0, z + 4], body[turn, 1, z + 4]
            if turn == 0:
                was_p, was_q = old[0, z], old[1, z]
            else:
                was_p, was_q = body[0, 0, z + 4], body[0, 1, z + 4]
            mixed = coef[8, z] * first[1]
            new_p = (
                now_p
                + stay * (now_p - was_p)
                + (coef[6, z] * whole[0] + coef[7, z] * first[0] + mixed)
            )
            new_q = (
                now_q
                + stay * (now_q - was_q)
                + (coef[9, z] * (whole[0] - first[0]) + coef[10, z] * whole[1] + mixed)
            )
            store(z, new_p, new_q)
            return 0

        lax.fori_loop(0, depth, layer, 0)

    def keep(z, new_p, new_q):
        body[1, 0, z + 4] = new_p
        body[1, 1, z + 4] = new_q

    def finish(z, new_p, new_q):
        next_p[z] = new_p
        next_q[z] = new_q

    late = (high == 0) & on_border

    @pl.when(late)
    def _():
        post()

    arrive(0)
    unpack(0)
    advance(0, keep)
    pack(1)
    begin(1)

    @pl.when(jnp.logical_not(late))
    def _():
        post()

    def add_up(label, values):
        label_x, label_y = label >> 7, label & 127
        pieces = []
        for rest in values:
            for _ in range(3):
                rounded = rest.astype(jnp.bfloat16).astype(jnp.float32)
                pieces.append(rounded)
                rest = rest - rounded
        total = jnp.zeros((len(pieces) * across, along), jnp.float32)
        for r in range(0, 2 * GROUP, 2):

            def flat(array):
                return jnp.concatenate([array[r : r + 1], array[r + 1 : r + 2]], axis=1)

            at_x = iota((across, 2 * along), 0) == flat(label_x)
            left = jnp.concatenate([jnp.where(at_x, flat(piece), 0.0) for piece in pieces], axis=0)
            right = jnp.where(iota((along, 2 * along), 0) == flat(label_y), 1.0, 0.0)
            total = total + lax.dot_general(
                left.astype(jnp.bfloat16),
                right.astype(jnp.bfloat16),
                (((1,), (1,)), ((), ())),
                preferred_element_type=jnp.float32,
            )
        return [
            total[24 * k : 24 * k + 8] + total[24 * k + 8 : 24 * k + 16] + total[24 * k + 16 : 24 * k + 24]
            for k in range(len(values))
        ]

    def plane_there(d, e):
        crosses = jnp.bool_(False)
        if d == 1:
            crosses = i == half - 1
        if d == -1:
            crosses = i == half
        return there((d, e, 0)) & jnp.logical_not(crosses)

    def plane_copy(number):
        d, e = BESIDE[number]
        if e == 0:
            rows = pl.ds(4 if d == 1 else 0, 4)
            source, target = plane.at[0, rows], plane_side.at[rows]
        else:
            source, target = plane_parcel, plane_packed.at[{0: 0, 1: 1, -1: 2}[d], 0 if e == 1 else 1]
        return pltpu.make_async_remote_copy(
            src_ref=source,
            dst_ref=target,
            send_sem=plane_send.at[number],
            recv_sem=plane_recv.at[number],
            device_id=device((d, e, 0)),
            device_id_type=MESH,
        )

    @pl.when(surface)
    def _():
        for layer in range(n_gz):
            for k in range(half):
                if layer > 0 or k > 0:
                    parcel_of(k, layer).wait_recv()
        place = iota((2 * GROUP, along), 1) % WORDS // SLOTS
        parts = [heap[layer].reshape(2 * GROUP, along) for layer in range(4)]

        def gather(kind):
            total = jnp.zeros((2 * GROUP, along), jnp.float32)
            for layer in range(4):
                shift = SLOTS * (layer - kind) % along
                moved = parts[layer] if shift == 0 else pltpu.roll(parts[layer], shift, 1)
                total = jnp.where(place == layer, moved, total)
            return total

        sums = add_up(gather(2).astype(jnp.int32) - 1, [gather(0), gather(1)])
        plane[0] = sums[0]
        plane[1] = sums[1]

    @pl.when(surface & on_border)
    def _():
        for layer in range(n_gz):
            for place in range(half):

                @pl.when((layer > 0) | (border != place))
                def _(layer=layer, place=place):
                    far_parcel(layer, place).wait_recv()

        parts = [jnp.sum(heap_far[layer], axis=0) for layer in range(4)]
        front = lane % 8 < 4
        values, labels = [], []
        for k in (0, 2):
            values.append(jnp.where(front, parts[k], pltpu.roll(parts[k + 1], SLOTS, 1)))
            labels.append(jnp.where(front, pltpu.roll(parts[k], along - SLOTS, 1), parts[k + 1]))
        label = jnp.concatenate(labels, axis=0).astype(jnp.int32) - 1
        [total] = add_up(label, [jnp.concatenate(values, axis=0)])
        plane_far[...] = total

        @pl.when(high == 0)
        def _():
            plane_side[0:4] = total[0:4]

        @pl.when(high != 0)
        def _():
            plane_side[4:8] = total[4:8]

    @pl.when(surface)
    def _():
        plane_parcel[...] = jnp.where(
            lane < 8, pltpu.roll(plane[0], 4, 1), pltpu.roll(plane_far[...], 12, 1)
        )
        for number, (d, e) in enumerate(BESIDE):

            @pl.when(plane_there(d, e))
            def _(number=number):
                plane_copy(number).start()

    depart(1)
    arrive(1)
    unpack(1)

    @pl.when(surface)
    def _():
        for number, (d, e) in enumerate(BESIDE):

            @pl.when(plane_there(-d, -e))
            def _(number=number):
                plane_copy(number).wait_recv()

        def pair(kind):
            return jnp.where(lane % 8 < 4, plane_packed[kind, 0], plane_packed[kind, 1])

        same = pair(0)
        edge = pltpu.roll(same, along - 4, 1)
        corner = pltpu.roll(jnp.where(sub < 4, pair(2), pair(1)), along - 4, 1) + pltpu.roll(
            same, along - 12, 1
        )
        for f in range(2):
            body[1, f, 4] = body[1, f, 4] + plane[0]
            side[1, f, 4] = side[1, f, 4] + plane_side[...]
            edge_y[f, 4] = edge_y[f, 4] + edge
            edge_xy[f, 0] = edge_xy[f, 0] + corner

    for f, prior in enumerate((prior_p, prior_q)):
        prior[...] = body[1, f, 4:12]
    advance(1, finish)

    @pl.when(surface)
    def _():
        for result in (next_p, next_q):
            result[0] = result[0] + plane[1]

    depart(0)
    for k in range(-quarter, quarter):
        if k != 0:
            letter(k).wait_send()
    for k in near_ring:
        relay(k).wait_send()
    for k in range(1, half):
        parcel_of(k, g).wait_send()

    @pl.when(jnp.logical_not(surface))
    def _():
        parcel_of(0, g).wait_send()

    @pl.when(jnp.logical_not(surface & on_border))
    def _():
        far_parcel(g, low).wait_send()

    @pl.when(surface)
    def _():
        for number, (d, e) in enumerate(BESIDE):

            @pl.when(plane_there(d, e))
            def _(number=number):
                plane_copy(number).wait_send()


def hand_over(*refs):
    sources, targets, sem = refs[:4], refs[4:8], refs[8]
    copies = [pltpu.make_async_copy(a, b, sem.at[k]) for k, (a, b) in enumerate(zip(sources, targets))]
    for copy in copies:
        copy.start()
    for copy in copies:
        copy.wait()


def local(sizes, *args):
    fields = args[:11]
    samples, weights, gain, row, column, line = args[11:]
    block = fields[0].shape
    n_traces = samples.shape[0]
    receivers = [ids.reshape(1, -1) for ids in (row, column, line)]
    f32 = jnp.float32
    outs = pl.pallas_call(
        functools.partial(kernel, sizes),
        out_shape=[pltpu.VMEM(block, f32)] * 4,
        in_specs=[pl.BlockSpec(memory_space=pltpu.HBM)] * 17,
        out_specs=[pl.BlockSpec(memory_space=pltpu.VMEM)] * 4,
        scratch_shapes=[
            pltpu.VMEM((2, 2, 16, 8, 128), f32),
            pltpu.VMEM((2, 2, 16, 8, 128), f32),
            pltpu.VMEM((2, 5, 2, 8, 128), f32),
            pltpu.VMEM((2, 8, 128), f32),
            pltpu.VMEM((2, 16, 8, 128), f32),
            pltpu.VMEM((2, 8, 8, 128), f32),
            pltpu.VMEM((2, 8, 8, 128), f32),
            pltpu.VMEM((7, 8, 8, 128), f32),
            pltpu.VMEM((12, 8, 8, 128), f32),
            pltpu.VMEM(samples.shape, f32),
            pltpu.VMEM(weights.shape, f32),
            pltpu.VMEM((1, gain.shape[0]), f32),
            pltpu.VMEM((3, 1, n_traces), jnp.int32),
            pltpu.VMEM((2, RING, 128), f32),
            pltpu.VMEM((2, RING, 128), f32),
            pltpu.VMEM((2, RING, 128), f32),
            pltpu.VMEM((2, GROUP, 128), f32),
            pltpu.VMEM((8, 128), f32),
            pltpu.VMEM((4, 2, GROUP, 128), f32),
            pltpu.VMEM((4, GROUP, 8, 128), f32),
            pltpu.VMEM((2, 8, 128), f32),
            pltpu.VMEM((8, 128), f32),
            pltpu.VMEM((8, 128), f32),
            pltpu.VMEM((8, 128), f32),
            pltpu.VMEM((3, 2, 8, 128), f32),
            pltpu.SemaphoreType.DMA((17,)),
            pltpu.SemaphoreType.DMA((2, len(OFFSETS))),
            pltpu.SemaphoreType.DMA((2, len(OFFSETS))),
            pltpu.SemaphoreType.DMA((9,)),
            pltpu.SemaphoreType.DMA((9,)),
            pltpu.SemaphoreType.DMA((9,)),
            pltpu.SemaphoreType.DMA((9,)),
            pltpu.SemaphoreType.DMA((GROUP,)),
            pltpu.SemaphoreType.DMA((4, GROUP)),
            pltpu.SemaphoreType.DMA,
            pltpu.SemaphoreType.DMA((4, GROUP)),
            pltpu.SemaphoreType.DMA((8,)),
            pltpu.SemaphoreType.DMA((8,)),
        ],
        compiler_params=pltpu.CompilerParams(
            collective_id=0, has_side_effects=True, vmem_limit_bytes=60 * 2**20
        ),
        name="wave_steps",
    )(*fields, samples, weights, gain.reshape(1, -1), *receivers)
    return pl.pallas_call(
        hand_over,
        out_shape=[jax.ShapeDtypeStruct(block, f32)] * 4,
        in_specs=[pl.BlockSpec(memory_space=pl.ANY)] * 4,
        out_specs=[pl.BlockSpec(memory_space=pltpu.HBM)] * 4,
        scratch_shapes=[pltpu.SemaphoreType.DMA((4,))],
        compiler_params=pltpu.CompilerParams(vmem_limit_bytes=2**20),
        name="hand_over",
    )(*outs)


def solution(mesh):
    sizes = tuple(mesh.shape[axis] for axis in ("inl", "xl", "gz"))
    cells = P("gz", "inl", "xl")
    traces = P(("inl", "xl", "gz"))
    return jax.shard_map(
        functools.partial(local, sizes),
        mesh=mesh,
        in_specs=(cells,) * 11 + (P(("inl", "xl", "gz"), None), P(), P(), traces, traces, traces),
        out_specs=(cells,) * 4,
        check_vma=False,
    )
```

```python
import functools

import jax
import jax.numpy as jnp
from jax import lax
from jax.experimental import pallas as pl
from jax.experimental.pallas import tpu as pltpu
from jax.sharding import PartitionSpec as P

MESH = pl.DeviceIdType.MESH
second_coef = (-205.0 / 72.0, 8.0 / 5.0, -1.0 / 5.0, 8.0 / 315.0, -1.0 / 560.0)
first_coef = (0.0, 4.0 / 5.0, -1.0 / 5.0, 4.0 / 105.0, -1.0 / 280.0)

OFFSETS = (
    [(d, 0, 0) for d in (1, -1)]
    + [(d, 0, e) for d in (1, -1) for e in (1, -1)]
    + [(d, e, 0) for d in (1, -1) for e in (1, -1)]
    + [(0, d, e) for d in (1, -1) for e in (1, -1)]
    + [(0, d, 0) for d in (1, -1)]
    + [(0, 0, d) for d in (1, -1)]
)
RING = 16
GROUP = 8
SLOTS = 4
WORDS = 16
BESIDE = [(d, e) for d in (1, -1, 0) for e in (1, -1, 0) if d != 0 or e != 0]


def iota(shape, axis):
    return lax.broadcasted_iota(jnp.int32, shape, axis)


def shifted(body, halo, axis):
    size = body.shape[axis]
    place = iota(body.shape, axis)
    above = [pltpu.roll(jnp.where(place < k, halo, body), size - k, axis) for k in range(1, 5)]
    below = [pltpu.roll(jnp.where(place >= size - k, halo, body), k, axis) for k in range(1, 5)]
    return above, below


def slope(above, below):
    total = first_coef[1] * (above[0] - below[0])
    for k in range(2, 5):
        total = total + first_coef[k] * (above[k - 1] - below[k - 1])
    return total


def bend(center, above, below):
    total = second_coef[0] * center
    for k in range(1, 5):
        total = total + second_coef[k] * (above[k - 1] + below[k - 1])
    return total


def kernel(sizes, *refs):
    n_inl, n_xl, n_gz = sizes
    (
        wave_p,
        wave_p_old,
        wave_q,
        wave_q_old,
        courant,
        epsilon,
        delta,
        tilt,
        azimuth,
        shear,
        damping,
        samples,
        weights,
        gain,
        inline,
        crossline,
        shot,
        next_p,
        next_q,
        prior_p,
        prior_q,
        body,
        side,
        packed,
        parcel,
        edge_y,
        edge_xy,
        old,
        field,
        coef,
        trace,
        small_w,
        small_g,
        small_r,
        letters,
        transit,
        mail,
        passing,
        passing_parcel,
        bundle,
        bundle_far,
        heap,
        heap_far,
        plane,
        plane_far,
        plane_side,
        plane_parcel,
        plane_packed,
        load_sem,
        send_sem,
        recv_sem,
        letter_send,
        letter_recv,
        relay_send,
        relay_recv,
        bundle_send,
        bundle_recv,
        far_send,
        far_recv,
        plane_send,
        plane_recv,
        pass_send,
        pass_recv,
        onward_send,
        known,
    ) = refs
    i = lax.axis_index("inl")
    j = lax.axis_index("xl")
    g = lax.axis_index("gz")
    depth, across, along = 8, 8, 128
    half = n_inl // 2
    ring = 2 * n_xl
    high, low = i // half, i % half
    level = high * n_xl + j
    quarter = ring // 4
    border = jnp.where(high == 0, half - 1, 0)
    on_border = low == border
    surface = g == 0
    near_side, far_side = i == half - 1, i == half
    forwards = (low == half - 1) & (level >= quarter) & (level < quarter + n_xl)

    loads = [
        (wave_p, body.at[0, 0, pl.ds(4, depth)]),
        (wave_q, body.at[0, 1, pl.ds(4, depth)]),
        (wave_p_old, old.at[0]),
        (wave_q_old, old.at[1]),
        (courant, field.at[0]),
        (epsilon, field.at[1]),
        (delta, field.at[2]),
        (tilt, field.at[3]),
        (azimuth, field.at[4]),
        (shear, field.at[5]),
        (damping, field.at[6]),
        (samples, trace),
        (weights, small_w),
        (gain, small_g),
        (inline, small_r.at[0]),
        (crossline, small_r.at[1]),
        (shot, small_r.at[2]),
    ]
    loads = [pltpu.make_async_copy(a, b, load_sem.at[k]) for k, (a, b) in enumerate(loads)]
    nothing = jnp.zeros((2, 4, across, along), jnp.float32)
    for turn in range(2):
        body[turn, :, 0:4] = nothing
        body[turn, :, 12:16] = nothing
        for k in range(4):
            side[turn, :, 4 * k : 4 * k + 4] = nothing
        packed[turn] = jnp.zeros((5, 2, across, along), jnp.float32)
    mail[...] = jnp.zeros((2, RING, along), jnp.float32)
    heap[...] = jnp.zeros((4, 2, GROUP, along), jnp.float32)
    for layer in range(4):
        heap_far[layer] = jnp.zeros((GROUP, across, along), jnp.float32)
    plane_far[...] = jnp.zeros((across, along), jnp.float32)
    plane_side[...] = jnp.zeros((across, along), jnp.float32)
    plane_packed[...] = jnp.zeros((3, 2, across, along), jnp.float32)

    def there(offset):
        d, e, f = offset
        ok = []
        for step, place, count in ((d, i, n_inl), (e, j, n_xl), (f, g, n_gz)):
            if step == 1:
                ok.append(place < count - 1)
            if step == -1:
                ok.append(place > 0)
        return functools.reduce(jnp.logical_and, ok)

    def device(offset):
        d, e, f = offset
        return (
            jnp.clip(i + d, 0, n_inl - 1),
            jnp.clip(j + e, 0, n_xl - 1),
            jnp.clip(g + f, 0, n_gz - 1),
        )

    def on_ring(k):
        place = lax.rem(level + k + ring, ring)
        return (place // n_xl * half + low, lax.rem(place, n_xl), g)

    def in_group(k, layer):
        return (high * half + lax.rem(low + k, half), j, layer)

    barrier = pltpu.get_barrier_semaphore()
    count = jnp.int32(2 * quarter) + jnp.where(surface, half - 1, half)
    near_ring = [k for k in range(-quarter, quarter + 1) if k != 0]
    for k in near_ring:
        pl.semaphore_signal(barrier, inc=1, device_id=on_ring(k), device_id_type=MESH)

    def inside(place, count):
        return (place >= 0) & (place < count)

    def from_half_way(offset):
        _, e, f = offset
        ok = far_side & inside(j - e, n_xl) & inside(g - f, n_gz)
        place = jnp.clip(j - e, 0, n_xl - 1) + quarter
        return ok, (place // n_xl * half + half - 1, lax.rem(place, n_xl), jnp.clip(g - f, 0, n_gz - 1))

    def to_far_side(offset):
        _, e, f = offset
        place = level - quarter + e
        ok = forwards & inside(place, n_xl) & inside(g + f, n_gz)
        return ok, (half, jnp.clip(place, 0, n_xl - 1), jnp.clip(g + f, 0, n_gz - 1))

    for offset in OFFSETS:
        d = offset[0]
        hears = there(offset)
        if d == -1:
            hears = hears & jnp.logical_not(far_side)
        if d == 1:
            ok, whom = from_half_way(offset)

            @pl.when(ok)
            def _(whom=whom):
                pl.semaphore_signal(barrier, inc=1, device_id=whom, device_id_type=MESH)

            count = count + to_far_side(offset)[0].astype(jnp.int32)

        @pl.when(hears)
        def _(offset=offset):
            pl.semaphore_signal(barrier, inc=1, device_id=device(offset), device_id_type=MESH)

        direct = there(offset)
        if d == 1:
            direct = direct & jnp.logical_not(near_side)
        count = count + direct.astype(jnp.int32)

    @pl.when(surface)
    def _():
        for layer in range(n_gz):
            for k in range(half):
                if layer > 0 or k > 0:
                    pl.semaphore_signal(
                        barrier, inc=1, device_id=in_group(k, layer), device_id_type=MESH
                    )

    for copy in loads:
        copy.start()
    for copy in loads:
        copy.wait()

    def prepare(z, _):
        sin_t, cos_t = jnp.sin(field[3, z]), jnp.cos(field[3, z])
        sin_f, cos_f = jnp.sin(field[4, z]), jnp.cos(field[4, z])
        coef[0, z] = sin_t * sin_t * cos_f * cos_f
        coef[1, z] = sin_t * sin_t * sin_f * sin_f
        coef[2, z] = cos_t * cos_t
        coef[3, z] = 2.0 * sin_t * sin_t * sin_f * cos_f
        coef[4, z] = 2.0 * sin_t * cos_t * cos_f
        coef[5, z] = 2.0 * sin_t * cos_t * sin_f
        c, s = field[0, z], field[5, z]
        grow, lean = 1.0 + 2.0 * field[1, z], 1.0 + 2.0 * field[2, z]
        coef[6, z] = c * grow
        coef[7, z] = c * (s - grow)
        coef[8, z] = c * (1.0 - s)
        coef[9, z] = c * (lean - s)
        coef[10, z] = c * s
        coef[11, z] = 1.0 - field[6, z]
        return 0

    lax.fori_loop(0, depth, prepare, 0)

    n_traces = trace.shape[0]
    row, column, line = small_r[0], small_r[1], small_r[2]
    lines = small_g.shape[1]
    picked = jnp.where(iota((lines, n_traces), 0) == line, 1.0, 0.0).astype(jnp.float32)
    gains = jnp.dot(
        small_g[...],
        picked,
        precision=lax.Precision.HIGHEST,
        preferred_element_type=jnp.float32,
    )
    amplitude = (
        lax.dot_general(
            small_w[...],
            trace[...],
            (((1,), (1,)), ((), ())),
            precision=lax.Precision.HIGHEST,
            preferred_element_type=jnp.float32,
        )
        * gains
    )
    to_inl, to_xl = row >> 3, column >> 7
    cell = ((row & 7) << 7) + (column & 127) + 1
    to_high = jnp.where(to_inl >= half, 1, 0)
    to_low = to_inl - to_high * half
    owner = to_inl * n_xl + to_xl
    columns = n_inl * n_xl
    member = jnp.where(iota((columns, n_traces), 0) == owner, 1.0, 0.0).astype(jnp.float32)
    earlier = jnp.where(
        iota((n_traces, n_traces), 0) < iota((n_traces, n_traces), 1), 1.0, 0.0
    ).astype(jnp.float32)
    before = jnp.dot(
        member.astype(jnp.bfloat16),
        earlier.astype(jnp.bfloat16),
        preferred_element_type=jnp.float32,
    )
    rank = jnp.sum(member * before, axis=0, keepdims=True).astype(jnp.int32)
    to_level = to_high * n_xl + to_xl
    block = to_low - low
    block = jnp.where(block < 0, block + half, block)
    word = block * WORDS + rank
    spot = iota((along, n_traces), 0)
    content = (
        jnp.where(spot == word, amplitude[0:1, :], 0.0)
        + jnp.where(spot == word + SLOTS, amplitude[1:2, :], 0.0)
        + jnp.where(spot == word + 2 * SLOTS, cell.astype(jnp.float32), 0.0)
    )
    leaves = (to_inl == half - 1) & ((row & 7) >= 4)
    enters = (to_inl == half) & ((row & 7) < 4)
    far_level = jnp.where(leaves, n_xl + to_xl, to_xl)
    far_word = 2 * SLOTS * level + rank
    far_content = jnp.where(spot == far_word, amplitude[0:1, :], 0.0) + jnp.where(
        spot == far_word + SLOTS, cell.astype(jnp.float32), 0.0
    )

    def write(target, wanted, words):
        hop = target - level + ring // 2
        hop = jnp.where(hop < 0, hop + ring, jnp.where(hop >= ring, hop - ring, hop))
        address = (iota((RING, n_traces), 0) == hop) & wanted
        return lax.dot_general(
            jnp.where(address, 1.0, 0.0).astype(jnp.float32),
            words,
            (((1,), (1,)), ((), ())),
            precision=lax.Precision.HIGHEST,
            preferred_element_type=jnp.float32,
        )

    letters[0] = write(to_level, to_level >= 0, content)
    letters[1] = write(far_level, leaves | enters, far_content)

    lane = iota((across, along), 1)
    sub = iota((across, along), 0)

    def pack(turn):
        total = jnp.zeros((across, along), jnp.float32)
        for f in range(2):
            for z in range(depth):
                tile = f * depth + z
                moved = pltpu.roll(body[turn, f, 4 + z], (8 * tile + 4) % along, 1)
                total = jnp.where(lane // 8 == tile, moved, total)
        parcel[turn] = total

    pack(0)

    def copies(turn):
        out = []
        mine = body.at[turn]
        beside = side.at[turn]
        for number, offset in enumerate(OFFSETS):
            d, e, f = offset
            if e != 0:
                kind = 0
                if f != 0:
                    kind = 1 if f == 1 else 2
                if d != 0:
                    kind = 3 if d == 1 else 4
                source = parcel.at[turn]
                target = packed.at[turn, kind, 0 if e == 1 else 1]
            else:
                deep = {0: (4, 8, 4), 1: (8, 4, 0), -1: (4, 4, 12)}[f]
                if d == 0:
                    source = mine.at[:, pl.ds(deep[0], deep[1])]
                    target = mine.at[:, pl.ds(deep[2], deep[1])]
                else:
                    wide = pl.ds(4 if d == 1 else 0, 4)
                    source = mine.at[:, pl.ds(deep[0], deep[1]), wide]
                    target = beside.at[:, pl.ds(deep[2], deep[1]), wide]
            out.append(
                pltpu.make_async_remote_copy(
                    src_ref=source,
                    dst_ref=target,
                    send_sem=send_sem.at[turn, number],
                    recv_sem=recv_sem.at[turn, number],
                    device_id=device(offset),
                    device_id_type=MESH,
                )
            )
        return out

    def sends(turn, offset):
        if turn == 0 and offset[0] == 1:
            return there(offset) & jnp.logical_not(near_side)
        return there(offset)

    def begin(turn):
        for offset, copy in zip(OFFSETS, copies(turn)):

            @pl.when(sends(turn, offset))
            def _(copy=copy):
                copy.start()

    def arrive(turn):
        for offset, copy in zip(OFFSETS, copies(turn)):

            @pl.when(there(tuple(-d for d in offset)))
            def _(copy=copy):
                copy.wait_recv()

    def depart(turn):
        for offset, copy in zip(OFFSETS, copies(turn)):

            @pl.when(sends(turn, offset))
            def _(copy=copy):
                copy.wait_send()

    def to_half_way(part):
        source = body.at[0, :, pl.ds(4, depth), pl.ds(4, 4)] if part == 0 else parcel.at[0]
        return pltpu.make_async_remote_copy(
            src_ref=source,
            dst_ref=passing if part == 0 else passing_parcel,
            send_sem=pass_send.at[part],
            recv_sem=pass_recv.at[part],
            device_id=on_ring(quarter),
            device_id_type=MESH,
        )

    def onward(number):
        _, e, f = OFFSETS[number]
        if e != 0:
            source = passing_parcel
            target = packed.at[0, 3, 0 if e == 1 else 1]
        else:
            first, deep, goal = {0: (0, 8, 4), 1: (4, 4, 0), -1: (0, 4, 12)}[f]
            source = passing.at[:, pl.ds(first, deep)]
            target = side.at[0, :, pl.ds(goal, deep), pl.ds(4, 4)]
        return pltpu.make_async_remote_copy(
            src_ref=source,
            dst_ref=target,
            send_sem=onward_send.at[number],
            recv_sem=recv_sem.at[0, number],
            device_id=to_far_side(OFFSETS[number])[1],
            device_id_type=MESH,
        )

    crossing = [number for number, offset in enumerate(OFFSETS) if offset[0] == 1]

    def letter(k):
        rows = pl.ds(2 * (k + quarter), 2)
        return pltpu.make_async_remote_copy(
            src_ref=letters.at[:, rows],
            dst_ref=transit.at[:, rows],
            send_sem=letter_send.at[k + quarter],
            recv_sem=letter_recv.at[k + quarter],
            device_id=on_ring(k),
            device_id_type=MESH,
        )

    def relay_rows(k):
        first = max(2 * (k + quarter) - 1, 0)
        return first, min(2 * (k + quarter) + 1, ring) - first

    def relay(k):
        rows = pl.ds(*relay_rows(k))
        return pltpu.make_async_remote_copy(
            src_ref=transit.at[:, rows],
            dst_ref=mail.at[:, rows],
            send_sem=relay_send.at[k + quarter],
            recv_sem=relay_recv.at[k + quarter],
            device_id=on_ring(k),
            device_id_type=MESH,
        )

    def parcel_of(k, layer):
        return pltpu.make_async_remote_copy(
            src_ref=bundle.at[:, pl.ds(k, 1)],
            dst_ref=heap.at[layer, :, pl.ds(k, 1)],
            send_sem=bundle_send.at[k],
            recv_sem=bundle_recv.at[layer, k],
            device_id=in_group(k, 0),
            device_id_type=MESH,
        )

    def far_parcel(layer, place):
        return pltpu.make_async_remote_copy(
            src_ref=bundle_far,
            dst_ref=heap_far.at[layer, place],
            send_sem=far_send,
            recv_sem=far_recv.at[layer, place],
            device_id=(high * half + border, j, 0),
            device_id_type=MESH,
        )

    def post():
        for k in near_ring:
            relay(k).wait_recv()
        for t in range(2):
            got = mail[0, 8 * t : 8 * t + 8, :]
            turned = jnp.zeros((GROUP, along), jnp.float32)
            for d in range(GROUP):
                moved = got if d == 0 else pltpu.roll(pltpu.roll(got, d, 0), along - WORDS * d, 1)
                turned = jnp.where(((sub - lane // WORDS) & 7) == d, moved, turned)
            bundle[t] = turned
        far = jnp.sum(mail[1], axis=0, keepdims=True)
        bundle_far[...] = jnp.where(sub == low, far, 0.0)
        for k in range(1, half):
            parcel_of(k, g).start()

        @pl.when(jnp.logical_not(surface))
        def _():
            parcel_of(0, g).start()

        @pl.when(surface)
        def _():
            heap[0, :, 0:1] = bundle[:, 0:1]

        @pl.when(jnp.logical_not(surface & on_border))
        def _():
            far_parcel(g, low).start()

        @pl.when(surface & on_border)
        def _():
            heap_far[0, border] = bundle_far[...]

    pl.semaphore_wait(barrier, count)
    for k in range(-quarter, quarter):
        if k != 0:
            letter(k).start()

    @pl.when(near_side)
    def _():
        for part in range(2):
            to_half_way(part).start()

    begin(0)

    @pl.when(forwards)
    def _():
        pl.semaphore_signal(known, inc=1, device_id=on_ring(-quarter), device_id_type=MESH)
        for part in range(2):
            to_half_way(part).wait_recv()
        for number in crossing:

            @pl.when(to_far_side(OFFSETS[number])[0])
            def _(number=number):
                onward(number).start()

    own = pl.ds(2 * quarter, 2)
    transit[:, own] = letters[:, own]
    for k in range(-quarter, quarter):
        if k != 0:
            letter(k).wait_recv()
    for k in near_ring:
        relay(k).start()
    kept = pl.ds(*relay_rows(0))
    mail[:, kept] = transit[:, kept]

    def unpack(turn):
        def pair(kind):
            return jnp.where(lane % 8 < 4, packed[turn, kind, 0], packed[turn, kind, 1])

        plain = pair(0)
        deep = jnp.where((lane // 8) % 8 >= 4, pair(1), pair(2))
        wide = jnp.where(sub < 4, pair(4), pair(3))
        for f in range(2):
            for z in range(depth):
                turnback = (along - 4 - 8 * (f * depth + z)) % along
                edge_y[f, 4 + z] = pltpu.roll(plain, turnback, 1)
                edge_y[f, z - 4 if z >= 4 else 12 + z] = pltpu.roll(deep, turnback, 1)
                edge_xy[f, z] = pltpu.roll(wide, turnback, 1)

    def advance(turn, store):
        def layer(z, _):
            first, whole = [], []
            for f in range(2):
                center = body[turn, f, z + 4]
                beside = side[turn, f, z + 4]
                edge = edge_y[f, z + 4]
                above = [body[turn, f, z + 4 + k] for k in range(1, 5)]
                below = [body[turn, f, z + 4 - k] for k in range(1, 5)]
                u_zz = bend(center, above, below)
                grad_z = slope(above, below)
                grad_z_side = slope(
                    [side[turn, f, z + 4 + k] for k in range(1, 5)],
                    [side[turn, f, z + 4 - k] for k in range(1, 5)],
                )
                grad_z_edge = slope(
                    [edge_y[f, z + 4 + k] for k in range(1, 5)],
                    [edge_y[f, z + 4 - k] for k in range(1, 5)],
                )
                x_moves = shifted(center, beside, 0)
                u_xx = bend(center, *x_moves)
                grad_x = slope(*x_moves)
                grad_x_edge = slope(*shifted(edge, edge_xy[f, z], 0))
                u_yy = bend(center, *shifted(center, edge, 1))
                u_xy = slope(*shifted(grad_x, grad_x_edge, 1))
                u_xz = slope(*shifted(grad_z, grad_z_side, 0))
                u_yz = slope(*shifted(grad_z, grad_z_edge, 1))
                first.append(
                    coef[0, z] * u_xx
                    + coef[1, z] * u_yy
                    + coef[2, z] * u_zz
                    + coef[3, z] * u_xy
                    + coef[4, z] * u_xz
                    + coef[5, z] * u_yz
                )
                whole.append(u_xx + u_yy + u_zz)
            stay = coef[11, z]
            now_p, now_q = body[turn, 0, z + 4], body[turn, 1, z + 4]
            if turn == 0:
                was_p, was_q = old[0, z], old[1, z]
            else:
                was_p, was_q = body[0, 0, z + 4], body[0, 1, z + 4]
            mixed = coef[8, z] * first[1]
            new_p = (
                now_p
                + stay * (now_p - was_p)
                + (coef[6, z] * whole[0] + coef[7, z] * first[0] + mixed)
            )
            new_q = (
                now_q
                + stay * (now_q - was_q)
                + (coef[9, z] * (whole[0] - first[0]) + coef[10, z] * whole[1] + mixed)
            )
            store(z, new_p, new_q)
            return 0

        lax.fori_loop(0, depth, layer, 0)

    def keep(z, new_p, new_q):
        body[1, 0, z + 4] = new_p
        body[1, 1, z + 4] = new_q

    def finish(z, new_p, new_q):
        next_p[z] = new_p
        next_q[z] = new_q

    late = (high == 0) & on_border

    @pl.when(late)
    def _():
        post()

    arrive(0)
    unpack(0)
    advance(0, keep)
    pack(1)

    @pl.when(near_side)
    def _():
        pl.semaphore_wait(known, 1)

    begin(1)

    @pl.when(jnp.logical_not(late))
    def _():
        post()

    def add_up(label, values):
        label_x, label_y = label >> 7, label & 127
        pieces = []
        for rest in values:
            for _ in range(3):
                rounded = rest.astype(jnp.bfloat16).astype(jnp.float32)
                pieces.append(rounded)
                rest = rest - rounded
        total = jnp.zeros((len(pieces) * across, along), jnp.float32)
        for r in range(0, 2 * GROUP, 2):

            def flat(array):
                return jnp.concatenate([array[r : r + 1], array[r + 1 : r + 2]], axis=1)

            at_x = iota((across, 2 * along), 0) == flat(label_x)
            left = jnp.concatenate([jnp.where(at_x, flat(piece), 0.0) for piece in pieces], axis=0)
            right = jnp.where(iota((along, 2 * along), 0) == flat(label_y), 1.0, 0.0)
            total = total + lax.dot_general(
                left.astype(jnp.bfloat16),
                right.astype(jnp.bfloat16),
                (((1,), (1,)), ((), ())),
                preferred_element_type=jnp.float32,
            )
        return [
            total[24 * k : 24 * k + 8] + total[24 * k + 8 : 24 * k + 16] + total[24 * k + 16 : 24 * k + 24]
            for k in range(len(values))
        ]

    def plane_there(d, e):
        crosses = jnp.bool_(False)
        if d == 1:
            crosses = i == half - 1
        if d == -1:
            crosses = i == half
        return there((d, e, 0)) & jnp.logical_not(crosses)

    def plane_copy(number):
        d, e = BESIDE[number]
        if e == 0:
            rows = pl.ds(4 if d == 1 else 0, 4)
            source, target = plane.at[0, rows], plane_side.at[rows]
        else:
            source, target = plane_parcel, plane_packed.at[{0: 0, 1: 1, -1: 2}[d], 0 if e == 1 else 1]
        return pltpu.make_async_remote_copy(
            src_ref=source,
            dst_ref=target,
            send_sem=plane_send.at[number],
            recv_sem=plane_recv.at[number],
            device_id=device((d, e, 0)),
            device_id_type=MESH,
        )

    @pl.when(surface)
    def _():
        for layer in range(n_gz):
            for k in range(half):
                if layer > 0 or k > 0:
                    parcel_of(k, layer).wait_recv()
        place = iota((2 * GROUP, along), 1) % WORDS // SLOTS
        parts = [heap[layer].reshape(2 * GROUP, along) for layer in range(4)]

        def gather(kind):
            total = jnp.zeros((2 * GROUP, along), jnp.float32)
            for layer in range(4):
                shift = SLOTS * (layer - kind) % along
                moved = parts[layer] if shift == 0 else pltpu.roll(parts[layer], shift, 1)
                total = jnp.where(place == layer, moved, total)
            return total

        sums = add_up(gather(2).astype(jnp.int32) - 1, [gather(0), gather(1)])
        plane[0] = sums[0]
        plane[1] = sums[1]

    @pl.when(surface & on_border)
    def _():
        for layer in range(n_gz):
            for place in range(half):

                @pl.when((layer > 0) | (border != place))
                def _(layer=layer, place=place):
                    far_parcel(layer, place).wait_recv()

        parts = [jnp.sum(heap_far[layer], axis=0) for layer in range(4)]
        front = lane % 8 < 4
        values, labels = [], []
        for k in (0, 2):
            values.append(jnp.where(front, parts[k], pltpu.roll(parts[k + 1], SLOTS, 1)))
            labels.append(jnp.where(front, pltpu.roll(parts[k], along - SLOTS, 1), parts[k + 1]))
        label = jnp.concatenate(labels, axis=0).astype(jnp.int32) - 1
        [total] = add_up(label, [jnp.concatenate(values, axis=0)])
        plane_far[...] = total

        @pl.when(high == 0)
        def _():
            plane_side[0:4] = total[0:4]

        @pl.when(high != 0)
        def _():
            plane_side[4:8] = total[4:8]

    @pl.when(surface)
    def _():
        plane_parcel[...] = jnp.where(
            lane < 8, pltpu.roll(plane[0], 4, 1), pltpu.roll(plane_far[...], 12, 1)
        )
        for number, (d, e) in enumerate(BESIDE):

            @pl.when(plane_there(d, e))
            def _(number=number):
                plane_copy(number).start()

    depart(1)
    arrive(1)
    unpack(1)

    @pl.when(surface)
    def _():
        for number, (d, e) in enumerate(BESIDE):

            @pl.when(plane_there(-d, -e))
            def _(number=number):
                plane_copy(number).wait_recv()

        def pair(kind):
            return jnp.where(lane % 8 < 4, plane_packed[kind, 0], plane_packed[kind, 1])

        same = pair(0)
        edge = pltpu.roll(same, along - 4, 1)
        corner = pltpu.roll(jnp.where(sub < 4, pair(2), pair(1)), along - 4, 1) + pltpu.roll(
            same, along - 12, 1
        )
        for f in range(2):
            body[1, f, 4] = body[1, f, 4] + plane[0]
            side[1, f, 4] = side[1, f, 4] + plane_side[...]
            edge_y[f, 4] = edge_y[f, 4] + edge
            edge_xy[f, 0] = edge_xy[f, 0] + corner

    for f, prior in enumerate((prior_p, prior_q)):
        prior[...] = body[1, f, 4:12]
    advance(1, finish)

    @pl.when(surface)
    def _():
        for result in (next_p, next_q):
            result[0] = result[0] + plane[1]

    depart(0)

    @pl.when(near_side)
    def _():
        for part in range(2):
            to_half_way(part).wait_send()

    @pl.when(forwards)
    def _():
        for number in crossing:

            @pl.when(to_far_side(OFFSETS[number])[0])
            def _(number=number):
                onward(number).wait_send()

    for k in range(-quarter, quarter):
        if k != 0:
            letter(k).wait_send()
    for k in near_ring:
        relay(k).wait_send()
    for k in range(1, half):
        parcel_of(k, g).wait_send()

    @pl.when(jnp.logical_not(surface))
    def _():
        parcel_of(0, g).wait_send()

    @pl.when(jnp.logical_not(surface & on_border))
    def _():
        far_parcel(g, low).wait_send()

    @pl.when(surface)
    def _():
        for number, (d, e) in enumerate(BESIDE):

            @pl.when(plane_there(d, e))
            def _(number=number):
                plane_copy(number).wait_send()


def hand_over(*refs):
    sources, targets, sem = refs[:4], refs[4:8], refs[8]
    copies = [pltpu.make_async_copy(a, b, sem.at[k]) for k, (a, b) in enumerate(zip(sources, targets))]
    for copy in copies:
        copy.start()
    for copy in copies:
        copy.wait()


def local(sizes, *args):
    fields = args[:11]
    samples, weights, gain, row, column, line = args[11:]
    block = fields[0].shape
    n_traces = samples.shape[0]
    receivers = [ids.reshape(1, -1) for ids in (row, column, line)]
    f32 = jnp.float32
    outs = pl.pallas_call(
        functools.partial(kernel, sizes),
        out_shape=[pltpu.VMEM(block, f32)] * 4,
        in_specs=[pl.BlockSpec(memory_space=pltpu.HBM)] * 17,
        out_specs=[pl.BlockSpec(memory_space=pltpu.VMEM)] * 4,
        scratch_shapes=[
            pltpu.VMEM((2, 2, 16, 8, 128), f32),
            pltpu.VMEM((2, 2, 16, 8, 128), f32),
            pltpu.VMEM((2, 5, 2, 8, 128), f32),
            pltpu.VMEM((2, 8, 128), f32),
            pltpu.VMEM((2, 16, 8, 128), f32),
            pltpu.VMEM((2, 8, 8, 128), f32),
            pltpu.VMEM((2, 8, 8, 128), f32),
            pltpu.VMEM((7, 8, 8, 128), f32),
            pltpu.VMEM((12, 8, 8, 128), f32),
            pltpu.VMEM(samples.shape, f32),
            pltpu.VMEM(weights.shape, f32),
            pltpu.VMEM((1, gain.shape[0]), f32),
            pltpu.VMEM((3, 1, n_traces), jnp.int32),
            pltpu.VMEM((2, RING, 128), f32),
            pltpu.VMEM((2, RING, 128), f32),
            pltpu.VMEM((2, RING, 128), f32),
            pltpu.VMEM((2, 8, 4, 128), f32),
            pltpu.VMEM((8, 128), f32),
            pltpu.VMEM((2, GROUP, 128), f32),
            pltpu.VMEM((8, 128), f32),
            pltpu.VMEM((4, 2, GROUP, 128), f32),
            pltpu.VMEM((4, GROUP, 8, 128), f32),
            pltpu.VMEM((2, 8, 128), f32),
            pltpu.VMEM((8, 128), f32),
            pltpu.VMEM((8, 128), f32),
            pltpu.VMEM((8, 128), f32),
            pltpu.VMEM((3, 2, 8, 128), f32),
            pltpu.SemaphoreType.DMA((17,)),
            pltpu.SemaphoreType.DMA((2, len(OFFSETS))),
            pltpu.SemaphoreType.DMA((2, len(OFFSETS))),
            pltpu.SemaphoreType.DMA((9,)),
            pltpu.SemaphoreType.DMA((9,)),
            pltpu.SemaphoreType.DMA((9,)),
            pltpu.SemaphoreType.DMA((9,)),
            pltpu.SemaphoreType.DMA((GROUP,)),
            pltpu.SemaphoreType.DMA((4, GROUP)),
            pltpu.SemaphoreType.DMA,
            pltpu.SemaphoreType.DMA((4, GROUP)),
            pltpu.SemaphoreType.DMA((8,)),
            pltpu.SemaphoreType.DMA((8,)),
            pltpu.SemaphoreType.DMA((2,)),
            pltpu.SemaphoreType.DMA((2,)),
            pltpu.SemaphoreType.DMA((len(OFFSETS),)),
            pltpu.SemaphoreType.REGULAR,
        ],
        compiler_params=pltpu.CompilerParams(
            collective_id=0, has_side_effects=True, vmem_limit_bytes=60 * 2**20
        ),
        name="wave_steps",
    )(*fields, samples, weights, gain.reshape(1, -1), *receivers)
    return pl.pallas_call(
        hand_over,
        out_shape=[jax.ShapeDtypeStruct(block, f32)] * 4,
        in_specs=[pl.BlockSpec(memory_space=pl.ANY)] * 4,
        out_specs=[pl.BlockSpec(memory_space=pltpu.HBM)] * 4,
        scratch_shapes=[pltpu.SemaphoreType.DMA((4,))],
        compiler_params=pltpu.CompilerParams(vmem_limit_bytes=2**20),
        name="hand_over",
    )(*outs)


def solution(mesh):
    sizes = tuple(mesh.shape[axis] for axis in ("inl", "xl", "gz"))
    cells = P("gz", "inl", "xl")
    traces = P(("inl", "xl", "gz"))
    return jax.shard_map(
        functools.partial(local, sizes),
        mesh=mesh,
        in_specs=(cells,) * 11 + (P(("inl", "xl", "gz"), None), P(), P(), traces, traces, traces),
        out_specs=(cells,) * 4,
        check_vma=False,
    )
```

```python
import functools

import jax
import jax.numpy as jnp
from jax import lax
from jax.experimental import pallas as pl
from jax.experimental.pallas import tpu as pltpu
from jax.sharding import PartitionSpec as P

MESH = pl.DeviceIdType.MESH
second_coef = (-205.0 / 72.0, 8.0 / 5.0, -1.0 / 5.0, 8.0 / 315.0, -1.0 / 560.0)
first_coef = (0.0, 4.0 / 5.0, -1.0 / 5.0, 4.0 / 105.0, -1.0 / 280.0)

OFFSETS = (
    [(d, 0, 0) for d in (1, -1)]
    + [(d, 0, e) for d in (1, -1) for e in (1, -1)]
    + [(d, e, 0) for d in (1, -1) for e in (1, -1)]
    + [(0, d, e) for d in (1, -1) for e in (1, -1)]
    + [(0, d, 0) for d in (1, -1)]
    + [(0, 0, d) for d in (1, -1)]
)
RING = 16
GROUP = 8
SLOTS = 4
WORDS = 16
BESIDE = [(d, e) for d in (1, -1, 0) for e in (1, -1, 0) if d != 0 or e != 0]


def iota(shape, axis):
    return lax.broadcasted_iota(jnp.int32, shape, axis)


def shifted(body, halo, axis):
    size = body.shape[axis]
    place = iota(body.shape, axis)
    above = [pltpu.roll(jnp.where(place < k, halo, body), size - k, axis) for k in range(1, 5)]
    below = [pltpu.roll(jnp.where(place >= size - k, halo, body), k, axis) for k in range(1, 5)]
    return above, below


def slope(above, below):
    total = first_coef[1] * (above[0] - below[0])
    for k in range(2, 5):
        total = total + first_coef[k] * (above[k - 1] - below[k - 1])
    return total


def bend(center, above, below):
    total = second_coef[0] * center
    for k in range(1, 5):
        total = total + second_coef[k] * (above[k - 1] + below[k - 1])
    return total


def kernel(sizes, *refs):
    n_inl, n_xl, n_gz = sizes
    (
        wave_p,
        wave_p_old,
        wave_q,
        wave_q_old,
        courant,
        epsilon,
        delta,
        tilt,
        azimuth,
        shear,
        damping,
        samples,
        weights,
        gain,
        inline,
        crossline,
        shot,
        next_p,
        next_q,
        prior_p,
        prior_q,
        body,
        side,
        packed,
        parcel,
        edge_y,
        edge_xy,
        old,
        field,
        coef,
        trace,
        small_w,
        small_g,
        small_r,
        letters,
        transit,
        mail,
        passing,
        passing_parcel,
        bundle,
        bundle_far,
        heap,
        heap_far,
        plane,
        plane_far,
        plane_side,
        plane_parcel,
        plane_packed,
        load_sem,
        send_sem,
        recv_sem,
        letter_send,
        letter_recv,
        relay_send,
        relay_recv,
        bundle_send,
        bundle_recv,
        far_send,
        far_recv,
        plane_send,
        plane_recv,
        pass_send,
        pass_recv,
        onward_send,
        known,
    ) = refs
    i = lax.axis_index("inl")
    j = lax.axis_index("xl")
    g = lax.axis_index("gz")
    depth, across, along = 8, 8, 128
    half = n_inl // 2
    ring = 2 * n_xl
    high, low = i // half, i % half
    level = high * n_xl + j
    quarter = ring // 4
    border = jnp.where(high == 0, half - 1, 0)
    on_border = low == border
    surface = g == 0
    near_side, far_side = i == half - 1, i == half
    forwards = (low == half - 1) & (level >= quarter) & (level < quarter + n_xl)

    loads = [
        (wave_p, body.at[0, 0, pl.ds(4, depth)]),
        (wave_q, body.at[0, 1, pl.ds(4, depth)]),
        (wave_p_old, old.at[0]),
        (wave_q_old, old.at[1]),
        (courant, field.at[0]),
        (epsilon, field.at[1]),
        (delta, field.at[2]),
        (tilt, field.at[3]),
        (azimuth, field.at[4]),
        (shear, field.at[5]),
        (damping, field.at[6]),
        (samples, trace),
        (weights, small_w),
        (gain, small_g),
        (inline, small_r.at[0]),
        (crossline, small_r.at[1]),
        (shot, small_r.at[2]),
    ]
    loads = [pltpu.make_async_copy(a, b, load_sem.at[k]) for k, (a, b) in enumerate(loads)]
    nothing = jnp.zeros((2, 4, across, along), jnp.float32)
    for turn in range(2):
        body[turn, :, 0:4] = nothing
        body[turn, :, 12:16] = nothing
        for k in range(4):
            side[turn, :, 4 * k : 4 * k + 4] = nothing
        packed[turn] = jnp.zeros((5, 2, across, along), jnp.float32)
    mail[...] = jnp.zeros((2, RING, along), jnp.float32)
    heap[...] = jnp.zeros((4, 2, GROUP, along), jnp.float32)
    for layer in range(4):
        heap_far[layer] = jnp.zeros((GROUP, across, along), jnp.float32)
    plane_far[...] = jnp.zeros((across, along), jnp.float32)
    plane_side[...] = jnp.zeros((across, along), jnp.float32)
    plane_packed[...] = jnp.zeros((3, 2, across, along), jnp.float32)

    def there(offset):
        d, e, f = offset
        ok = []
        for step, place, count in ((d, i, n_inl), (e, j, n_xl), (f, g, n_gz)):
            if step == 1:
                ok.append(place < count - 1)
            if step == -1:
                ok.append(place > 0)
        return functools.reduce(jnp.logical_and, ok)

    def device(offset):
        d, e, f = offset
        return (
            jnp.clip(i + d, 0, n_inl - 1),
            jnp.clip(j + e, 0, n_xl - 1),
            jnp.clip(g + f, 0, n_gz - 1),
        )

    def on_ring(k):
        place = lax.rem(level + k + ring, ring)
        return (place // n_xl * half + low, lax.rem(place, n_xl), g)

    def in_group(k, layer):
        return (high * half + lax.rem(low + k, half), j, layer)

    barrier = pltpu.get_barrier_semaphore()
    count = jnp.int32(2 * quarter) + jnp.where(surface, half - 1, half)
    near_ring = [k for k in range(-quarter, quarter + 1) if k != 0]
    for k in near_ring:
        pl.semaphore_signal(barrier, inc=1, device_id=on_ring(k), device_id_type=MESH)

    def inside(place, count):
        return (place >= 0) & (place < count)

    def from_half_way(offset):
        _, e, f = offset
        ok = far_side & inside(j - e, n_xl) & inside(g - f, n_gz)
        place = jnp.clip(j - e, 0, n_xl - 1) + quarter
        return ok, (place // n_xl * half + half - 1, lax.rem(place, n_xl), jnp.clip(g - f, 0, n_gz - 1))

    def to_far_side(offset):
        _, e, f = offset
        place = level - quarter + e
        ok = forwards & inside(place, n_xl) & inside(g + f, n_gz)
        return ok, (half, jnp.clip(place, 0, n_xl - 1), jnp.clip(g + f, 0, n_gz - 1))

    for offset in OFFSETS:
        d = offset[0]
        hears = there(offset)
        if d == -1:
            hears = hears & jnp.logical_not(far_side)
        if d == 1:
            ok, whom = from_half_way(offset)

            @pl.when(ok)
            def _(whom=whom):
                pl.semaphore_signal(barrier, inc=1, device_id=whom, device_id_type=MESH)

            count = count + to_far_side(offset)[0].astype(jnp.int32)

        @pl.when(hears)
        def _(offset=offset):
            pl.semaphore_signal(barrier, inc=1, device_id=device(offset), device_id_type=MESH)

        direct = there(offset)
        if d == 1:
            direct = direct & jnp.logical_not(near_side)
        count = count + direct.astype(jnp.int32)

    @pl.when(surface)
    def _():
        for layer in range(n_gz):
            for k in range(half):
                if layer > 0 or k > 0:
                    pl.semaphore_signal(
                        barrier, inc=1, device_id=in_group(k, layer), device_id_type=MESH
                    )

    for copy in loads:
        copy.start()
    for copy in loads:
        copy.wait()

    def prepare(z, _):
        sin_t, cos_t = jnp.sin(field[3, z]), jnp.cos(field[3, z])
        sin_f, cos_f = jnp.sin(field[4, z]), jnp.cos(field[4, z])
        coef[0, z] = sin_t * sin_t * cos_f * cos_f
        coef[1, z] = sin_t * sin_t * sin_f * sin_f
        coef[2, z] = cos_t * cos_t
        coef[3, z] = 2.0 * sin_t * sin_t * sin_f * cos_f
        coef[4, z] = 2.0 * sin_t * cos_t * cos_f
        coef[5, z] = 2.0 * sin_t * cos_t * sin_f
        c, s = field[0, z], field[5, z]
        grow, lean = 1.0 + 2.0 * field[1, z], 1.0 + 2.0 * field[2, z]
        coef[6, z] = c * grow
        coef[7, z] = c * (s - grow)
        coef[8, z] = c * (1.0 - s)
        coef[9, z] = c * (lean - s)
        coef[10, z] = c * s
        coef[11, z] = 1.0 - field[6, z]
        return 0

    lax.fori_loop(0, depth, prepare, 0)

    n_traces = trace.shape[0]
    row, column, line = small_r[0], small_r[1], small_r[2]
    lines = small_g.shape[1]
    picked = jnp.where(iota((lines, n_traces), 0) == line, 1.0, 0.0).astype(jnp.float32)
    gains = jnp.dot(
        small_g[...],
        picked,
        precision=lax.Precision.HIGHEST,
        preferred_element_type=jnp.float32,
    )
    amplitude = (
        lax.dot_general(
            small_w[...],
            trace[...],
            (((1,), (1,)), ((), ())),
            precision=lax.Precision.HIGHEST,
            preferred_element_type=jnp.float32,
        )
        * gains
    )
    to_inl, to_xl = row >> 3, column >> 7
    cell = ((row & 7) << 7) + (column & 127) + 1
    to_high = jnp.where(to_inl >= half, 1, 0)
    to_low = to_inl - to_high * half
    owner = to_inl * n_xl + to_xl
    columns = n_inl * n_xl
    member = jnp.where(iota((columns, n_traces), 0) == owner, 1.0, 0.0).astype(jnp.float32)
    earlier = jnp.where(
        iota((n_traces, n_traces), 0) < iota((n_traces, n_traces), 1), 1.0, 0.0
    ).astype(jnp.float32)
    before = jnp.dot(
        member.astype(jnp.bfloat16),
        earlier.astype(jnp.bfloat16),
        preferred_element_type=jnp.float32,
    )
    rank = jnp.sum(member * before, axis=0, keepdims=True).astype(jnp.int32)
    to_level = to_high * n_xl + to_xl
    block = to_low - low
    block = jnp.where(block < 0, block + half, block)
    word = block * WORDS + rank
    spot = iota((along, n_traces), 0)
    content = (
        jnp.where(spot == word, amplitude[0:1, :], 0.0)
        + jnp.where(spot == word + SLOTS, amplitude[1:2, :], 0.0)
        + jnp.where(spot == word + 2 * SLOTS, cell.astype(jnp.float32), 0.0)
    )
    leaves = (to_inl == half - 1) & ((row & 7) >= 4)
    enters = (to_inl == half) & ((row & 7) < 4)
    far_level = jnp.where(leaves, n_xl + to_xl, to_xl)
    far_word = 2 * SLOTS * level + rank
    far_content = jnp.where(spot == far_word, amplitude[0:1, :], 0.0) + jnp.where(
        spot == far_word + SLOTS, cell.astype(jnp.float32), 0.0
    )

    def write(target, wanted, words):
        hop = target - level + ring // 2
        hop = jnp.where(hop < 0, hop + ring, jnp.where(hop >= ring, hop - ring, hop))
        address = (iota((RING, n_traces), 0) == hop) & wanted
        return lax.dot_general(
            jnp.where(address, 1.0, 0.0).astype(jnp.float32),
            words,
            (((1,), (1,)), ((), ())),
            precision=lax.Precision.HIGHEST,
            preferred_element_type=jnp.float32,
        )

    letters[0] = write(to_level, to_level >= 0, content)
    letters[1] = write(far_level, leaves | enters, far_content)

    lane = iota((across, along), 1)
    sub = iota((across, along), 0)

    def pack(turn):
        total = jnp.zeros((across, along), jnp.float32)
        for f in range(2):
            for z in range(depth):
                tile = f * depth + z
                moved = pltpu.roll(body[turn, f, 4 + z], (8 * tile + 4) % along, 1)
                total = jnp.where(lane // 8 == tile, moved, total)
        parcel[turn] = total

    pack(0)

    def copies(turn):
        out = []
        mine = body.at[turn]
        beside = side.at[turn]
        for number, offset in enumerate(OFFSETS):
            d, e, f = offset
            if e != 0:
                kind = 0
                if f != 0:
                    kind = 1 if f == 1 else 2
                if d != 0:
                    kind = 3 if d == 1 else 4
                source = parcel.at[turn]
                target = packed.at[turn, kind, 0 if e == 1 else 1]
            else:
                deep = {0: (4, 8, 4), 1: (8, 4, 0), -1: (4, 4, 12)}[f]
                if d == 0:
                    source = mine.at[:, pl.ds(deep[0], deep[1])]
                    target = mine.at[:, pl.ds(deep[2], deep[1])]
                else:
                    wide = pl.ds(4 if d == 1 else 0, 4)
                    source = mine.at[:, pl.ds(deep[0], deep[1]), wide]
                    target = beside.at[:, pl.ds(deep[2], deep[1]), wide]
            out.append(
                pltpu.make_async_remote_copy(
                    src_ref=source,
                    dst_ref=target,
                    send_sem=send_sem.at[turn, number],
                    recv_sem=recv_sem.at[turn, number],
                    device_id=device(offset),
                    device_id_type=MESH,
                )
            )
        return out

    def sends(turn, offset):
        if turn == 0 and offset[0] == 1:
            return there(offset) & jnp.logical_not(near_side)
        return there(offset)

    def begin(turn):
        for offset, copy in zip(OFFSETS, copies(turn)):

            @pl.when(sends(turn, offset))
            def _(copy=copy):
                copy.start()

    def arrive(turn):
        for offset, copy in zip(OFFSETS, copies(turn)):

            @pl.when(there(tuple(-d for d in offset)))
            def _(copy=copy):
                copy.wait_recv()

    def depart(turn):
        for offset, copy in zip(OFFSETS, copies(turn)):

            @pl.when(sends(turn, offset))
            def _(copy=copy):
                copy.wait_send()

    def to_half_way(part):
        source = body.at[0, :, pl.ds(4, depth), pl.ds(4, 4)] if part == 0 else parcel.at[0]
        return pltpu.make_async_remote_copy(
            src_ref=source,
            dst_ref=passing if part == 0 else passing_parcel,
            send_sem=pass_send.at[part],
            recv_sem=pass_recv.at[part],
            device_id=on_ring(quarter),
            device_id_type=MESH,
        )

    def onward(number):
        _, e, f = OFFSETS[number]
        if e != 0:
            source = passing_parcel
            target = packed.at[0, 3, 0 if e == 1 else 1]
        else:
            first, deep, goal = {0: (0, 8, 4), 1: (4, 4, 0), -1: (0, 4, 12)}[f]
            source = passing.at[:, pl.ds(first, deep)]
            target = side.at[0, :, pl.ds(goal, deep), pl.ds(4, 4)]
        return pltpu.make_async_remote_copy(
            src_ref=source,
            dst_ref=target,
            send_sem=onward_send.at[number],
            recv_sem=recv_sem.at[0, number],
            device_id=to_far_side(OFFSETS[number])[1],
            device_id_type=MESH,
        )

    crossing = [number for number, offset in enumerate(OFFSETS) if offset[0] == 1]

    def letter(k):
        rows = pl.ds(2 * (k + quarter), 2)
        return pltpu.make_async_remote_copy(
            src_ref=letters.at[:, rows],
            dst_ref=transit.at[:, rows],
            send_sem=letter_send.at[k + quarter],
            recv_sem=letter_recv.at[k + quarter],
            device_id=on_ring(k),
            device_id_type=MESH,
        )

    def relay_rows(k):
        first = max(2 * (k + quarter) - 1, 0)
        return first, min(2 * (k + quarter) + 1, ring) - first

    def relay(k):
        rows = pl.ds(*relay_rows(k))
        return pltpu.make_async_remote_copy(
            src_ref=transit.at[:, rows],
            dst_ref=mail.at[:, rows],
            send_sem=relay_send.at[k + quarter],
            recv_sem=relay_recv.at[k + quarter],
            device_id=on_ring(k),
            device_id_type=MESH,
        )

    def parcel_of(k, layer):
        return pltpu.make_async_remote_copy(
            src_ref=bundle.at[:, pl.ds(k, 1)],
            dst_ref=heap.at[layer, :, pl.ds(k, 1)],
            send_sem=bundle_send.at[k],
            recv_sem=bundle_recv.at[layer, k],
            device_id=in_group(k, 0),
            device_id_type=MESH,
        )

    def far_parcel(layer, place):
        return pltpu.make_async_remote_copy(
            src_ref=bundle_far,
            dst_ref=heap_far.at[layer, place],
            send_sem=far_send,
            recv_sem=far_recv.at[layer, place],
            device_id=(high * half + border, j, 0),
            device_id_type=MESH,
        )

    def post():
        for k in near_ring:
            relay(k).wait_recv()
        for t in range(2):
            got = mail[0, 8 * t : 8 * t + 8, :]
            turned = jnp.zeros((GROUP, along), jnp.float32)
            for d in range(GROUP):
                moved = got if d == 0 else pltpu.roll(pltpu.roll(got, d, 0), along - WORDS * d, 1)
                turned = jnp.where(((sub - lane // WORDS) & 7) == d, moved, turned)
            bundle[t] = turned
        far = jnp.sum(mail[1], axis=0, keepdims=True)
        bundle_far[...] = jnp.where(sub == low, far, 0.0)
        for k in range(1, half):
            parcel_of(k, g).start()

        @pl.when(jnp.logical_not(surface))
        def _():
            parcel_of(0, g).start()

        @pl.when(surface)
        def _():
            heap[0, :, 0:1] = bundle[:, 0:1]

        @pl.when(jnp.logical_not(surface & on_border))
        def _():
            far_parcel(g, low).start()

        @pl.when(surface & on_border)
        def _():
            heap_far[0, border] = bundle_far[...]

    pl.semaphore_wait(barrier, count)
    for k in range(-quarter, quarter):
        if k != 0:
            letter(k).start()

    @pl.when(near_side)
    def _():
        for part in range(2):
            to_half_way(part).start()

    begin(0)

    @pl.when(forwards)
    def _():
        pl.semaphore_signal(known, inc=1, device_id=on_ring(-quarter), device_id_type=MESH)
        for part in range(2):
            to_half_way(part).wait_recv()
        for number in crossing:

            @pl.when(to_far_side(OFFSETS[number])[0])
            def _(number=number):
                onward(number).start()

    own = pl.ds(2 * quarter, 2)
    transit[:, own] = letters[:, own]
    for k in range(-quarter, quarter):
        if k != 0:
            letter(k).wait_recv()
    for k in near_ring:
        relay(k).start()
    kept = pl.ds(*relay_rows(0))
    mail[:, kept] = transit[:, kept]

    def unpack(turn):
        def pair(kind):
            return jnp.where(lane % 8 < 4, packed[turn, kind, 0], packed[turn, kind, 1])

        plain = pair(0)
        deep = jnp.where((lane // 8) % 8 >= 4, pair(1), pair(2))
        wide = jnp.where(sub < 4, pair(4), pair(3))
        for f in range(2):
            for z in range(depth):
                turnback = (along - 4 - 8 * (f * depth + z)) % along
                edge_y[f, 4 + z] = pltpu.roll(plain, turnback, 1)
                edge_y[f, z - 4 if z >= 4 else 12 + z] = pltpu.roll(deep, turnback, 1)
                edge_xy[f, z] = pltpu.roll(wide, turnback, 1)

    def advance(turn, store):
        def layer(z, _):
            first, whole = [], []
            for f in range(2):
                center = body[turn, f, z + 4]
                beside = side[turn, f, z + 4]
                edge = edge_y[f, z + 4]
                above = [body[turn, f, z + 4 + k] for k in range(1, 5)]
                below = [body[turn, f, z + 4 - k] for k in range(1, 5)]
                u_zz = bend(center, above, below)
                grad_z = slope(above, below)
                grad_z_side = slope(
                    [side[turn, f, z + 4 + k] for k in range(1, 5)],
                    [side[turn, f, z + 4 - k] for k in range(1, 5)],
                )
                grad_z_edge = slope(
                    [edge_y[f, z + 4 + k] for k in range(1, 5)],
                    [edge_y[f, z + 4 - k] for k in range(1, 5)],
                )
                x_moves = shifted(center, beside, 0)
                u_xx = bend(center, *x_moves)
                grad_x = slope(*x_moves)
                grad_x_edge = slope(*shifted(edge, edge_xy[f, z], 0))
                u_yy = bend(center, *shifted(center, edge, 1))
                u_xy = slope(*shifted(grad_x, grad_x_edge, 1))
                u_xz = slope(*shifted(grad_z, grad_z_side, 0))
                u_yz = slope(*shifted(grad_z, grad_z_edge, 1))
                first.append(
                    coef[0, z] * u_xx
                    + coef[1, z] * u_yy
                    + coef[2, z] * u_zz
                    + coef[3, z] * u_xy
                    + coef[4, z] * u_xz
                    + coef[5, z] * u_yz
                )
                whole.append(u_xx + u_yy + u_zz)
            stay = coef[11, z]
            now_p, now_q = body[turn, 0, z + 4], body[turn, 1, z + 4]
            if turn == 0:
                was_p, was_q = old[0, z], old[1, z]
            else:
                was_p, was_q = body[0, 0, z + 4], body[0, 1, z + 4]
            mixed = coef[8, z] * first[1]
            new_p = (
                now_p
                + stay * (now_p - was_p)
                + (coef[6, z] * whole[0] + coef[7, z] * first[0] + mixed)
            )
            new_q = (
                now_q
                + stay * (now_q - was_q)
                + (coef[9, z] * (whole[0] - first[0]) + coef[10, z] * whole[1] + mixed)
            )
            store(z, new_p, new_q)
            return 0

        lax.fori_loop(0, depth, layer, 0, unroll=8)

    def keep(z, new_p, new_q):
        body[1, 0, z + 4] = new_p
        body[1, 1, z + 4] = new_q

    def finish(z, new_p, new_q):
        next_p[z] = new_p
        next_q[z] = new_q

    late = (high == 0) & on_border

    @pl.when(late)
    def _():
        post()

    arrive(0)
    unpack(0)
    advance(0, keep)
    pack(1)

    @pl.when(near_side)
    def _():
        pl.semaphore_wait(known, 1)

    begin(1)

    @pl.when(jnp.logical_not(late))
    def _():
        post()

    def add_up(label, values):
        label_x, label_y = label >> 7, label & 127
        pieces = []
        for rest in values:
            for _ in range(3):
                rounded = rest.astype(jnp.bfloat16).astype(jnp.float32)
                pieces.append(rounded)
                rest = rest - rounded
        total = jnp.zeros((len(pieces) * across, along), jnp.float32)
        for r in range(0, 2 * GROUP, 2):

            def flat(array):
                return jnp.concatenate([array[r : r + 1], array[r + 1 : r + 2]], axis=1)

            at_x = iota((across, 2 * along), 0) == flat(label_x)
            left = jnp.concatenate([jnp.where(at_x, flat(piece), 0.0) for piece in pieces], axis=0)
            right = jnp.where(iota((along, 2 * along), 0) == flat(label_y), 1.0, 0.0)
            total = total + lax.dot_general(
                left.astype(jnp.bfloat16),
                right.astype(jnp.bfloat16),
                (((1,), (1,)), ((), ())),
                preferred_element_type=jnp.float32,
            )
        return [
            total[24 * k : 24 * k + 8] + total[24 * k + 8 : 24 * k + 16] + total[24 * k + 16 : 24 * k + 24]
            for k in range(len(values))
        ]

    def plane_there(d, e):
        crosses = jnp.bool_(False)
        if d == 1:
            crosses = i == half - 1
        if d == -1:
            crosses = i == half
        return there((d, e, 0)) & jnp.logical_not(crosses)

    def plane_copy(number):
        d, e = BESIDE[number]
        if e == 0:
            rows = pl.ds(4 if d == 1 else 0, 4)
            source, target = plane.at[0, rows], plane_side.at[rows]
        else:
            source, target = plane_parcel, plane_packed.at[{0: 0, 1: 1, -1: 2}[d], 0 if e == 1 else 1]
        return pltpu.make_async_remote_copy(
            src_ref=source,
            dst_ref=target,
            send_sem=plane_send.at[number],
            recv_sem=plane_recv.at[number],
            device_id=device((d, e, 0)),
            device_id_type=MESH,
        )

    @pl.when(surface)
    def _():
        for layer in range(n_gz):
            for k in range(half):
                if layer > 0 or k > 0:
                    parcel_of(k, layer).wait_recv()
        place = iota((2 * GROUP, along), 1) % WORDS // SLOTS
        parts = [heap[layer].reshape(2 * GROUP, along) for layer in range(4)]

        def gather(kind):
            total = jnp.zeros((2 * GROUP, along), jnp.float32)
            for layer in range(4):
                shift = SLOTS * (layer - kind) % along
                moved = parts[layer] if shift == 0 else pltpu.roll(parts[layer], shift, 1)
                total = jnp.where(place == layer, moved, total)
            return total

        sums = add_up(gather(2).astype(jnp.int32) - 1, [gather(0), gather(1)])
        plane[0] = sums[0]
        plane[1] = sums[1]

    @pl.when(surface & on_border)
    def _():
        for layer in range(n_gz):
            for place in range(half):

                @pl.when((layer > 0) | (border != place))
                def _(layer=layer, place=place):
                    far_parcel(layer, place).wait_recv()

        parts = [jnp.sum(heap_far[layer], axis=0) for layer in range(4)]
        front = lane % 8 < 4
        values, labels = [], []
        for k in (0, 2):
            values.append(jnp.where(front, parts[k], pltpu.roll(parts[k + 1], SLOTS, 1)))
            labels.append(jnp.where(front, pltpu.roll(parts[k], along - SLOTS, 1), parts[k + 1]))
        label = jnp.concatenate(labels, axis=0).astype(jnp.int32) - 1
        [total] = add_up(label, [jnp.concatenate(values, axis=0)])
        plane_far[...] = total

        @pl.when(high == 0)
        def _():
            plane_side[0:4] = total[0:4]

        @pl.when(high != 0)
        def _():
            plane_side[4:8] = total[4:8]

    @pl.when(surface)
    def _():
        plane_parcel[...] = jnp.where(
            lane < 8, pltpu.roll(plane[0], 4, 1), pltpu.roll(plane_far[...], 12, 1)
        )
        for number, (d, e) in enumerate(BESIDE):

            @pl.when(plane_there(d, e))
            def _(number=number):
                plane_copy(number).start()

    depart(1)
    arrive(1)
    unpack(1)

    @pl.when(surface)
    def _():
        for number, (d, e) in enumerate(BESIDE):

            @pl.when(plane_there(-d, -e))
            def _(number=number):
                plane_copy(number).wait_recv()

        def pair(kind):
            return jnp.where(lane % 8 < 4, plane_packed[kind, 0], plane_packed[kind, 1])

        same = pair(0)
        edge = pltpu.roll(same, along - 4, 1)
        corner = pltpu.roll(jnp.where(sub < 4, pair(2), pair(1)), along - 4, 1) + pltpu.roll(
            same, along - 12, 1
        )
        for f in range(2):
            body[1, f, 4] = body[1, f, 4] + plane[0]
            side[1, f, 4] = side[1, f, 4] + plane_side[...]
            edge_y[f, 4] = edge_y[f, 4] + edge
            edge_xy[f, 0] = edge_xy[f, 0] + corner

    for f, prior in enumerate((prior_p, prior_q)):
        prior[...] = body[1, f, 4:12]
    advance(1, finish)

    @pl.when(surface)
    def _():
        for result in (next_p, next_q):
            result[0] = result[0] + plane[1]

    depart(0)

    @pl.when(near_side)
    def _():
        for part in range(2):
            to_half_way(part).wait_send()

    @pl.when(forwards)
    def _():
        for number in crossing:

            @pl.when(to_far_side(OFFSETS[number])[0])
            def _(number=number):
                onward(number).wait_send()

    for k in range(-quarter, quarter):
        if k != 0:
            letter(k).wait_send()
    for k in near_ring:
        relay(k).wait_send()
    for k in range(1, half):
        parcel_of(k, g).wait_send()

    @pl.when(jnp.logical_not(surface))
    def _():
        parcel_of(0, g).wait_send()

    @pl.when(jnp.logical_not(surface & on_border))
    def _():
        far_parcel(g, low).wait_send()

    @pl.when(surface)
    def _():
        for number, (d, e) in enumerate(BESIDE):

            @pl.when(plane_there(d, e))
            def _(number=number):
                plane_copy(number).wait_send()


def hand_over(*refs):
    sources, targets, sem = refs[:4], refs[4:8], refs[8]
    copies = [pltpu.make_async_copy(a, b, sem.at[k]) for k, (a, b) in enumerate(zip(sources, targets))]
    for copy in copies:
        copy.start()
    for copy in copies:
        copy.wait()


def local(sizes, *args):
    fields = args[:11]
    samples, weights, gain, row, column, line = args[11:]
    block = fields[0].shape
    n_traces = samples.shape[0]
    receivers = [ids.reshape(1, -1) for ids in (row, column, line)]
    f32 = jnp.float32
    outs = pl.pallas_call(
        functools.partial(kernel, sizes),
        out_shape=[pltpu.VMEM(block, f32)] * 4,
        in_specs=[pl.BlockSpec(memory_space=pltpu.HBM)] * 17,
        out_specs=[pl.BlockSpec(memory_space=pltpu.VMEM)] * 4,
        scratch_shapes=[
            pltpu.VMEM((2, 2, 16, 8, 128), f32),
            pltpu.VMEM((2, 2, 16, 8, 128), f32),
            pltpu.VMEM((2, 5, 2, 8, 128), f32),
            pltpu.VMEM((2, 8, 128), f32),
            pltpu.VMEM((2, 16, 8, 128), f32),
            pltpu.VMEM((2, 8, 8, 128), f32),
            pltpu.VMEM((2, 8, 8, 128), f32),
            pltpu.VMEM((7, 8, 8, 128), f32),
            pltpu.VMEM((12, 8, 8, 128), f32),
            pltpu.VMEM(samples.shape, f32),
            pltpu.VMEM(weights.shape, f32),
            pltpu.VMEM((1, gain.shape[0]), f32),
            pltpu.VMEM((3, 1, n_traces), jnp.int32),
            pltpu.VMEM((2, RING, 128), f32),
            pltpu.VMEM((2, RING, 128), f32),
            pltpu.VMEM((2, RING, 128), f32),
            pltpu.VMEM((2, 8, 4, 128), f32),
            pltpu.VMEM((8, 128), f32),
            pltpu.VMEM((2, GROUP, 128), f32),
            pltpu.VMEM((8, 128), f32),
            pltpu.VMEM((4, 2, GROUP, 128), f32),
            pltpu.VMEM((4, GROUP, 8, 128), f32),
            pltpu.VMEM((2, 8, 128), f32),
            pltpu.VMEM((8, 128), f32),
            pltpu.VMEM((8, 128), f32),
            pltpu.VMEM((8, 128), f32),
            pltpu.VMEM((3, 2, 8, 128), f32),
            pltpu.SemaphoreType.DMA((17,)),
            pltpu.SemaphoreType.DMA((2, len(OFFSETS))),
            pltpu.SemaphoreType.DMA((2, len(OFFSETS))),
            pltpu.SemaphoreType.DMA((9,)),
            pltpu.SemaphoreType.DMA((9,)),
            pltpu.SemaphoreType.DMA((9,)),
            pltpu.SemaphoreType.DMA((9,)),
            pltpu.SemaphoreType.DMA((GROUP,)),
            pltpu.SemaphoreType.DMA((4, GROUP)),
            pltpu.SemaphoreType.DMA,
            pltpu.SemaphoreType.DMA((4, GROUP)),
            pltpu.SemaphoreType.DMA((8,)),
            pltpu.SemaphoreType.DMA((8,)),
            pltpu.SemaphoreType.DMA((2,)),
            pltpu.SemaphoreType.DMA((2,)),
            pltpu.SemaphoreType.DMA((len(OFFSETS),)),
            pltpu.SemaphoreType.REGULAR,
        ],
        compiler_params=pltpu.CompilerParams(
            collective_id=0, has_side_effects=True, vmem_limit_bytes=60 * 2**20
        ),
        name="wave_steps",
    )(*fields, samples, weights, gain.reshape(1, -1), *receivers)
    return pl.pallas_call(
        hand_over,
        out_shape=[jax.ShapeDtypeStruct(block, f32)] * 4,
        in_specs=[pl.BlockSpec(memory_space=pl.ANY)] * 4,
        out_specs=[pl.BlockSpec(memory_space=pltpu.HBM)] * 4,
        scratch_shapes=[pltpu.SemaphoreType.DMA((4,))],
        compiler_params=pltpu.CompilerParams(vmem_limit_bytes=2**20),
        name="hand_over",
    )(*outs)


def solution(mesh):
    sizes = tuple(mesh.shape[axis] for axis in ("inl", "xl", "gz"))
    cells = P("gz", "inl", "xl")
    traces = P(("inl", "xl", "gz"))
    return jax.shard_map(
        functools.partial(local, sizes),
        mesh=mesh,
        in_specs=(cells,) * 11 + (P(("inl", "xl", "gz"), None), P(), P(), traces, traces, traces),
        out_specs=(cells,) * 4,
        check_vma=False,
    )
```

```python
import functools

import jax
import jax.numpy as jnp
from jax import lax
from jax.experimental import pallas as pl
from jax.experimental.pallas import tpu as pltpu
from jax.sharding import PartitionSpec as P

MESH = pl.DeviceIdType.MESH
second_coef = (-205.0 / 72.0, 8.0 / 5.0, -1.0 / 5.0, 8.0 / 315.0, -1.0 / 560.0)
first_coef = (0.0, 4.0 / 5.0, -1.0 / 5.0, 4.0 / 105.0, -1.0 / 280.0)

OFFSETS = (
    [(d, 0, 0) for d in (1, -1)]
    + [(d, 0, e) for d in (1, -1) for e in (1, -1)]
    + [(d, e, 0) for d in (1, -1) for e in (1, -1)]
    + [(0, d, e) for d in (1, -1) for e in (1, -1)]
    + [(0, d, 0) for d in (1, -1)]
    + [(0, 0, d) for d in (1, -1)]
)
RING = 16
GROUP = 8
SLOTS = 4
WORDS = 16
BESIDE = [(d, e) for d in (1, -1, 0) for e in (1, -1, 0) if d != 0 or e != 0]


def iota(shape, axis):
    return lax.broadcasted_iota(jnp.int32, shape, axis)


def shifted(body, halo, axis):
    size = body.shape[axis]
    place = iota(body.shape, axis)
    above = [pltpu.roll(jnp.where(place < k, halo, body), size - k, axis) for k in range(1, 5)]
    below = [pltpu.roll(jnp.where(place >= size - k, halo, body), k, axis) for k in range(1, 5)]
    return above, below


def slope(above, below):
    total = first_coef[1] * (above[0] - below[0])
    for k in range(2, 5):
        total = total + first_coef[k] * (above[k - 1] - below[k - 1])
    return total


def bend(center, above, below):
    total = second_coef[0] * center
    for k in range(1, 5):
        total = total + second_coef[k] * (above[k - 1] + below[k - 1])
    return total


def kernel(sizes, *refs):
    n_inl, n_xl, n_gz = sizes
    (
        wave_p,
        wave_p_old,
        wave_q,
        wave_q_old,
        courant,
        epsilon,
        delta,
        tilt,
        azimuth,
        shear,
        damping,
        samples,
        weights,
        gain,
        inline,
        crossline,
        shot,
        next_p,
        next_q,
        prior_p,
        prior_q,
        body,
        side,
        packed,
        parcel,
        edge_y,
        edge_xy,
        old,
        field,
        coef,
        trace,
        small_w,
        small_g,
        small_r,
        letters,
        transit,
        mail,
        passing,
        passing_parcel,
        bundle,
        bundle_far,
        heap,
        heap_far,
        plane,
        plane_far,
        plane_side,
        plane_parcel,
        plane_packed,
        load_sem,
        send_sem,
        recv_sem,
        letter_send,
        letter_recv,
        relay_send,
        relay_recv,
        bundle_send,
        bundle_recv,
        far_send,
        far_recv,
        plane_send,
        plane_recv,
        pass_send,
        pass_recv,
        onward_send,
        known,
        direct_send,
        direct_recv,
    ) = refs
    i = lax.axis_index("inl")
    j = lax.axis_index("xl")
    g = lax.axis_index("gz")
    depth, across, along = 8, 8, 128
    half = n_inl // 2
    ring = 2 * n_xl
    high, low = i // half, i % half
    level = high * n_xl + j
    quarter = ring // 4
    border = jnp.where(high == 0, half - 1, 0)
    on_border = low == border
    surface = g == 0
    even, odd = low % 2 == 0, low % 2 == 1
    near_side, far_side = i == half - 1, i == half
    forwards = (low == half - 1) & (level >= quarter) & (level < quarter + n_xl)

    loads = [
        (wave_p, body.at[0, 0, pl.ds(4, depth)]),
        (wave_q, body.at[0, 1, pl.ds(4, depth)]),
        (wave_p_old, old.at[0]),
        (wave_q_old, old.at[1]),
        (courant, field.at[0]),
        (epsilon, field.at[1]),
        (delta, field.at[2]),
        (tilt, field.at[3]),
        (azimuth, field.at[4]),
        (shear, field.at[5]),
        (damping, field.at[6]),
        (samples, trace),
        (weights, small_w),
        (gain, small_g),
        (inline, small_r.at[0]),
        (crossline, small_r.at[1]),
        (shot, small_r.at[2]),
    ]
    loads = [pltpu.make_async_copy(a, b, load_sem.at[k]) for k, (a, b) in enumerate(loads)]
    nothing = jnp.zeros((2, 4, across, along), jnp.float32)
    for turn in range(2):
        body[turn, :, 0:4] = nothing
        body[turn, :, 12:16] = nothing
        for k in range(4):
            side[turn, :, 4 * k : 4 * k + 4] = nothing
        packed[turn] = jnp.zeros((5, 2, across, along), jnp.float32)
    mail[...] = jnp.zeros((2, RING, along), jnp.float32)
    heap[...] = jnp.zeros((4, 2, GROUP, along), jnp.float32)
    for layer in range(4):
        heap_far[layer] = jnp.zeros((GROUP, across, along), jnp.float32)
    plane_far[...] = jnp.zeros((across, along), jnp.float32)
    plane_side[...] = jnp.zeros((across, along), jnp.float32)
    plane_packed[...] = jnp.zeros((3, 2, across, along), jnp.float32)

    def there(offset):
        d, e, f = offset
        ok = []
        for step, place, count in ((d, i, n_inl), (e, j, n_xl), (f, g, n_gz)):
            if step == 1:
                ok.append(place < count - 1)
            if step == -1:
                ok.append(place > 0)
        return functools.reduce(jnp.logical_and, ok)

    def device(offset):
        d, e, f = offset
        return (
            jnp.clip(i + d, 0, n_inl - 1),
            jnp.clip(j + e, 0, n_xl - 1),
            jnp.clip(g + f, 0, n_gz - 1),
        )

    def on_ring(k):
        place = lax.rem(level + k + ring, ring)
        return (place // n_xl * half + low, lax.rem(place, n_xl), g)

    def in_group(k, layer):
        return (high * half + lax.rem(low + k, half), j, layer)

    barrier = pltpu.get_barrier_semaphore()
    count = jnp.where(even, ring - 1, 2 * quarter) + jnp.where(surface, half - 1, half)
    near_ring = [k for k in range(-quarter, quarter + 1) if k != 0]
    far_ring = [k for k in range(-ring // 2, ring // 2) if k != 0]

    @pl.when(even)
    def _():
        for k in far_ring:
            pl.semaphore_signal(barrier, inc=1, device_id=on_ring(k), device_id_type=MESH)

    @pl.when(odd)
    def _():
        for k in near_ring:
            pl.semaphore_signal(barrier, inc=1, device_id=on_ring(k), device_id_type=MESH)

    def inside(place, count):
        return (place >= 0) & (place < count)

    def from_half_way(offset):
        _, e, f = offset
        ok = far_side & inside(j - e, n_xl) & inside(g - f, n_gz)
        place = jnp.clip(j - e, 0, n_xl - 1) + quarter
        return ok, (place // n_xl * half + half - 1, lax.rem(place, n_xl), jnp.clip(g - f, 0, n_gz - 1))

    def to_far_side(offset):
        _, e, f = offset
        place = level - quarter + e
        ok = forwards & inside(place, n_xl) & inside(g + f, n_gz)
        return ok, (half, jnp.clip(place, 0, n_xl - 1), jnp.clip(g + f, 0, n_gz - 1))

    for offset in OFFSETS:
        d = offset[0]
        hears = there(offset)
        if d == -1:
            hears = hears & jnp.logical_not(far_side)
        if d == 1:
            ok, whom = from_half_way(offset)

            @pl.when(ok)
            def _(whom=whom):
                pl.semaphore_signal(barrier, inc=1, device_id=whom, device_id_type=MESH)

            count = count + to_far_side(offset)[0].astype(jnp.int32)

        @pl.when(hears)
        def _(offset=offset):
            pl.semaphore_signal(barrier, inc=1, device_id=device(offset), device_id_type=MESH)

        direct = there(offset)
        if d == 1:
            direct = direct & jnp.logical_not(near_side)
        count = count + direct.astype(jnp.int32)

    @pl.when(surface)
    def _():
        for layer in range(n_gz):
            for k in range(half):
                if layer > 0 or k > 0:
                    pl.semaphore_signal(
                        barrier, inc=1, device_id=in_group(k, layer), device_id_type=MESH
                    )

    for copy in loads:
        copy.start()
    for copy in loads:
        copy.wait()

    def prepare(z, _):
        sin_t, cos_t = jnp.sin(field[3, z]), jnp.cos(field[3, z])
        sin_f, cos_f = jnp.sin(field[4, z]), jnp.cos(field[4, z])
        coef[0, z] = sin_t * sin_t * cos_f * cos_f
        coef[1, z] = sin_t * sin_t * sin_f * sin_f
        coef[2, z] = cos_t * cos_t
        coef[3, z] = 2.0 * sin_t * sin_t * sin_f * cos_f
        coef[4, z] = 2.0 * sin_t * cos_t * cos_f
        coef[5, z] = 2.0 * sin_t * cos_t * sin_f
        c, s = field[0, z], field[5, z]
        grow, lean = 1.0 + 2.0 * field[1, z], 1.0 + 2.0 * field[2, z]
        coef[6, z] = c * grow
        coef[7, z] = c * (s - grow)
        coef[8, z] = c * (1.0 - s)
        coef[9, z] = c * (lean - s)
        coef[10, z] = c * s
        coef[11, z] = 1.0 - field[6, z]
        return 0

    lax.fori_loop(0, depth, prepare, 0)

    n_traces = trace.shape[0]
    row, column, line = small_r[0], small_r[1], small_r[2]
    lines = small_g.shape[1]
    picked = jnp.where(iota((lines, n_traces), 0) == line, 1.0, 0.0).astype(jnp.float32)
    gains = jnp.dot(
        small_g[...],
        picked,
        precision=lax.Precision.HIGHEST,
        preferred_element_type=jnp.float32,
    )
    amplitude = (
        lax.dot_general(
            small_w[...],
            trace[...],
            (((1,), (1,)), ((), ())),
            precision=lax.Precision.HIGHEST,
            preferred_element_type=jnp.float32,
        )
        * gains
    )
    to_inl, to_xl = row >> 3, column >> 7
    cell = ((row & 7) << 7) + (column & 127) + 1
    to_high = jnp.where(to_inl >= half, 1, 0)
    to_low = to_inl - to_high * half
    owner = to_inl * n_xl + to_xl
    columns = n_inl * n_xl
    member = jnp.where(iota((columns, n_traces), 0) == owner, 1.0, 0.0).astype(jnp.float32)
    earlier = jnp.where(
        iota((n_traces, n_traces), 0) < iota((n_traces, n_traces), 1), 1.0, 0.0
    ).astype(jnp.float32)
    before = jnp.dot(
        member.astype(jnp.bfloat16),
        earlier.astype(jnp.bfloat16),
        preferred_element_type=jnp.float32,
    )
    rank = jnp.sum(member * before, axis=0, keepdims=True).astype(jnp.int32)
    to_level = to_high * n_xl + to_xl
    block = to_low - low
    block = jnp.where(block < 0, block + half, block)
    word = block * WORDS + rank
    spot = iota((along, n_traces), 0)
    content = (
        jnp.where(spot == word, amplitude[0:1, :], 0.0)
        + jnp.where(spot == word + SLOTS, amplitude[1:2, :], 0.0)
        + jnp.where(spot == word + 2 * SLOTS, cell.astype(jnp.float32), 0.0)
    )
    leaves = (to_inl == half - 1) & ((row & 7) >= 4)
    enters = (to_inl == half) & ((row & 7) < 4)
    far_level = jnp.where(leaves, n_xl + to_xl, to_xl)
    far_word = 2 * SLOTS * level + rank
    far_content = jnp.where(spot == far_word, amplitude[0:1, :], 0.0) + jnp.where(
        spot == far_word + SLOTS, cell.astype(jnp.float32), 0.0
    )

    def write(target, wanted, words):
        hop = target - level + ring // 2
        hop = jnp.where(hop < 0, hop + ring, jnp.where(hop >= ring, hop - ring, hop))
        address = (iota((RING, n_traces), 0) == hop) & wanted
        return lax.dot_general(
            jnp.where(address, 1.0, 0.0).astype(jnp.float32),
            words,
            (((1,), (1,)), ((), ())),
            precision=lax.Precision.HIGHEST,
            preferred_element_type=jnp.float32,
        )

    letters[0] = write(to_level, to_level >= 0, content)
    letters[1] = write(far_level, leaves | enters, far_content)

    lane = iota((across, along), 1)
    sub = iota((across, along), 0)

    def pack(turn):
        total = jnp.zeros((across, along), jnp.float32)
        for f in range(2):
            for z in range(depth):
                tile = f * depth + z
                moved = pltpu.roll(body[turn, f, 4 + z], (8 * tile + 4) % along, 1)
                total = jnp.where(lane // 8 == tile, moved, total)
        parcel[turn] = total

    pack(0)

    def copies(turn):
        out = []
        mine = body.at[turn]
        beside = side.at[turn]
        for number, offset in enumerate(OFFSETS):
            d, e, f = offset
            if e != 0:
                kind = 0
                if f != 0:
                    kind = 1 if f == 1 else 2
                if d != 0:
                    kind = 3 if d == 1 else 4
                source = parcel.at[turn]
                target = packed.at[turn, kind, 0 if e == 1 else 1]
            else:
                deep = {0: (4, 8, 4), 1: (8, 4, 0), -1: (4, 4, 12)}[f]
                if d == 0:
                    source = mine.at[:, pl.ds(deep[0], deep[1])]
                    target = mine.at[:, pl.ds(deep[2], deep[1])]
                else:
                    wide = pl.ds(4 if d == 1 else 0, 4)
                    source = mine.at[:, pl.ds(deep[0], deep[1]), wide]
                    target = beside.at[:, pl.ds(deep[2], deep[1]), wide]
            out.append(
                pltpu.make_async_remote_copy(
                    src_ref=source,
                    dst_ref=target,
                    send_sem=send_sem.at[turn, number],
                    recv_sem=recv_sem.at[turn, number],
                    device_id=device(offset),
                    device_id_type=MESH,
                )
            )
        return out

    def sends(turn, offset):
        if turn == 0 and offset[0] == 1:
            return there(offset) & jnp.logical_not(near_side)
        return there(offset)

    def begin(turn):
        for offset, copy in zip(OFFSETS, copies(turn)):

            @pl.when(sends(turn, offset))
            def _(copy=copy):
                copy.start()

    def arrive(turn):
        for offset, copy in zip(OFFSETS, copies(turn)):

            @pl.when(there(tuple(-d for d in offset)))
            def _(copy=copy):
                copy.wait_recv()

    def depart(turn):
        for offset, copy in zip(OFFSETS, copies(turn)):

            @pl.when(sends(turn, offset))
            def _(copy=copy):
                copy.wait_send()

    def to_half_way(part):
        source = body.at[0, :, pl.ds(4, depth), pl.ds(4, 4)] if part == 0 else parcel.at[0]
        return pltpu.make_async_remote_copy(
            src_ref=source,
            dst_ref=passing if part == 0 else passing_parcel,
            send_sem=pass_send.at[part],
            recv_sem=pass_recv.at[part],
            device_id=on_ring(quarter),
            device_id_type=MESH,
        )

    def onward(number):
        _, e, f = OFFSETS[number]
        if e != 0:
            source = passing_parcel
            target = packed.at[0, 3, 0 if e == 1 else 1]
        else:
            first, deep, goal = {0: (0, 8, 4), 1: (4, 4, 0), -1: (0, 4, 12)}[f]
            source = passing.at[:, pl.ds(first, deep)]
            target = side.at[0, :, pl.ds(goal, deep), pl.ds(4, 4)]
        return pltpu.make_async_remote_copy(
            src_ref=source,
            dst_ref=target,
            send_sem=onward_send.at[number],
            recv_sem=recv_sem.at[0, number],
            device_id=to_far_side(OFFSETS[number])[1],
            device_id_type=MESH,
        )

    crossing = [number for number, offset in enumerate(OFFSETS) if offset[0] == 1]

    def letter(k):
        rows = pl.ds(2 * (k + quarter), 2)
        return pltpu.make_async_remote_copy(
            src_ref=letters.at[:, rows],
            dst_ref=transit.at[:, rows],
            send_sem=letter_send.at[k + quarter],
            recv_sem=letter_recv.at[k + quarter],
            device_id=on_ring(k),
            device_id_type=MESH,
        )

    def direct_letter(k):
        row = pl.ds(k + ring // 2, 1)
        return pltpu.make_async_remote_copy(
            src_ref=letters.at[:, row],
            dst_ref=mail.at[:, row],
            send_sem=direct_send.at[k + ring // 2],
            recv_sem=direct_recv.at[k + ring // 2],
            device_id=on_ring(k),
            device_id_type=MESH,
        )

    def relay_rows(k):
        first = max(2 * (k + quarter) - 1, 0)
        return first, min(2 * (k + quarter) + 1, ring) - first

    def relay(k):
        rows = pl.ds(*relay_rows(k))
        return pltpu.make_async_remote_copy(
            src_ref=transit.at[:, rows],
            dst_ref=mail.at[:, rows],
            send_sem=relay_send.at[k + quarter],
            recv_sem=relay_recv.at[k + quarter],
            device_id=on_ring(k),
            device_id_type=MESH,
        )

    def parcel_of(k, layer):
        return pltpu.make_async_remote_copy(
            src_ref=bundle.at[:, pl.ds(k, 1)],
            dst_ref=heap.at[layer, :, pl.ds(k, 1)],
            send_sem=bundle_send.at[k],
            recv_sem=bundle_recv.at[layer, k],
            device_id=in_group(k, 0),
            device_id_type=MESH,
        )

    def far_parcel(layer, place):
        return pltpu.make_async_remote_copy(
            src_ref=bundle_far,
            dst_ref=heap_far.at[layer, place],
            send_sem=far_send,
            recv_sem=far_recv.at[layer, place],
            device_id=(high * half + border, j, 0),
            device_id_type=MESH,
        )

    def post():
        @pl.when(even)
        def _():
            for k in far_ring:
                direct_letter(k).wait_recv()

        @pl.when(odd)
        def _():
            for k in near_ring:
                relay(k).wait_recv()

        for t in range(2):
            got = mail[0, 8 * t : 8 * t + 8, :]
            turned = jnp.zeros((GROUP, along), jnp.float32)
            for d in range(GROUP):
                moved = got if d == 0 else pltpu.roll(pltpu.roll(got, d, 0), along - WORDS * d, 1)
                turned = jnp.where(((sub - lane // WORDS) & 7) == d, moved, turned)
            bundle[t] = turned
        far = jnp.sum(mail[1], axis=0, keepdims=True)
        bundle_far[...] = jnp.where(sub == low, far, 0.0)
        for k in range(1, half):
            parcel_of(k, g).start()

        @pl.when(jnp.logical_not(surface))
        def _():
            parcel_of(0, g).start()

        @pl.when(surface)
        def _():
            heap[0, :, 0:1] = bundle[:, 0:1]

        @pl.when(jnp.logical_not(surface & on_border))
        def _():
            far_parcel(g, low).start()

        @pl.when(surface & on_border)
        def _():
            heap_far[0, border] = bundle_far[...]

    pl.semaphore_wait(barrier, count)

    @pl.when(even)
    def _():
        for k in far_ring:
            direct_letter(k).start()

    @pl.when(odd)
    def _():
        for k in range(-quarter, quarter):
            if k != 0:
                letter(k).start()

    @pl.when(near_side)
    def _():
        for part in range(2):
            to_half_way(part).start()

    begin(0)

    @pl.when(forwards)
    def _():
        pl.semaphore_signal(known, inc=1, device_id=on_ring(-quarter), device_id_type=MESH)
        for part in range(2):
            to_half_way(part).wait_recv()
        for number in crossing:

            @pl.when(to_far_side(OFFSETS[number])[0])
            def _(number=number):
                onward(number).start()

    @pl.when(even)
    def _():
        own = pl.ds(ring // 2, 1)
        mail[:, own] = letters[:, own]

    @pl.when(odd)
    def _():
        own = pl.ds(2 * quarter, 2)
        transit[:, own] = letters[:, own]
        for k in range(-quarter, quarter):
            if k != 0:
                letter(k).wait_recv()
        for k in near_ring:
            relay(k).start()
        kept = pl.ds(*relay_rows(0))
        mail[:, kept] = transit[:, kept]

    def unpack(turn):
        def pair(kind):
            return jnp.where(lane % 8 < 4, packed[turn, kind, 0], packed[turn, kind, 1])

        plain = pair(0)
        deep = jnp.where((lane // 8) % 8 >= 4, pair(1), pair(2))
        wide = jnp.where(sub < 4, pair(4), pair(3))
        for f in range(2):
            for z in range(depth):
                turnback = (along - 4 - 8 * (f * depth + z)) % along
                edge_y[f, 4 + z] = pltpu.roll(plain, turnback, 1)
                edge_y[f, z - 4 if z >= 4 else 12 + z] = pltpu.roll(deep, turnback, 1)
                edge_xy[f, z] = pltpu.roll(wide, turnback, 1)

    def advance(turn, store):
        def layer(z, _):
            first, whole = [], []
            for f in range(2):
                center = body[turn, f, z + 4]
                beside = side[turn, f, z + 4]
                edge = edge_y[f, z + 4]
                above = [body[turn, f, z + 4 + k] for k in range(1, 5)]
                below = [body[turn, f, z + 4 - k] for k in range(1, 5)]
                u_zz = bend(center, above, below)
                grad_z = slope(above, below)
                grad_z_side = slope(
                    [side[turn, f, z + 4 + k] for k in range(1, 5)],
                    [side[turn, f, z + 4 - k] for k in range(1, 5)],
                )
                grad_z_edge = slope(
                    [edge_y[f, z + 4 + k] for k in range(1, 5)],
                    [edge_y[f, z + 4 - k] for k in range(1, 5)],
                )
                x_moves = shifted(center, beside, 0)
                u_xx = bend(center, *x_moves)
                grad_x = slope(*x_moves)
                grad_x_edge = slope(*shifted(edge, edge_xy[f, z], 0))
                u_yy = bend(center, *shifted(center, edge, 1))
                u_xy = slope(*shifted(grad_x, grad_x_edge, 1))
                u_xz = slope(*shifted(grad_z, grad_z_side, 0))
                u_yz = slope(*shifted(grad_z, grad_z_edge, 1))
                first.append(
                    coef[0, z] * u_xx
                    + coef[1, z] * u_yy
                    + coef[2, z] * u_zz
                    + coef[3, z] * u_xy
                    + coef[4, z] * u_xz
                    + coef[5, z] * u_yz
                )
                whole.append(u_xx + u_yy + u_zz)
            stay = coef[11, z]
            now_p, now_q = body[turn, 0, z + 4], body[turn, 1, z + 4]
            if turn == 0:
                was_p, was_q = old[0, z], old[1, z]
            else:
                was_p, was_q = body[0, 0, z + 4], body[0, 1, z + 4]
            mixed = coef[8, z] * first[1]
            new_p = (
                now_p
                + stay * (now_p - was_p)
                + (coef[6, z] * whole[0] + coef[7, z] * first[0] + mixed)
            )
            new_q = (
                now_q
                + stay * (now_q - was_q)
                + (coef[9, z] * (whole[0] - first[0]) + coef[10, z] * whole[1] + mixed)
            )
            store(z, new_p, new_q)
            return 0

        lax.fori_loop(0, depth, layer, 0, unroll=8)

    def keep(z, new_p, new_q):
        body[1, 0, z + 4] = new_p
        body[1, 1, z + 4] = new_q

    def finish(z, new_p, new_q):
        next_p[z] = new_p
        next_q[z] = new_q

    late = (high == 0) & on_border

    @pl.when(late)
    def _():
        post()

    arrive(0)
    unpack(0)
    advance(0, keep)
    pack(1)

    @pl.when(near_side)
    def _():
        pl.semaphore_wait(known, 1)

    begin(1)

    @pl.when(jnp.logical_not(late))
    def _():
        post()

    def add_up(label, values):
        label_x, label_y = label >> 7, label & 127
        pieces = []
        for rest in values:
            for _ in range(3):
                rounded = rest.astype(jnp.bfloat16).astype(jnp.float32)
                pieces.append(rounded)
                rest = rest - rounded
        total = jnp.zeros((len(pieces) * across, along), jnp.float32)
        for r in range(0, 2 * GROUP, 2):

            def flat(array):
                return jnp.concatenate([array[r : r + 1], array[r + 1 : r + 2]], axis=1)

            at_x = iota((across, 2 * along), 0) == flat(label_x)
            left = jnp.concatenate([jnp.where(at_x, flat(piece), 0.0) for piece in pieces], axis=0)
            right = jnp.where(iota((along, 2 * along), 0) == flat(label_y), 1.0, 0.0)
            total = total + lax.dot_general(
                left.astype(jnp.bfloat16),
                right.astype(jnp.bfloat16),
                (((1,), (1,)), ((), ())),
                preferred_element_type=jnp.float32,
            )
        return [
            total[24 * k : 24 * k + 8] + total[24 * k + 8 : 24 * k + 16] + total[24 * k + 16 : 24 * k + 24]
            for k in range(len(values))
        ]

    def plane_there(d, e):
        crosses = jnp.bool_(False)
        if d == 1:
            crosses = i == half - 1
        if d == -1:
            crosses = i == half
        return there((d, e, 0)) & jnp.logical_not(crosses)

    def plane_copy(number):
        d, e = BESIDE[number]
        if e == 0:
            rows = pl.ds(4 if d == 1 else 0, 4)
            source, target = plane.at[0, rows], plane_side.at[rows]
        else:
            source, target = plane_parcel, plane_packed.at[{0: 0, 1: 1, -1: 2}[d], 0 if e == 1 else 1]
        return pltpu.make_async_remote_copy(
            src_ref=source,
            dst_ref=target,
            send_sem=plane_send.at[number],
            recv_sem=plane_recv.at[number],
            device_id=device((d, e, 0)),
            device_id_type=MESH,
        )

    def plane_start(parcels):
        for number, (d, e) in enumerate(BESIDE):
            if (e != 0) == parcels:

                @pl.when(plane_there(d, e))
                def _(number=number):
                    plane_copy(number).start()

    @pl.when(surface)
    def _():
        for layer in range(n_gz):
            for k in range(half):
                if layer > 0 or k > 0:
                    parcel_of(k, layer).wait_recv()
        place = iota((2 * GROUP, along), 1) % WORDS // SLOTS
        parts = [heap[layer].reshape(2 * GROUP, along) for layer in range(4)]

        def gather(kind):
            total = jnp.zeros((2 * GROUP, along), jnp.float32)
            for layer in range(4):
                shift = SLOTS * (layer - kind) % along
                moved = parts[layer] if shift == 0 else pltpu.roll(parts[layer], shift, 1)
                total = jnp.where(place == layer, moved, total)
            return total

        sums = add_up(gather(2).astype(jnp.int32) - 1, [gather(0), gather(1)])
        plane[0] = sums[0]
        plane[1] = sums[1]
        plane_start(False)

    @pl.when(surface & on_border)
    def _():
        for layer in range(n_gz):
            for place in range(half):

                @pl.when((layer > 0) | (border != place))
                def _(layer=layer, place=place):
                    far_parcel(layer, place).wait_recv()

        parts = [jnp.sum(heap_far[layer], axis=0) for layer in range(4)]
        front = lane % 8 < 4
        values, labels = [], []
        for k in (0, 2):
            values.append(jnp.where(front, parts[k], pltpu.roll(parts[k + 1], SLOTS, 1)))
            labels.append(jnp.where(front, pltpu.roll(parts[k], along - SLOTS, 1), parts[k + 1]))
        label = jnp.concatenate(labels, axis=0).astype(jnp.int32) - 1
        [total] = add_up(label, [jnp.concatenate(values, axis=0)])
        plane_far[...] = total

        @pl.when(high == 0)
        def _():
            plane_side[0:4] = total[0:4]

        @pl.when(high != 0)
        def _():
            plane_side[4:8] = total[4:8]

    @pl.when(surface)
    def _():
        plane_parcel[...] = jnp.where(
            lane < 8, pltpu.roll(plane[0], 4, 1), pltpu.roll(plane_far[...], 12, 1)
        )
        plane_start(True)

    depart(1)
    arrive(1)
    unpack(1)

    @pl.when(surface)
    def _():
        for number, (d, e) in enumerate(BESIDE):

            @pl.when(plane_there(-d, -e))
            def _(number=number):
                plane_copy(number).wait_recv()

        def pair(kind):
            return jnp.where(lane % 8 < 4, plane_packed[kind, 0], plane_packed[kind, 1])

        same = pair(0)
        edge = pltpu.roll(same, along - 4, 1)
        corner = pltpu.roll(jnp.where(sub < 4, pair(2), pair(1)), along - 4, 1) + pltpu.roll(
            same, along - 12, 1
        )
        for f in range(2):
            body[1, f, 4] = body[1, f, 4] + plane[0]
            side[1, f, 4] = side[1, f, 4] + plane_side[...]
            edge_y[f, 4] = edge_y[f, 4] + edge
            edge_xy[f, 0] = edge_xy[f, 0] + corner

    for f, prior in enumerate((prior_p, prior_q)):
        prior[...] = body[1, f, 4:12]
    advance(1, finish)

    @pl.when(surface)
    def _():
        for result in (next_p, next_q):
            result[0] = result[0] + plane[1]

    depart(0)

    @pl.when(near_side)
    def _():
        for part in range(2):
            to_half_way(part).wait_send()

    @pl.when(forwards)
    def _():
        for number in crossing:

            @pl.when(to_far_side(OFFSETS[number])[0])
            def _(number=number):
                onward(number).wait_send()

    @pl.when(even)
    def _():
        for k in far_ring:
            direct_letter(k).wait_send()

    @pl.when(odd)
    def _():
        for k in range(-quarter, quarter):
            if k != 0:
                letter(k).wait_send()
        for k in near_ring:
            relay(k).wait_send()

    for k in range(1, half):
        parcel_of(k, g).wait_send()

    @pl.when(jnp.logical_not(surface))
    def _():
        parcel_of(0, g).wait_send()

    @pl.when(jnp.logical_not(surface & on_border))
    def _():
        far_parcel(g, low).wait_send()

    @pl.when(surface)
    def _():
        for number, (d, e) in enumerate(BESIDE):

            @pl.when(plane_there(d, e))
            def _(number=number):
                plane_copy(number).wait_send()


def hand_over(*refs):
    sources, targets, sem = refs[:4], refs[4:8], refs[8]
    copies = [pltpu.make_async_copy(a, b, sem.at[k]) for k, (a, b) in enumerate(zip(sources, targets))]
    for copy in copies:
        copy.start()
    for copy in copies:
        copy.wait()


def local(sizes, *args):
    fields = args[:11]
    samples, weights, gain, row, column, line = args[11:]
    block = fields[0].shape
    n_traces = samples.shape[0]
    receivers = [ids.reshape(1, -1) for ids in (row, column, line)]
    f32 = jnp.float32
    outs = pl.pallas_call(
        functools.partial(kernel, sizes),
        out_shape=[pltpu.VMEM(block, f32)] * 4,
        in_specs=[pl.BlockSpec(memory_space=pltpu.HBM)] * 17,
        out_specs=[pl.BlockSpec(memory_space=pltpu.VMEM)] * 4,
        scratch_shapes=[
            pltpu.VMEM((2, 2, 16, 8, 128), f32),
            pltpu.VMEM((2, 2, 16, 8, 128), f32),
            pltpu.VMEM((2, 5, 2, 8, 128), f32),
            pltpu.VMEM((2, 8, 128), f32),
            pltpu.VMEM((2, 16, 8, 128), f32),
            pltpu.VMEM((2, 8, 8, 128), f32),
            pltpu.VMEM((2, 8, 8, 128), f32),
            pltpu.VMEM((7, 8, 8, 128), f32),
            pltpu.VMEM((12, 8, 8, 128), f32),
            pltpu.VMEM(samples.shape, f32),
            pltpu.VMEM(weights.shape, f32),
            pltpu.VMEM((1, gain.shape[0]), f32),
            pltpu.VMEM((3, 1, n_traces), jnp.int32),
            pltpu.VMEM((2, RING, 128), f32),
            pltpu.VMEM((2, RING, 128), f32),
            pltpu.VMEM((2, RING, 128), f32),
            pltpu.VMEM((2, 8, 4, 128), f32),
            pltpu.VMEM((8, 128), f32),
            pltpu.VMEM((2, GROUP, 128), f32),
            pltpu.VMEM((8, 128), f32),
            pltpu.VMEM((4, 2, GROUP, 128), f32),
            pltpu.VMEM((4, GROUP, 8, 128), f32),
            pltpu.VMEM((2, 8, 128), f32),
            pltpu.VMEM((8, 128), f32),
            pltpu.VMEM((8, 128), f32),
            pltpu.VMEM((8, 128), f32),
            pltpu.VMEM((3, 2, 8, 128), f32),
            pltpu.SemaphoreType.DMA((17,)),
            pltpu.SemaphoreType.DMA((2, len(OFFSETS))),
            pltpu.SemaphoreType.DMA((2, len(OFFSETS))),
            pltpu.SemaphoreType.DMA((9,)),
            pltpu.SemaphoreType.DMA((9,)),
            pltpu.SemaphoreType.DMA((9,)),
            pltpu.SemaphoreType.DMA((9,)),
            pltpu.SemaphoreType.DMA((GROUP,)),
            pltpu.SemaphoreType.DMA((4, GROUP)),
            pltpu.SemaphoreType.DMA,
            pltpu.SemaphoreType.DMA((4, GROUP)),
            pltpu.SemaphoreType.DMA((8,)),
            pltpu.SemaphoreType.DMA((8,)),
            pltpu.SemaphoreType.DMA((2,)),
            pltpu.SemaphoreType.DMA((2,)),
            pltpu.SemaphoreType.DMA((len(OFFSETS),)),
            pltpu.SemaphoreType.REGULAR,
            pltpu.SemaphoreType.DMA((RING,)),
            pltpu.SemaphoreType.DMA((RING,)),
        ],
        compiler_params=pltpu.CompilerParams(
            collective_id=0, has_side_effects=True, vmem_limit_bytes=60 * 2**20
        ),
        name="wave_steps",
    )(*fields, samples, weights, gain.reshape(1, -1), *receivers)
    return pl.pallas_call(
        hand_over,
        out_shape=[jax.ShapeDtypeStruct(block, f32)] * 4,
        in_specs=[pl.BlockSpec(memory_space=pl.ANY)] * 4,
        out_specs=[pl.BlockSpec(memory_space=pltpu.HBM)] * 4,
        scratch_shapes=[pltpu.SemaphoreType.DMA((4,))],
        compiler_params=pltpu.CompilerParams(vmem_limit_bytes=2**20),
        name="hand_over",
    )(*outs)


def solution(mesh):
    sizes = tuple(mesh.shape[axis] for axis in ("inl", "xl", "gz"))
    cells = P("gz", "inl", "xl")
    traces = P(("inl", "xl", "gz"))
    return jax.shard_map(
        functools.partial(local, sizes),
        mesh=mesh,
        in_specs=(cells,) * 11 + (P(("inl", "xl", "gz"), None), P(), P(), traces, traces, traces),
        out_specs=(cells,) * 4,
        check_vma=False,
    )
```

```python
import functools

import jax
import jax.numpy as jnp
from jax import lax
from jax.experimental import pallas as pl
from jax.experimental.pallas import tpu as pltpu
from jax.sharding import PartitionSpec as P

MESH = pl.DeviceIdType.MESH
second_coef = (-205.0 / 72.0, 8.0 / 5.0, -1.0 / 5.0, 8.0 / 315.0, -1.0 / 560.0)
first_coef = (0.0, 4.0 / 5.0, -1.0 / 5.0, 4.0 / 105.0, -1.0 / 280.0)

OFFSETS = (
    [(d, e, f) for d in (-1, 1) for e, f in ((0, 0), (0, 1), (0, -1), (1, 0), (-1, 0))]
    + [(0, d, e) for d in (1, -1) for e in (1, -1)]
    + [(0, d, 0) for d in (1, -1)]
    + [(0, 0, d) for d in (1, -1)]
)
RING = 16
GROUP = 8
SLOTS = 4
WORDS = 16
BESIDE = [(d, e) for d in (1, -1, 0) for e in (1, -1, 0) if d != 0 or e != 0]


def iota(shape, axis):
    return lax.broadcasted_iota(jnp.int32, shape, axis)


def shifted(body, halo, axis):
    size = body.shape[axis]
    place = iota(body.shape, axis)
    above = [pltpu.roll(jnp.where(place < k, halo, body), size - k, axis) for k in range(1, 5)]
    below = [pltpu.roll(jnp.where(place >= size - k, halo, body), k, axis) for k in range(1, 5)]
    return above, below


def slope(above, below):
    total = first_coef[1] * (above[0] - below[0])
    for k in range(2, 5):
        total = total + first_coef[k] * (above[k - 1] - below[k - 1])
    return total


def bend(center, above, below):
    total = second_coef[0] * center
    for k in range(1, 5):
        total = total + second_coef[k] * (above[k - 1] + below[k - 1])
    return total


def kernel(sizes, *refs):
    n_inl, n_xl, n_gz = sizes
    (
        wave_p,
        wave_p_old,
        wave_q,
        wave_q_old,
        courant,
        epsilon,
        delta,
        tilt,
        azimuth,
        shear,
        damping,
        samples,
        weights,
        gain,
        inline,
        crossline,
        shot,
        next_p,
        next_q,
        prior_p,
        prior_q,
        body,
        side,
        packed,
        parcel,
        edge_y,
        edge_xy,
        old,
        field,
        coef,
        trace,
        small_w,
        small_g,
        small_r,
        letters,
        transit,
        mail,
        passing,
        passing_parcel,
        bundle,
        bundle_far,
        heap,
        heap_far,
        plane,
        plane_far,
        plane_side,
        plane_parcel,
        plane_packed,
        load_sem,
        send_sem,
        recv_sem,
        letter_send,
        letter_recv,
        relay_send,
        relay_recv,
        bundle_send,
        bundle_recv,
        far_send,
        far_recv,
        plane_send,
        plane_recv,
        pass_send,
        pass_recv,
        onward_send,
        known,
        direct_send,
        direct_recv,
    ) = refs
    i = lax.axis_index("inl")
    j = lax.axis_index("xl")
    g = lax.axis_index("gz")
    depth, across, along = 8, 8, 128
    half = n_inl // 2
    ring = 2 * n_xl
    high, low = i // half, i % half
    level = high * n_xl + j
    quarter = ring // 4
    border = jnp.where(high == 0, half - 1, 0)
    on_border = low == border
    surface = g == 0
    even, odd = low % 2 == 0, low % 2 == 1
    near_side, far_side = i == half - 1, i == half
    forwards = (low == half - 1) & (level >= quarter) & (level < quarter + n_xl)

    loads = [
        (wave_p, body.at[0, 0, pl.ds(4, depth)]),
        (wave_q, body.at[0, 1, pl.ds(4, depth)]),
        (wave_p_old, old.at[0]),
        (wave_q_old, old.at[1]),
        (courant, field.at[0]),
        (epsilon, field.at[1]),
        (delta, field.at[2]),
        (tilt, field.at[3]),
        (azimuth, field.at[4]),
        (shear, field.at[5]),
        (damping, field.at[6]),
        (samples, trace),
        (weights, small_w),
        (gain, small_g),
        (inline, small_r.at[0]),
        (crossline, small_r.at[1]),
        (shot, small_r.at[2]),
    ]
    loads = [pltpu.make_async_copy(a, b, load_sem.at[k]) for k, (a, b) in enumerate(loads)]
    nothing = jnp.zeros((2, 4, across, along), jnp.float32)
    for turn in range(2):
        body[turn, :, 0:4] = nothing
        body[turn, :, 12:16] = nothing
        for k in range(4):
            side[turn, :, 4 * k : 4 * k + 4] = nothing
        packed[turn] = jnp.zeros((5, 2, across, along), jnp.float32)
    mail[...] = jnp.zeros((2, RING, along), jnp.float32)
    heap[...] = jnp.zeros((4, 2, GROUP, along), jnp.float32)
    for layer in range(4):
        heap_far[layer] = jnp.zeros((GROUP, across, along), jnp.float32)
    plane_far[...] = jnp.zeros((across, along), jnp.float32)
    plane_side[...] = jnp.zeros((across, along), jnp.float32)
    plane_packed[...] = jnp.zeros((3, 2, across, along), jnp.float32)

    def there(offset):
        d, e, f = offset
        ok = []
        for step, place, count in ((d, i, n_inl), (e, j, n_xl), (f, g, n_gz)):
            if step == 1:
                ok.append(place < count - 1)
            if step == -1:
                ok.append(place > 0)
        return functools.reduce(jnp.logical_and, ok)

    def device(offset):
        d, e, f = offset
        return (
            jnp.clip(i + d, 0, n_inl - 1),
            jnp.clip(j + e, 0, n_xl - 1),
            jnp.clip(g + f, 0, n_gz - 1),
        )

    def on_ring(k):
        place = lax.rem(level + k + ring, ring)
        return (place // n_xl * half + low, lax.rem(place, n_xl), g)

    def in_group(k, layer):
        return (high * half + lax.rem(low + k, half), j, layer)

    barrier = pltpu.get_barrier_semaphore()
    count = jnp.where(even, ring - 1, 2 * quarter) + jnp.where(surface, half - 1, half)
    near_ring = [k for k in range(-quarter, quarter + 1) if k != 0]
    far_ring = [k for k in range(-ring // 2, ring // 2) if k != 0]

    @pl.when(even)
    def _():
        for k in far_ring:
            pl.semaphore_signal(barrier, inc=1, device_id=on_ring(k), device_id_type=MESH)

    @pl.when(odd)
    def _():
        for k in near_ring:
            pl.semaphore_signal(barrier, inc=1, device_id=on_ring(k), device_id_type=MESH)

    def inside(place, count):
        return (place >= 0) & (place < count)

    def from_half_way(offset):
        _, e, f = offset
        ok = far_side & inside(j - e, n_xl) & inside(g - f, n_gz)
        place = jnp.clip(j - e, 0, n_xl - 1) + quarter
        return ok, (place // n_xl * half + half - 1, lax.rem(place, n_xl), jnp.clip(g - f, 0, n_gz - 1))

    def to_far_side(offset):
        _, e, f = offset
        place = level - quarter + e
        ok = forwards & inside(place, n_xl) & inside(g + f, n_gz)
        return ok, (half, jnp.clip(place, 0, n_xl - 1), jnp.clip(g + f, 0, n_gz - 1))

    for offset in OFFSETS:
        d = offset[0]
        hears = there(offset)
        if d == -1:
            hears = hears & jnp.logical_not(far_side)
        if d == 1:
            ok, whom = from_half_way(offset)

            @pl.when(ok)
            def _(whom=whom):
                pl.semaphore_signal(barrier, inc=1, device_id=whom, device_id_type=MESH)

            count = count + to_far_side(offset)[0].astype(jnp.int32)

        @pl.when(hears)
        def _(offset=offset):
            pl.semaphore_signal(barrier, inc=1, device_id=device(offset), device_id_type=MESH)

        direct = there(offset)
        if d == 1:
            direct = direct & jnp.logical_not(near_side)
        count = count + direct.astype(jnp.int32)

    @pl.when(surface)
    def _():
        for layer in range(n_gz):
            for k in range(half):
                if layer > 0 or k > 0:
                    pl.semaphore_signal(
                        barrier, inc=1, device_id=in_group(k, layer), device_id_type=MESH
                    )

    for copy in loads:
        copy.start()
    for copy in loads:
        copy.wait()

    def prepare(z, _):
        sin_t, cos_t = jnp.sin(field[3, z]), jnp.cos(field[3, z])
        sin_f, cos_f = jnp.sin(field[4, z]), jnp.cos(field[4, z])
        coef[0, z] = sin_t * sin_t * cos_f * cos_f
        coef[1, z] = sin_t * sin_t * sin_f * sin_f
        coef[2, z] = cos_t * cos_t
        coef[3, z] = 2.0 * sin_t * sin_t * sin_f * cos_f
        coef[4, z] = 2.0 * sin_t * cos_t * cos_f
        coef[5, z] = 2.0 * sin_t * cos_t * sin_f
        c, s = field[0, z], field[5, z]
        grow, lean = 1.0 + 2.0 * field[1, z], 1.0 + 2.0 * field[2, z]
        coef[6, z] = c * grow
        coef[7, z] = c * (s - grow)
        coef[8, z] = c * (1.0 - s)
        coef[9, z] = c * (lean - s)
        coef[10, z] = c * s
        coef[11, z] = 1.0 - field[6, z]
        return 0

    lax.fori_loop(0, depth, prepare, 0)

    n_traces = trace.shape[0]
    row, column, line = small_r[0], small_r[1], small_r[2]
    lines = small_g.shape[1]
    picked = jnp.where(iota((lines, n_traces), 0) == line, 1.0, 0.0).astype(jnp.float32)
    gains = jnp.dot(
        small_g[...],
        picked,
        precision=lax.Precision.HIGHEST,
        preferred_element_type=jnp.float32,
    )
    amplitude = (
        lax.dot_general(
            small_w[...],
            trace[...],
            (((1,), (1,)), ((), ())),
            precision=lax.Precision.HIGHEST,
            preferred_element_type=jnp.float32,
        )
        * gains
    )
    to_inl, to_xl = row >> 3, column >> 7
    cell = ((row & 7) << 7) + (column & 127) + 1
    to_high = jnp.where(to_inl >= half, 1, 0)
    to_low = to_inl - to_high * half
    owner = to_inl * n_xl + to_xl
    columns = n_inl * n_xl
    member = jnp.where(iota((columns, n_traces), 0) == owner, 1.0, 0.0).astype(jnp.float32)
    earlier = jnp.where(
        iota((n_traces, n_traces), 0) < iota((n_traces, n_traces), 1), 1.0, 0.0
    ).astype(jnp.float32)
    before = jnp.dot(
        member.astype(jnp.bfloat16),
        earlier.astype(jnp.bfloat16),
        preferred_element_type=jnp.float32,
    )
    rank = jnp.sum(member * before, axis=0, keepdims=True).astype(jnp.int32)
    to_level = to_high * n_xl + to_xl
    block = to_low - low
    block = jnp.where(block < 0, block + half, block)
    word = block * WORDS + rank
    spot = iota((along, n_traces), 0)
    content = (
        jnp.where(spot == word, amplitude[0:1, :], 0.0)
        + jnp.where(spot == word + SLOTS, amplitude[1:2, :], 0.0)
        + jnp.where(spot == word + 2 * SLOTS, cell.astype(jnp.float32), 0.0)
    )
    leaves = (to_inl == half - 1) & ((row & 7) >= 4)
    enters = (to_inl == half) & ((row & 7) < 4)
    far_level = jnp.where(leaves, n_xl + to_xl, to_xl)
    far_word = 2 * SLOTS * level + rank
    far_content = jnp.where(spot == far_word, amplitude[0:1, :], 0.0) + jnp.where(
        spot == far_word + SLOTS, cell.astype(jnp.float32), 0.0
    )

    def write(target, wanted, words):
        hop = target - level + ring // 2
        hop = jnp.where(hop < 0, hop + ring, jnp.where(hop >= ring, hop - ring, hop))
        address = (iota((RING, n_traces), 0) == hop) & wanted
        return lax.dot_general(
            jnp.where(address, 1.0, 0.0).astype(jnp.float32),
            words,
            (((1,), (1,)), ((), ())),
            precision=lax.Precision.HIGHEST,
            preferred_element_type=jnp.float32,
        )

    letters[0] = write(to_level, to_level >= 0, content)
    letters[1] = write(far_level, leaves | enters, far_content)

    lane = iota((across, along), 1)
    sub = iota((across, along), 0)

    def pack(turn):
        total = jnp.zeros((across, along), jnp.float32)
        for f in range(2):
            for z in range(depth):
                tile = f * depth + z
                moved = pltpu.roll(body[turn, f, 4 + z], (8 * tile + 4) % along, 1)
                total = jnp.where(lane // 8 == tile, moved, total)
        parcel[turn] = total

    pack(0)

    def copies(turn):
        out = []
        mine = body.at[turn]
        beside = side.at[turn]
        for number, offset in enumerate(OFFSETS):
            d, e, f = offset
            if e != 0:
                kind = 0
                if f != 0:
                    kind = 1 if f == 1 else 2
                if d != 0:
                    kind = 3 if d == 1 else 4
                source = parcel.at[turn]
                target = packed.at[turn, kind, 0 if e == 1 else 1]
            else:
                deep = {0: (4, 8, 4), 1: (8, 4, 0), -1: (4, 4, 12)}[f]
                if d == 0:
                    source = mine.at[:, pl.ds(deep[0], deep[1])]
                    target = mine.at[:, pl.ds(deep[2], deep[1])]
                else:
                    wide = pl.ds(4 if d == 1 else 0, 4)
                    source = mine.at[:, pl.ds(deep[0], deep[1]), wide]
                    target = beside.at[:, pl.ds(deep[2], deep[1]), wide]
            out.append(
                pltpu.make_async_remote_copy(
                    src_ref=source,
                    dst_ref=target,
                    send_sem=send_sem.at[turn, number],
                    recv_sem=recv_sem.at[turn, number],
                    device_id=device(offset),
                    device_id_type=MESH,
                )
            )
        return out

    def sends(turn, offset):
        if turn == 0 and offset[0] == 1:
            return there(offset) & jnp.logical_not(near_side)
        return there(offset)

    def begin(turn):
        for offset, copy in zip(OFFSETS, copies(turn)):

            @pl.when(sends(turn, offset))
            def _(copy=copy):
                copy.start()

    def arrive(turn):
        for offset, copy in list(zip(OFFSETS, copies(turn)))[::-1]:

            @pl.when(there(tuple(-d for d in offset)))
            def _(copy=copy):
                copy.wait_recv()

    def depart(turn):
        for offset, copy in zip(OFFSETS, copies(turn)):

            @pl.when(sends(turn, offset))
            def _(copy=copy):
                copy.wait_send()

    def to_half_way(part):
        source = body.at[0, :, pl.ds(4, depth), pl.ds(4, 4)] if part == 0 else parcel.at[0]
        return pltpu.make_async_remote_copy(
            src_ref=source,
            dst_ref=passing if part == 0 else passing_parcel,
            send_sem=pass_send.at[part],
            recv_sem=pass_recv.at[part],
            device_id=on_ring(quarter),
            device_id_type=MESH,
        )

    def onward(number):
        _, e, f = OFFSETS[number]
        if e != 0:
            source = passing_parcel
            target = packed.at[0, 3, 0 if e == 1 else 1]
        else:
            first, deep, goal = {0: (0, 8, 4), 1: (4, 4, 0), -1: (0, 4, 12)}[f]
            source = passing.at[:, pl.ds(first, deep)]
            target = side.at[0, :, pl.ds(goal, deep), pl.ds(4, 4)]
        return pltpu.make_async_remote_copy(
            src_ref=source,
            dst_ref=target,
            send_sem=onward_send.at[number],
            recv_sem=recv_sem.at[0, number],
            device_id=to_far_side(OFFSETS[number])[1],
            device_id_type=MESH,
        )

    crossing = [number for number, offset in enumerate(OFFSETS) if offset[0] == 1]

    def letter(k):
        rows = pl.ds(2 * (k + quarter), 2)
        return pltpu.make_async_remote_copy(
            src_ref=letters.at[:, rows],
            dst_ref=transit.at[:, rows],
            send_sem=letter_send.at[k + quarter],
            recv_sem=letter_recv.at[k + quarter],
            device_id=on_ring(k),
            device_id_type=MESH,
        )

    def direct_letter(k):
        row = pl.ds(k + ring // 2, 1)
        return pltpu.make_async_remote_copy(
            src_ref=letters.at[:, row],
            dst_ref=mail.at[:, row],
            send_sem=direct_send.at[k + ring // 2],
            recv_sem=direct_recv.at[k + ring // 2],
            device_id=on_ring(k),
            device_id_type=MESH,
        )

    def relay_rows(k):
        first = max(2 * (k + quarter) - 1, 0)
        return first, min(2 * (k + quarter) + 1, ring) - first

    def relay(k):
        rows = pl.ds(*relay_rows(k))
        return pltpu.make_async_remote_copy(
            src_ref=transit.at[:, rows],
            dst_ref=mail.at[:, rows],
            send_sem=relay_send.at[k + quarter],
            recv_sem=relay_recv.at[k + quarter],
            device_id=on_ring(k),
            device_id_type=MESH,
        )

    def parcel_of(k, layer):
        return pltpu.make_async_remote_copy(
            src_ref=bundle.at[:, pl.ds(k, 1)],
            dst_ref=heap.at[layer, :, pl.ds(k, 1)],
            send_sem=bundle_send.at[k],
            recv_sem=bundle_recv.at[layer, k],
            device_id=in_group(k, 0),
            device_id_type=MESH,
        )

    def far_parcel(layer, place):
        return pltpu.make_async_remote_copy(
            src_ref=bundle_far,
            dst_ref=heap_far.at[layer, place],
            send_sem=far_send,
            recv_sem=far_recv.at[layer, place],
            device_id=(high * half + border, j, 0),
            device_id_type=MESH,
        )

    def post():
        @pl.when(even)
        def _():
            for k in far_ring:
                direct_letter(k).wait_recv()

        @pl.when(odd)
        def _():
            for k in near_ring:
                relay(k).wait_recv()

        for t in range(2):
            got = mail[0, 8 * t : 8 * t + 8, :]
            turned = jnp.zeros((GROUP, along), jnp.float32)
            for d in range(GROUP):
                moved = got if d == 0 else pltpu.roll(pltpu.roll(got, d, 0), along - WORDS * d, 1)
                turned = jnp.where(((sub - lane // WORDS) & 7) == d, moved, turned)
            bundle[t] = turned
        far = jnp.sum(mail[1], axis=0, keepdims=True)
        bundle_far[...] = jnp.where(sub == low, far, 0.0)
        for k in range(1, half):
            parcel_of(k, g).start()

        @pl.when(jnp.logical_not(surface))
        def _():
            parcel_of(0, g).start()

        @pl.when(surface)
        def _():
            heap[0, :, 0:1] = bundle[:, 0:1]

        @pl.when(jnp.logical_not(surface & on_border))
        def _():
            far_parcel(g, low).start()

        @pl.when(surface & on_border)
        def _():
            heap_far[0, border] = bundle_far[...]

    pl.semaphore_wait(barrier, count)

    @pl.when(even)
    def _():
        for k in far_ring:
            direct_letter(k).start()

    @pl.when(odd)
    def _():
        for k in range(-quarter, quarter):
            if k != 0:
                letter(k).start()

    @pl.when(near_side)
    def _():
        for part in range(2):
            to_half_way(part).start()

    begin(0)

    @pl.when(forwards)
    def _():
        pl.semaphore_signal(known, inc=1, device_id=on_ring(-quarter), device_id_type=MESH)
        for part in range(2):
            to_half_way(part).wait_recv()
        for number in crossing:

            @pl.when(to_far_side(OFFSETS[number])[0])
            def _(number=number):
                onward(number).start()

    @pl.when(even)
    def _():
        own = pl.ds(ring // 2, 1)
        mail[:, own] = letters[:, own]

    @pl.when(odd)
    def _():
        own = pl.ds(2 * quarter, 2)
        transit[:, own] = letters[:, own]
        for k in range(-quarter, quarter):
            if k != 0:
                letter(k).wait_recv()
        for k in near_ring:
            relay(k).start()
        kept = pl.ds(*relay_rows(0))
        mail[:, kept] = transit[:, kept]

    def unpack(turn):
        def pair(kind):
            return jnp.where(lane % 8 < 4, packed[turn, kind, 0], packed[turn, kind, 1])

        plain = pair(0)
        deep = jnp.where((lane // 8) % 8 >= 4, pair(1), pair(2))
        wide = jnp.where(sub < 4, pair(4), pair(3))
        for f in range(2):
            for z in range(depth):
                turnback = (along - 4 - 8 * (f * depth + z)) % along
                edge_y[f, 4 + z] = pltpu.roll(plain, turnback, 1)
                edge_y[f, z - 4 if z >= 4 else 12 + z] = pltpu.roll(deep, turnback, 1)
                edge_xy[f, z] = pltpu.roll(wide, turnback, 1)

    def advance(turn, store):
        def layer(z, _):
            first, whole = [], []
            for f in range(2):
                center = body[turn, f, z + 4]
                beside = side[turn, f, z + 4]
                edge = edge_y[f, z + 4]
                above = [body[turn, f, z + 4 + k] for k in range(1, 5)]
                below = [body[turn, f, z + 4 - k] for k in range(1, 5)]
                u_zz = bend(center, above, below)
                grad_z = slope(above, below)
                grad_z_side = slope(
                    [side[turn, f, z + 4 + k] for k in range(1, 5)],
                    [side[turn, f, z + 4 - k] for k in range(1, 5)],
                )
                grad_z_edge = slope(
                    [edge_y[f, z + 4 + k] for k in range(1, 5)],
                    [edge_y[f, z + 4 - k] for k in range(1, 5)],
                )
                x_moves = shifted(center, beside, 0)
                u_xx = bend(center, *x_moves)
                grad_x = slope(*x_moves)
                grad_x_edge = slope(*shifted(edge, edge_xy[f, z], 0))
                u_yy = bend(center, *shifted(center, edge, 1))
                u_xy = slope(*shifted(grad_x, grad_x_edge, 1))
                u_xz = slope(*shifted(grad_z, grad_z_side, 0))
                u_yz = slope(*shifted(grad_z, grad_z_edge, 1))
                first.append(
                    coef[0, z] * u_xx
                    + coef[1, z] * u_yy
                    + coef[2, z] * u_zz
                    + coef[3, z] * u_xy
                    + coef[4, z] * u_xz
                    + coef[5, z] * u_yz
                )
                whole.append(u_xx + u_yy + u_zz)
            stay = coef[11, z]
            now_p, now_q = body[turn, 0, z + 4], body[turn, 1, z + 4]
            if turn == 0:
                was_p, was_q = old[0, z], old[1, z]
            else:
                was_p, was_q = body[0, 0, z + 4], body[0, 1, z + 4]
            mixed = coef[8, z] * first[1]
            new_p = (
                now_p
                + stay * (now_p - was_p)
                + (coef[6, z] * whole[0] + coef[7, z] * first[0] + mixed)
            )
            new_q = (
                now_q
                + stay * (now_q - was_q)
                + (coef[9, z] * (whole[0] - first[0]) + coef[10, z] * whole[1] + mixed)
            )
            store(z, new_p, new_q)
            return 0

        lax.fori_loop(0, depth, layer, 0, unroll=8)

    def keep(z, new_p, new_q):
        body[1, 0, z + 4] = new_p
        body[1, 1, z + 4] = new_q

    def finish(z, new_p, new_q):
        next_p[z] = new_p
        next_q[z] = new_q

    late = (high == 0) & on_border

    @pl.when(late)
    def _():
        post()

    arrive(0)
    unpack(0)
    advance(0, keep)
    pack(1)

    @pl.when(near_side)
    def _():
        pl.semaphore_wait(known, 1)

    begin(1)

    @pl.when(jnp.logical_not(late))
    def _():
        post()

    def add_up(label, values):
        label_x, label_y = label >> 7, label & 127
        pieces = []
        for rest in values:
            for _ in range(3):
                rounded = rest.astype(jnp.bfloat16).astype(jnp.float32)
                pieces.append(rounded)
                rest = rest - rounded
        total = jnp.zeros((len(pieces) * across, along), jnp.float32)
        for r in range(0, 2 * GROUP, 2):

            def flat(array):
                return jnp.concatenate([array[r : r + 1], array[r + 1 : r + 2]], axis=1)

            at_x = iota((across, 2 * along), 0) == flat(label_x)
            left = jnp.concatenate([jnp.where(at_x, flat(piece), 0.0) for piece in pieces], axis=0)
            right = jnp.where(iota((along, 2 * along), 0) == flat(label_y), 1.0, 0.0)
            total = total + lax.dot_general(
                left.astype(jnp.bfloat16),
                right.astype(jnp.bfloat16),
                (((1,), (1,)), ((), ())),
                preferred_element_type=jnp.float32,
            )
        return [
            total[24 * k : 24 * k + 8] + total[24 * k + 8 : 24 * k + 16] + total[24 * k + 16 : 24 * k + 24]
            for k in range(len(values))
        ]

    def plane_there(d, e):
        crosses = jnp.bool_(False)
        if d == 1:
            crosses = i == half - 1
        if d == -1:
            crosses = i == half
        return there((d, e, 0)) & jnp.logical_not(crosses)

    def plane_copy(number):
        d, e = BESIDE[number]
        if e == 0:
            rows = pl.ds(4 if d == 1 else 0, 4)
            source, target = plane.at[0, rows], plane_side.at[rows]
        else:
            source, target = plane_parcel, plane_packed.at[{0: 0, 1: 1, -1: 2}[d], 0 if e == 1 else 1]
        return pltpu.make_async_remote_copy(
            src_ref=source,
            dst_ref=target,
            send_sem=plane_send.at[number],
            recv_sem=plane_recv.at[number],
            device_id=device((d, e, 0)),
            device_id_type=MESH,
        )

    def plane_start(parcels):
        for number, (d, e) in enumerate(BESIDE):
            if (e != 0) == parcels:

                @pl.when(plane_there(d, e))
                def _(number=number):
                    plane_copy(number).start()

    @pl.when(surface)
    def _():
        for layer in range(n_gz):
            for k in range(half):
                if layer > 0 or k > 0:
                    parcel_of(k, layer).wait_recv()
        place = iota((2 * GROUP, along), 1) % WORDS // SLOTS
        parts = [heap[layer].reshape(2 * GROUP, along) for layer in range(4)]

        def gather(kind):
            total = jnp.zeros((2 * GROUP, along), jnp.float32)
            for layer in range(4):
                shift = SLOTS * (layer - kind) % along
                moved = parts[layer] if shift == 0 else pltpu.roll(parts[layer], shift, 1)
                total = jnp.where(place == layer, moved, total)
            return total

        sums = add_up(gather(2).astype(jnp.int32) - 1, [gather(0), gather(1)])
        plane[0] = sums[0]
        plane[1] = sums[1]
        plane_start(False)

    @pl.when(surface & on_border)
    def _():
        for layer in range(n_gz):
            for place in range(half):

                @pl.when((layer > 0) | (border != place))
                def _(layer=layer, place=place):
                    far_parcel(layer, place).wait_recv()

        parts = [jnp.sum(heap_far[layer], axis=0) for layer in range(4)]
        front = lane % 8 < 4
        values, labels = [], []
        for k in (0, 2):
            values.append(jnp.where(front, parts[k], pltpu.roll(parts[k + 1], SLOTS, 1)))
            labels.append(jnp.where(front, pltpu.roll(parts[k], along - SLOTS, 1), parts[k + 1]))
        label = jnp.concatenate(labels, axis=0).astype(jnp.int32) - 1
        [total] = add_up(label, [jnp.concatenate(values, axis=0)])
        plane_far[...] = total

        @pl.when(high == 0)
        def _():
            plane_side[0:4] = total[0:4]

        @pl.when(high != 0)
        def _():
            plane_side[4:8] = total[4:8]

    @pl.when(surface)
    def _():
        plane_parcel[...] = jnp.where(
            lane < 8, pltpu.roll(plane[0], 4, 1), pltpu.roll(plane_far[...], 12, 1)
        )
        plane_start(True)

    depart(1)
    depart(0)

    @pl.when(near_side)
    def _():
        for part in range(2):
            to_half_way(part).wait_send()

    @pl.when(forwards)
    def _():
        for number in crossing:

            @pl.when(to_far_side(OFFSETS[number])[0])
            def _(number=number):
                onward(number).wait_send()

    @pl.when(even)
    def _():
        for k in far_ring:
            direct_letter(k).wait_send()

    @pl.when(odd)
    def _():
        for k in range(-quarter, quarter):
            if k != 0:
                letter(k).wait_send()
        for k in near_ring:
            relay(k).wait_send()

    for k in range(1, half):
        parcel_of(k, g).wait_send()

    @pl.when(jnp.logical_not(surface))
    def _():
        parcel_of(0, g).wait_send()

    @pl.when(jnp.logical_not(surface & on_border))
    def _():
        far_parcel(g, low).wait_send()

    @pl.when(surface)
    def _():
        for number, (d, e) in enumerate(BESIDE):

            @pl.when(plane_there(d, e))
            def _(number=number):
                plane_copy(number).wait_send()

    @pl.when(surface)
    def _():
        for number, (d, e) in enumerate(BESIDE):

            @pl.when(plane_there(-d, -e))
            def _(number=number):
                plane_copy(number).wait_recv()

    arrive(1)
    unpack(1)

    @pl.when(surface)
    def _():
        def pair(kind):
            return jnp.where(lane % 8 < 4, plane_packed[kind, 0], plane_packed[kind, 1])

        same = pair(0)
        edge = pltpu.roll(same, along - 4, 1)
        corner = pltpu.roll(jnp.where(sub < 4, pair(2), pair(1)), along - 4, 1) + pltpu.roll(
            same, along - 12, 1
        )
        for f in range(2):
            body[1, f, 4] = body[1, f, 4] + plane[0]
            side[1, f, 4] = side[1, f, 4] + plane_side[...]
            edge_y[f, 4] = edge_y[f, 4] + edge
            edge_xy[f, 0] = edge_xy[f, 0] + corner

    for f, prior in enumerate((prior_p, prior_q)):
        prior[...] = body[1, f, 4:12]
    advance(1, finish)

    @pl.when(surface)
    def _():
        for result in (next_p, next_q):
            result[0] = result[0] + plane[1]


def hand_over(*refs):
    sources, targets, sem = refs[:4], refs[4:8], refs[8]
    copies = [pltpu.make_async_copy(a, b, sem.at[k]) for k, (a, b) in enumerate(zip(sources, targets))]
    for copy in copies:
        copy.start()
    for copy in copies:
        copy.wait()


def local(sizes, *args):
    fields = args[:11]
    samples, weights, gain, row, column, line = args[11:]
    block = fields[0].shape
    n_traces = samples.shape[0]
    receivers = [ids.reshape(1, -1) for ids in (row, column, line)]
    f32 = jnp.float32
    outs = pl.pallas_call(
        functools.partial(kernel, sizes),
        out_shape=[pltpu.VMEM(block, f32)] * 4,
        in_specs=[pl.BlockSpec(memory_space=pltpu.HBM)] * 17,
        out_specs=[pl.BlockSpec(memory_space=pltpu.VMEM)] * 4,
        scratch_shapes=[
            pltpu.VMEM((2, 2, 16, 8, 128), f32),
            pltpu.VMEM((2, 2, 16, 8, 128), f32),
            pltpu.VMEM((2, 5, 2, 8, 128), f32),
            pltpu.VMEM((2, 8, 128), f32),
            pltpu.VMEM((2, 16, 8, 128), f32),
            pltpu.VMEM((2, 8, 8, 128), f32),
            pltpu.VMEM((2, 8, 8, 128), f32),
            pltpu.VMEM((7, 8, 8, 128), f32),
            pltpu.VMEM((12, 8, 8, 128), f32),
            pltpu.VMEM(samples.shape, f32),
            pltpu.VMEM(weights.shape, f32),
            pltpu.VMEM((1, gain.shape[0]), f32),
            pltpu.VMEM((3, 1, n_traces), jnp.int32),
            pltpu.VMEM((2, RING, 128), f32),
            pltpu.VMEM((2, RING, 128), f32),
            pltpu.VMEM((2, RING, 128), f32),
            pltpu.VMEM((2, 8, 4, 128), f32),
            pltpu.VMEM((8, 128), f32),
            pltpu.VMEM((2, GROUP, 128), f32),
            pltpu.VMEM((8, 128), f32),
            pltpu.VMEM((4, 2, GROUP, 128), f32),
            pltpu.VMEM((4, GROUP, 8, 128), f32),
            pltpu.VMEM((2, 8, 128), f32),
            pltpu.VMEM((8, 128), f32),
            pltpu.VMEM((8, 128), f32),
            pltpu.VMEM((8, 128), f32),
            pltpu.VMEM((3, 2, 8, 128), f32),
            pltpu.SemaphoreType.DMA((17,)),
            pltpu.SemaphoreType.DMA((2, len(OFFSETS))),
            pltpu.SemaphoreType.DMA((2, len(OFFSETS))),
            pltpu.SemaphoreType.DMA((9,)),
            pltpu.SemaphoreType.DMA((9,)),
            pltpu.SemaphoreType.DMA((9,)),
            pltpu.SemaphoreType.DMA((9,)),
            pltpu.SemaphoreType.DMA((GROUP,)),
            pltpu.SemaphoreType.DMA((4, GROUP)),
            pltpu.SemaphoreType.DMA,
            pltpu.SemaphoreType.DMA((4, GROUP)),
            pltpu.SemaphoreType.DMA((8,)),
            pltpu.SemaphoreType.DMA((8,)),
            pltpu.SemaphoreType.DMA((2,)),
            pltpu.SemaphoreType.DMA((2,)),
            pltpu.SemaphoreType.DMA((len(OFFSETS),)),
            pltpu.SemaphoreType.REGULAR,
            pltpu.SemaphoreType.DMA((RING,)),
            pltpu.SemaphoreType.DMA((RING,)),
        ],
        compiler_params=pltpu.CompilerParams(
            collective_id=0, has_side_effects=True, vmem_limit_bytes=60 * 2**20
        ),
        name="wave_steps",
    )(*fields, samples, weights, gain.reshape(1, -1), *receivers)
    return pl.pallas_call(
        hand_over,
        out_shape=[jax.ShapeDtypeStruct(block, f32)] * 4,
        in_specs=[pl.BlockSpec(memory_space=pl.ANY)] * 4,
        out_specs=[pl.BlockSpec(memory_space=pltpu.HBM)] * 4,
        scratch_shapes=[pltpu.SemaphoreType.DMA((4,))],
        compiler_params=pltpu.CompilerParams(vmem_limit_bytes=2**20),
        name="hand_over",
    )(*outs)


def solution(mesh):
    sizes = tuple(mesh.shape[axis] for axis in ("inl", "xl", "gz"))
    cells = P("gz", "inl", "xl")
    traces = P(("inl", "xl", "gz"))
    return jax.shard_map(
        functools.partial(local, sizes),
        mesh=mesh,
        in_specs=(cells,) * 11 + (P(("inl", "xl", "gz"), None), P(), P(), traces, traces, traces),
        out_specs=(cells,) * 4,
        check_vma=False,
    )
```

```python
import functools

import jax
import jax.numpy as jnp
from jax import lax
from jax.experimental import pallas as pl
from jax.experimental.pallas import tpu as pltpu
from jax.sharding import PartitionSpec as P

MESH = pl.DeviceIdType.MESH
second_coef = (-205.0 / 72.0, 8.0 / 5.0, -1.0 / 5.0, 8.0 / 315.0, -1.0 / 560.0)
first_coef = (0.0, 4.0 / 5.0, -1.0 / 5.0, 4.0 / 105.0, -1.0 / 280.0)

OFFSETS = (
    [(d, e, f) for d in (-1, 1) for e, f in ((0, 0), (0, 1), (0, -1), (1, 0), (-1, 0))]
    + [(0, d, e) for d in (1, -1) for e in (1, -1)]
    + [(0, d, 0) for d in (1, -1)]
    + [(0, 0, d) for d in (1, -1)]
)
RING = 16
GROUP = 8
SLOTS = 4
WORDS = 16
BESIDE = [(d, e) for d in (1, -1, 0) for e in (1, -1, 0) if d != 0 or e != 0]


def iota(shape, axis):
    return lax.broadcasted_iota(jnp.int32, shape, axis)


def shifted(body, halo, axis):
    size = body.shape[axis]
    place = iota(body.shape, axis)
    above = [pltpu.roll(jnp.where(place < k, halo, body), size - k, axis) for k in range(1, 5)]
    below = [pltpu.roll(jnp.where(place >= size - k, halo, body), k, axis) for k in range(1, 5)]
    return above, below


def slope(above, below):
    total = first_coef[1] * (above[0] - below[0])
    for k in range(2, 5):
        total = total + first_coef[k] * (above[k - 1] - below[k - 1])
    return total


def bend(center, above, below):
    total = second_coef[0] * center
    for k in range(1, 5):
        total = total + second_coef[k] * (above[k - 1] + below[k - 1])
    return total


def kernel(sizes, *refs):
    n_inl, n_xl, n_gz = sizes
    (
        wave_p,
        wave_p_old,
        wave_q,
        wave_q_old,
        courant,
        epsilon,
        delta,
        tilt,
        azimuth,
        shear,
        damping,
        samples,
        weights,
        gain,
        inline,
        crossline,
        shot,
        next_p,
        next_q,
        prior_p,
        prior_q,
        body,
        side,
        packed,
        parcel,
        edge_y,
        edge_xy,
        old,
        field,
        coef,
        trace,
        small_w,
        small_g,
        small_r,
        letters,
        transit,
        mail,
        passing,
        passing_parcel,
        bundle,
        bundle_far,
        heap,
        heap_far,
        plane,
        plane_far,
        plane_side,
        plane_parcel,
        plane_packed,
        load_sem,
        send_sem,
        recv_sem,
        letter_send,
        letter_recv,
        relay_send,
        relay_recv,
        bundle_send,
        bundle_recv,
        far_send,
        far_recv,
        plane_send,
        plane_recv,
        pass_send,
        pass_recv,
        onward_send,
        known,
        direct_send,
        direct_recv,
    ) = refs
    i = lax.axis_index("inl")
    j = lax.axis_index("xl")
    g = lax.axis_index("gz")
    depth, across, along = 8, 8, 128
    half = n_inl // 2
    ring = 2 * n_xl
    high, low = i // half, i % half
    level = high * n_xl + j
    quarter = ring // 4
    border = jnp.where(high == 0, half - 1, 0)
    on_border = low == border
    surface = g == 0
    even, odd = low % 2 == 0, low % 2 == 1
    near_side, far_side = i == half - 1, i == half
    forwards = (low == half - 1) & (level >= quarter) & (level < quarter + n_xl)

    loads = [
        (wave_p, body.at[0, 0, pl.ds(4, depth)]),
        (wave_q, body.at[0, 1, pl.ds(4, depth)]),
        (wave_p_old, old.at[0]),
        (wave_q_old, old.at[1]),
        (courant, field.at[0]),
        (epsilon, field.at[1]),
        (delta, field.at[2]),
        (tilt, field.at[3]),
        (azimuth, field.at[4]),
        (shear, field.at[5]),
        (damping, field.at[6]),
        (samples, trace),
        (weights, small_w),
        (gain, small_g),
        (inline, small_r.at[0]),
        (crossline, small_r.at[1]),
        (shot, small_r.at[2]),
    ]
    loads = [pltpu.make_async_copy(a, b, load_sem.at[k]) for k, (a, b) in enumerate(loads)]
    nothing = jnp.zeros((2, 4, across, along), jnp.float32)
    for turn in range(2):
        body[turn, :, 0:4] = nothing
        body[turn, :, 12:16] = nothing
        for k in range(4):
            side[turn, :, 4 * k : 4 * k + 4] = nothing
        packed[turn] = jnp.zeros((5, 2, across, along), jnp.float32)
    mail[...] = jnp.zeros((2, RING, along), jnp.float32)
    heap[...] = jnp.zeros((4, 2, GROUP, along), jnp.float32)
    for layer in range(4):
        heap_far[layer] = jnp.zeros((GROUP, across, along), jnp.float32)
    plane_far[...] = jnp.zeros((across, along), jnp.float32)
    plane_side[...] = jnp.zeros((across, along), jnp.float32)
    plane_packed[...] = jnp.zeros((3, 2, across, along), jnp.float32)

    def there(offset):
        d, e, f = offset
        ok = []
        for step, place, count in ((d, i, n_inl), (e, j, n_xl), (f, g, n_gz)):
            if step == 1:
                ok.append(place < count - 1)
            if step == -1:
                ok.append(place > 0)
        return functools.reduce(jnp.logical_and, ok)

    def device(offset):
        d, e, f = offset
        return (
            jnp.clip(i + d, 0, n_inl - 1),
            jnp.clip(j + e, 0, n_xl - 1),
            jnp.clip(g + f, 0, n_gz - 1),
        )

    def on_ring(k):
        place = lax.rem(level + k + ring, ring)
        return (place // n_xl * half + low, lax.rem(place, n_xl), g)

    def in_group(k, layer):
        return (high * half + lax.rem(low + k, half), j, layer)

    barrier = pltpu.get_barrier_semaphore()
    count = jnp.where(even, ring - 1, 2 * quarter) + jnp.where(surface, half - 1, half)
    near_ring = [k for k in range(-quarter, quarter + 1) if k != 0]
    far_ring = [k for k in range(-ring // 2, ring // 2) if k != 0]

    @pl.when(even)
    def _():
        for k in far_ring:
            pl.semaphore_signal(barrier, inc=1, device_id=on_ring(k), device_id_type=MESH)

    @pl.when(odd)
    def _():
        for k in near_ring:
            pl.semaphore_signal(barrier, inc=1, device_id=on_ring(k), device_id_type=MESH)

    def inside(place, count):
        return (place >= 0) & (place < count)

    def from_half_way(offset):
        _, e, f = offset
        ok = far_side & inside(j - e, n_xl) & inside(g - f, n_gz)
        place = jnp.clip(j - e, 0, n_xl - 1) + quarter
        return ok, (place // n_xl * half + half - 1, lax.rem(place, n_xl), jnp.clip(g - f, 0, n_gz - 1))

    def to_far_side(offset):
        _, e, f = offset
        place = level - quarter + e
        ok = forwards & inside(place, n_xl) & inside(g + f, n_gz)
        return ok, (half, jnp.clip(place, 0, n_xl - 1), jnp.clip(g + f, 0, n_gz - 1))

    for offset in OFFSETS:
        d = offset[0]
        hears = there(offset)
        if d == -1:
            hears = hears & jnp.logical_not(far_side)
        if d == 1:
            ok, whom = from_half_way(offset)

            @pl.when(ok)
            def _(whom=whom):
                pl.semaphore_signal(barrier, inc=1, device_id=whom, device_id_type=MESH)

            count = count + to_far_side(offset)[0].astype(jnp.int32)

        @pl.when(hears)
        def _(offset=offset):
            pl.semaphore_signal(barrier, inc=1, device_id=device(offset), device_id_type=MESH)

        direct = there(offset)
        if d == 1:
            direct = direct & jnp.logical_not(near_side)
        count = count + direct.astype(jnp.int32)

    @pl.when(surface)
    def _():
        for layer in range(n_gz):
            for k in range(half):
                if layer > 0 or k > 0:
                    pl.semaphore_signal(
                        barrier, inc=1, device_id=in_group(k, layer), device_id_type=MESH
                    )

    for copy in loads:
        copy.start()
    for copy in loads:
        copy.wait()

    def prepare(z, _):
        sin_t, cos_t = jnp.sin(field[3, z]), jnp.cos(field[3, z])
        sin_f, cos_f = jnp.sin(field[4, z]), jnp.cos(field[4, z])
        coef[0, z] = sin_t * sin_t * cos_f * cos_f
        coef[1, z] = sin_t * sin_t * sin_f * sin_f
        coef[2, z] = cos_t * cos_t
        coef[3, z] = 2.0 * sin_t * sin_t * sin_f * cos_f
        coef[4, z] = 2.0 * sin_t * cos_t * cos_f
        coef[5, z] = 2.0 * sin_t * cos_t * sin_f
        c, s = field[0, z], field[5, z]
        grow, lean = 1.0 + 2.0 * field[1, z], 1.0 + 2.0 * field[2, z]
        coef[6, z] = c * grow
        coef[7, z] = c * (s - grow)
        coef[8, z] = c * (1.0 - s)
        coef[9, z] = c * (lean - s)
        coef[10, z] = c * s
        coef[11, z] = 1.0 - field[6, z]
        return 0

    lax.fori_loop(0, depth, prepare, 0)

    n_traces = trace.shape[0]
    row, column, line = small_r[0], small_r[1], small_r[2]
    lines = small_g.shape[1]
    picked = jnp.where(iota((lines, n_traces), 0) == line, 1.0, 0.0).astype(jnp.float32)
    gains = jnp.dot(
        small_g[...],
        picked,
        precision=lax.Precision.HIGHEST,
        preferred_element_type=jnp.float32,
    )
    amplitude = (
        lax.dot_general(
            small_w[...],
            trace[...],
            (((1,), (1,)), ((), ())),
            precision=lax.Precision.HIGHEST,
            preferred_element_type=jnp.float32,
        )
        * gains
    )
    to_inl, to_xl = row >> 3, column >> 7
    cell = ((row & 7) << 7) + (column & 127) + 1
    to_high = jnp.where(to_inl >= half, 1, 0)
    to_low = to_inl - to_high * half
    owner = to_inl * n_xl + to_xl
    columns = n_inl * n_xl
    member = jnp.where(iota((columns, n_traces), 0) == owner, 1.0, 0.0).astype(jnp.float32)
    earlier = jnp.where(
        iota((n_traces, n_traces), 0) < iota((n_traces, n_traces), 1), 1.0, 0.0
    ).astype(jnp.float32)
    before = jnp.dot(
        member.astype(jnp.bfloat16),
        earlier.astype(jnp.bfloat16),
        preferred_element_type=jnp.float32,
    )
    rank = jnp.sum(member * before, axis=0, keepdims=True).astype(jnp.int32)
    to_level = to_high * n_xl + to_xl
    block = to_low - low
    block = jnp.where(block < 0, block + half, block)
    word = block * WORDS + rank
    spot = iota((along, n_traces), 0)
    content = (
        jnp.where(spot == word, amplitude[0:1, :], 0.0)
        + jnp.where(spot == word + SLOTS, amplitude[1:2, :], 0.0)
        + jnp.where(spot == word + 2 * SLOTS, cell.astype(jnp.float32), 0.0)
    )
    leaves = (to_inl == half - 1) & ((row & 7) >= 4)
    enters = (to_inl == half) & ((row & 7) < 4)
    far_level = jnp.where(leaves, n_xl + to_xl, to_xl)
    far_word = 2 * SLOTS * level + rank
    far_content = jnp.where(spot == far_word, amplitude[0:1, :], 0.0) + jnp.where(
        spot == far_word + SLOTS, cell.astype(jnp.float32), 0.0
    )

    def write(target, wanted, words):
        hop = target - level + ring // 2
        hop = jnp.where(hop < 0, hop + ring, jnp.where(hop >= ring, hop - ring, hop))
        address = (iota((RING, n_traces), 0) == hop) & wanted
        return lax.dot_general(
            jnp.where(address, 1.0, 0.0).astype(jnp.float32),
            words,
            (((1,), (1,)), ((), ())),
            precision=lax.Precision.HIGHEST,
            preferred_element_type=jnp.float32,
        )

    letters[0] = write(to_level, to_level >= 0, content)
    letters[1] = write(far_level, leaves | enters, far_content)

    lane = iota((across, along), 1)
    sub = iota((across, along), 0)

    def pack(turn):
        total = jnp.zeros((across, along), jnp.float32)
        for f in range(2):
            for z in range(depth):
                tile = f * depth + z
                moved = pltpu.roll(body[turn, f, 4 + z], (8 * tile + 4) % along, 1)
                total = jnp.where(lane // 8 == tile, moved, total)
        parcel[turn] = total

    pack(0)

    def copies(turn):
        out = []
        mine = body.at[turn]
        beside = side.at[turn]
        for number, offset in enumerate(OFFSETS):
            d, e, f = offset
            if e != 0:
                kind = 0
                if f != 0:
                    kind = 1 if f == 1 else 2
                if d != 0:
                    kind = 3 if d == 1 else 4
                source = parcel.at[turn]
                target = packed.at[turn, kind, 0 if e == 1 else 1]
            else:
                deep = {0: (4, 8, 4), 1: (8, 4, 0), -1: (4, 4, 12)}[f]
                if d == 0:
                    source = mine.at[:, pl.ds(deep[0], deep[1])]
                    target = mine.at[:, pl.ds(deep[2], deep[1])]
                else:
                    wide = pl.ds(4 if d == 1 else 0, 4)
                    source = mine.at[:, pl.ds(deep[0], deep[1]), wide]
                    target = beside.at[:, pl.ds(deep[2], deep[1]), wide]
            out.append(
                pltpu.make_async_remote_copy(
                    src_ref=source,
                    dst_ref=target,
                    send_sem=send_sem.at[turn, number],
                    recv_sem=recv_sem.at[turn, number],
                    device_id=device(offset),
                    device_id_type=MESH,
                )
            )
        return out

    def sends(turn, offset):
        if turn == 0 and offset[0] == 1:
            return there(offset) & jnp.logical_not(near_side)
        return there(offset)

    def begin(turn, packed_cells):
        for offset, copy in zip(OFFSETS, copies(turn)):
            if (offset[1] != 0) == packed_cells:

                @pl.when(sends(turn, offset))
                def _(copy=copy):
                    copy.start()

    def arrive(turn):
        for offset, copy in list(zip(OFFSETS, copies(turn)))[::-1]:

            @pl.when(there(tuple(-d for d in offset)))
            def _(copy=copy):
                copy.wait_recv()

    def depart(turn):
        for offset, copy in zip(OFFSETS, copies(turn)):

            @pl.when(sends(turn, offset))
            def _(copy=copy):
                copy.wait_send()

    def to_half_way(part):
        source = body.at[0, :, pl.ds(4, depth), pl.ds(4, 4)] if part == 0 else parcel.at[0]
        return pltpu.make_async_remote_copy(
            src_ref=source,
            dst_ref=passing if part == 0 else passing_parcel,
            send_sem=pass_send.at[part],
            recv_sem=pass_recv.at[part],
            device_id=on_ring(quarter),
            device_id_type=MESH,
        )

    def onward(number):
        _, e, f = OFFSETS[number]
        if e != 0:
            source = passing_parcel
            target = packed.at[0, 3, 0 if e == 1 else 1]
        else:
            first, deep, goal = {0: (0, 8, 4), 1: (4, 4, 0), -1: (0, 4, 12)}[f]
            source = passing.at[:, pl.ds(first, deep)]
            target = side.at[0, :, pl.ds(goal, deep), pl.ds(4, 4)]
        return pltpu.make_async_remote_copy(
            src_ref=source,
            dst_ref=target,
            send_sem=onward_send.at[number],
            recv_sem=recv_sem.at[0, number],
            device_id=to_far_side(OFFSETS[number])[1],
            device_id_type=MESH,
        )

    crossing = [number for number, offset in enumerate(OFFSETS) if offset[0] == 1]

    def letter(k):
        rows = pl.ds(2 * (k + quarter), 2)
        return pltpu.make_async_remote_copy(
            src_ref=letters.at[:, rows],
            dst_ref=transit.at[:, rows],
            send_sem=letter_send.at[k + quarter],
            recv_sem=letter_recv.at[k + quarter],
            device_id=on_ring(k),
            device_id_type=MESH,
        )

    def direct_letter(k):
        row = pl.ds(k + ring // 2, 1)
        return pltpu.make_async_remote_copy(
            src_ref=letters.at[:, row],
            dst_ref=mail.at[:, row],
            send_sem=direct_send.at[k + ring // 2],
            recv_sem=direct_recv.at[k + ring // 2],
            device_id=on_ring(k),
            device_id_type=MESH,
        )

    def relay_rows(k):
        first = max(2 * (k + quarter) - 1, 0)
        return first, min(2 * (k + quarter) + 1, ring) - first

    def relay(k):
        rows = pl.ds(*relay_rows(k))
        return pltpu.make_async_remote_copy(
            src_ref=transit.at[:, rows],
            dst_ref=mail.at[:, rows],
            send_sem=relay_send.at[k + quarter],
            recv_sem=relay_recv.at[k + quarter],
            device_id=on_ring(k),
            device_id_type=MESH,
        )

    def parcel_of(k, layer):
        return pltpu.make_async_remote_copy(
            src_ref=bundle.at[:, pl.ds(k, 1)],
            dst_ref=heap.at[layer, :, pl.ds(k, 1)],
            send_sem=bundle_send.at[k],
            recv_sem=bundle_recv.at[layer, k],
            device_id=in_group(k, 0),
            device_id_type=MESH,
        )

    def far_parcel(layer, place):
        return pltpu.make_async_remote_copy(
            src_ref=bundle_far,
            dst_ref=heap_far.at[layer, place],
            send_sem=far_send,
            recv_sem=far_recv.at[layer, place],
            device_id=(high * half + border, j, 0),
            device_id_type=MESH,
        )

    def post():
        @pl.when(even)
        def _():
            for k in far_ring:
                direct_letter(k).wait_recv()

        @pl.when(odd)
        def _():
            for k in near_ring:
                relay(k).wait_recv()

        for t in range(2):
            got = mail[0, 8 * t : 8 * t + 8, :]
            turned = jnp.zeros((GROUP, along), jnp.float32)
            for d in range(GROUP):
                moved = got if d == 0 else pltpu.roll(pltpu.roll(got, d, 0), along - WORDS * d, 1)
                turned = jnp.where(((sub - lane // WORDS) & 7) == d, moved, turned)
            bundle[t] = turned
        far = jnp.sum(mail[1], axis=0, keepdims=True)
        bundle_far[...] = jnp.where(sub == low, far, 0.0)
        for k in range(1, half):
            parcel_of(k, g).start()

        @pl.when(jnp.logical_not(surface))
        def _():
            parcel_of(0, g).start()

        @pl.when(surface)
        def _():
            heap[0, :, 0:1] = bundle[:, 0:1]

        @pl.when(jnp.logical_not(surface & on_border))
        def _():
            far_parcel(g, low).start()

        @pl.when(surface & on_border)
        def _():
            heap_far[0, border] = bundle_far[...]

    pl.semaphore_wait(barrier, count)

    @pl.when(even)
    def _():
        for k in far_ring:
            direct_letter(k).start()

    @pl.when(odd)
    def _():
        for k in range(-quarter, quarter):
            if k != 0:
                letter(k).start()

    @pl.when(near_side)
    def _():
        for part in range(2):
            to_half_way(part).start()

    begin(0, False)
    begin(0, True)

    @pl.when(forwards)
    def _():
        pl.semaphore_signal(known, inc=1, device_id=on_ring(-quarter), device_id_type=MESH)
        for part in range(2):
            to_half_way(part).wait_recv()
            for number in crossing:
                if (OFFSETS[number][1] != 0) == (part == 1):

                    @pl.when(to_far_side(OFFSETS[number])[0])
                    def _(number=number):
                        onward(number).start()

    @pl.when(even)
    def _():
        own = pl.ds(ring // 2, 1)
        mail[:, own] = letters[:, own]

    @pl.when(odd)
    def _():
        own = pl.ds(2 * quarter, 2)
        transit[:, own] = letters[:, own]
        for k in range(-quarter, quarter):
            if k != 0:
                letter(k).wait_recv()
        for k in near_ring:
            relay(k).start()
        kept = pl.ds(*relay_rows(0))
        mail[:, kept] = transit[:, kept]

    def unpack(turn):
        def pair(kind):
            return jnp.where(lane % 8 < 4, packed[turn, kind, 0], packed[turn, kind, 1])

        plain = pair(0)
        deep = jnp.where((lane // 8) % 8 >= 4, pair(1), pair(2))
        wide = jnp.where(sub < 4, pair(4), pair(3))
        for f in range(2):
            for z in range(depth):
                turnback = (along - 4 - 8 * (f * depth + z)) % along
                edge_y[f, 4 + z] = pltpu.roll(plain, turnback, 1)
                edge_y[f, z - 4 if z >= 4 else 12 + z] = pltpu.roll(deep, turnback, 1)
                edge_xy[f, z] = pltpu.roll(wide, turnback, 1)

    def advance(turn, store):
        def layer(z, _):
            first, whole = [], []
            for f in range(2):
                center = body[turn, f, z + 4]
                beside = side[turn, f, z + 4]
                edge = edge_y[f, z + 4]
                above = [body[turn, f, z + 4 + k] for k in range(1, 5)]
                below = [body[turn, f, z + 4 - k] for k in range(1, 5)]
                u_zz = bend(center, above, below)
                grad_z = slope(above, below)
                grad_z_side = slope(
                    [side[turn, f, z + 4 + k] for k in range(1, 5)],
                    [side[turn, f, z + 4 - k] for k in range(1, 5)],
                )
                grad_z_edge = slope(
                    [edge_y[f, z + 4 + k] for k in range(1, 5)],
                    [edge_y[f, z + 4 - k] for k in range(1, 5)],
                )
                x_moves = shifted(center, beside, 0)
                u_xx = bend(center, *x_moves)
                grad_x = slope(*x_moves)
                grad_x_edge = slope(*shifted(edge, edge_xy[f, z], 0))
                u_yy = bend(center, *shifted(center, edge, 1))
                u_xy = slope(*shifted(grad_x, grad_x_edge, 1))
                u_xz = slope(*shifted(grad_z, grad_z_side, 0))
                u_yz = slope(*shifted(grad_z, grad_z_edge, 1))
                first.append(
                    coef[0, z] * u_xx
                    + coef[1, z] * u_yy
                    + coef[2, z] * u_zz
                    + coef[3, z] * u_xy
                    + coef[4, z] * u_xz
                    + coef[5, z] * u_yz
                )
                whole.append(u_xx + u_yy + u_zz)
            stay = coef[11, z]
            now_p, now_q = body[turn, 0, z + 4], body[turn, 1, z + 4]
            if turn == 0:
                was_p, was_q = old[0, z], old[1, z]
            else:
                was_p, was_q = body[0, 0, z + 4], body[0, 1, z + 4]
            mixed = coef[8, z] * first[1]
            new_p = (
                now_p
                + stay * (now_p - was_p)
                + (coef[6, z] * whole[0] + coef[7, z] * first[0] + mixed)
            )
            new_q = (
                now_q
                + stay * (now_q - was_q)
                + (coef[9, z] * (whole[0] - first[0]) + coef[10, z] * whole[1] + mixed)
            )
            store(z, new_p, new_q)
            return 0

        lax.fori_loop(0, depth, layer, 0, unroll=8)

    def keep(z, new_p, new_q):
        body[1, 0, z + 4] = new_p
        body[1, 1, z + 4] = new_q

    def finish(z, new_p, new_q):
        next_p[z] = new_p
        next_q[z] = new_q

    late = (high == 0) & on_border

    @pl.when(late)
    def _():
        post()

    arrive(0)
    unpack(0)
    advance(0, keep)

    @pl.when(near_side)
    def _():
        pl.semaphore_wait(known, 1)

    begin(1, False)
    pack(1)
    begin(1, True)

    @pl.when(jnp.logical_not(late))
    def _():
        post()

    def add_up(label, values):
        label_x, label_y = label >> 7, label & 127
        pieces = []
        for rest in values:
            for _ in range(3):
                rounded = rest.astype(jnp.bfloat16).astype(jnp.float32)
                pieces.append(rounded)
                rest = rest - rounded
        total = jnp.zeros((len(pieces) * across, along), jnp.float32)
        for r in range(0, 2 * GROUP, 2):

            def flat(array):
                return jnp.concatenate([array[r : r + 1], array[r + 1 : r + 2]], axis=1)

            at_x = iota((across, 2 * along), 0) == flat(label_x)
            left = jnp.concatenate([jnp.where(at_x, flat(piece), 0.0) for piece in pieces], axis=0)
            right = jnp.where(iota((along, 2 * along), 0) == flat(label_y), 1.0, 0.0)
            total = total + lax.dot_general(
                left.astype(jnp.bfloat16),
                right.astype(jnp.bfloat16),
                (((1,), (1,)), ((), ())),
                preferred_element_type=jnp.float32,
            )
        return [
            total[24 * k : 24 * k + 8] + total[24 * k + 8 : 24 * k + 16] + total[24 * k + 16 : 24 * k + 24]
            for k in range(len(values))
        ]

    def plane_there(d, e):
        crosses = jnp.bool_(False)
        if d == 1:
            crosses = i == half - 1
        if d == -1:
            crosses = i == half
        return there((d, e, 0)) & jnp.logical_not(crosses)

    def plane_copy(number):
        d, e = BESIDE[number]
        if e == 0:
            rows = pl.ds(4 if d == 1 else 0, 4)
            source, target = plane.at[0, rows], plane_side.at[rows]
        else:
            source, target = plane_parcel, plane_packed.at[{0: 0, 1: 1, -1: 2}[d], 0 if e == 1 else 1]
        return pltpu.make_async_remote_copy(
            src_ref=source,
            dst_ref=target,
            send_sem=plane_send.at[number],
            recv_sem=plane_recv.at[number],
            device_id=device((d, e, 0)),
            device_id_type=MESH,
        )

    def plane_start(parcels):
        for number, (d, e) in enumerate(BESIDE):
            if (e != 0) == parcels:

                @pl.when(plane_there(d, e))
                def _(number=number):
                    plane_copy(number).start()

    @pl.when(surface)
    def _():
        for layer in range(n_gz):
            for k in range(half):
                if layer > 0 or k > 0:
                    parcel_of(k, layer).wait_recv()
        place = iota((2 * GROUP, along), 1) % WORDS // SLOTS
        parts = [heap[layer].reshape(2 * GROUP, along) for layer in range(4)]

        def gather(kind):
            total = jnp.zeros((2 * GROUP, along), jnp.float32)
            for layer in range(4):
                shift = SLOTS * (layer - kind) % along
                moved = parts[layer] if shift == 0 else pltpu.roll(parts[layer], shift, 1)
                total = jnp.where(place == layer, moved, total)
            return total

        sums = add_up(gather(2).astype(jnp.int32) - 1, [gather(0), gather(1)])
        plane[0] = sums[0]
        plane[1] = sums[1]
        plane_start(False)

    @pl.when(surface & on_border)
    def _():
        for layer in range(n_gz):
            for place in range(half):

                @pl.when((layer > 0) | (border != place))
                def _(layer=layer, place=place):
                    far_parcel(layer, place).wait_recv()

        parts = [jnp.sum(heap_far[layer], axis=0) for layer in range(4)]
        front = lane % 8 < 4
        values, labels = [], []
        for k in (0, 2):
            values.append(jnp.where(front, parts[k], pltpu.roll(parts[k + 1], SLOTS, 1)))
            labels.append(jnp.where(front, pltpu.roll(parts[k], along - SLOTS, 1), parts[k + 1]))
        label = jnp.concatenate(labels, axis=0).astype(jnp.int32) - 1
        [total] = add_up(label, [jnp.concatenate(values, axis=0)])
        plane_far[...] = total

        @pl.when(high == 0)
        def _():
            plane_side[0:4] = total[0:4]

        @pl.when(high != 0)
        def _():
            plane_side[4:8] = total[4:8]

    @pl.when(surface)
    def _():
        plane_parcel[...] = jnp.where(
            lane < 8, pltpu.roll(plane[0], 4, 1), pltpu.roll(plane_far[...], 12, 1)
        )
        plane_start(True)

    depart(1)
    depart(0)

    @pl.when(near_side)
    def _():
        for part in range(2):
            to_half_way(part).wait_send()

    @pl.when(forwards)
    def _():
        for number in crossing:

            @pl.when(to_far_side(OFFSETS[number])[0])
            def _(number=number):
                onward(number).wait_send()

    @pl.when(even)
    def _():
        for k in far_ring:
            direct_letter(k).wait_send()

    @pl.when(odd)
    def _():
        for k in range(-quarter, quarter):
            if k != 0:
                letter(k).wait_send()
        for k in near_ring:
            relay(k).wait_send()

    for k in range(1, half):
        parcel_of(k, g).wait_send()

    @pl.when(jnp.logical_not(surface))
    def _():
        parcel_of(0, g).wait_send()

    @pl.when(jnp.logical_not(surface & on_border))
    def _():
        far_parcel(g, low).wait_send()

    @pl.when(surface)
    def _():
        for number, (d, e) in enumerate(BESIDE):

            @pl.when(plane_there(d, e))
            def _(number=number):
                plane_copy(number).wait_send()

    @pl.when(surface)
    def _():
        for number, (d, e) in enumerate(BESIDE):

            @pl.when(plane_there(-d, -e))
            def _(number=number):
                plane_copy(number).wait_recv()

    arrive(1)
    unpack(1)

    @pl.when(surface)
    def _():
        def pair(kind):
            return jnp.where(lane % 8 < 4, plane_packed[kind, 0], plane_packed[kind, 1])

        same = pair(0)
        edge = pltpu.roll(same, along - 4, 1)
        corner = pltpu.roll(jnp.where(sub < 4, pair(2), pair(1)), along - 4, 1) + pltpu.roll(
            same, along - 12, 1
        )
        for f in range(2):
            body[1, f, 4] = body[1, f, 4] + plane[0]
            side[1, f, 4] = side[1, f, 4] + plane_side[...]
            edge_y[f, 4] = edge_y[f, 4] + edge
            edge_xy[f, 0] = edge_xy[f, 0] + corner

    for f, prior in enumerate((prior_p, prior_q)):
        prior[...] = body[1, f, 4:12]
    advance(1, finish)

    @pl.when(surface)
    def _():
        for result in (next_p, next_q):
            result[0] = result[0] + plane[1]


def hand_over(*refs):
    sources, targets, sem = refs[:4], refs[4:8], refs[8]
    copies = [pltpu.make_async_copy(a, b, sem.at[k]) for k, (a, b) in enumerate(zip(sources, targets))]
    for copy in copies:
        copy.start()
    for copy in copies:
        copy.wait()


def local(sizes, *args):
    fields = args[:11]
    samples, weights, gain, row, column, line = args[11:]
    block = fields[0].shape
    n_traces = samples.shape[0]
    receivers = [ids.reshape(1, -1) for ids in (row, column, line)]
    f32 = jnp.float32
    outs = pl.pallas_call(
        functools.partial(kernel, sizes),
        out_shape=[pltpu.VMEM(block, f32)] * 4,
        in_specs=[pl.BlockSpec(memory_space=pltpu.HBM)] * 17,
        out_specs=[pl.BlockSpec(memory_space=pltpu.VMEM)] * 4,
        scratch_shapes=[
            pltpu.VMEM((2, 2, 16, 8, 128), f32),
            pltpu.VMEM((2, 2, 16, 8, 128), f32),
            pltpu.VMEM((2, 5, 2, 8, 128), f32),
            pltpu.VMEM((2, 8, 128), f32),
            pltpu.VMEM((2, 16, 8, 128), f32),
            pltpu.VMEM((2, 8, 8, 128), f32),
            pltpu.VMEM((2, 8, 8, 128), f32),
            pltpu.VMEM((7, 8, 8, 128), f32),
            pltpu.VMEM((12, 8, 8, 128), f32),
            pltpu.VMEM(samples.shape, f32),
            pltpu.VMEM(weights.shape, f32),
            pltpu.VMEM((1, gain.shape[0]), f32),
            pltpu.VMEM((3, 1, n_traces), jnp.int32),
            pltpu.VMEM((2, RING, 128), f32),
            pltpu.VMEM((2, RING, 128), f32),
            pltpu.VMEM((2, RING, 128), f32),
            pltpu.VMEM((2, 8, 4, 128), f32),
            pltpu.VMEM((8, 128), f32),
            pltpu.VMEM((2, GROUP, 128), f32),
            pltpu.VMEM((8, 128), f32),
            pltpu.VMEM((4, 2, GROUP, 128), f32),
            pltpu.VMEM((4, GROUP, 8, 128), f32),
            pltpu.VMEM((2, 8, 128), f32),
            pltpu.VMEM((8, 128), f32),
            pltpu.VMEM((8, 128), f32),
            pltpu.VMEM((8, 128), f32),
            pltpu.VMEM((3, 2, 8, 128), f32),
            pltpu.SemaphoreType.DMA((17,)),
            pltpu.SemaphoreType.DMA((2, len(OFFSETS))),
            pltpu.SemaphoreType.DMA((2, len(OFFSETS))),
            pltpu.SemaphoreType.DMA((9,)),
            pltpu.SemaphoreType.DMA((9,)),
            pltpu.SemaphoreType.DMA((9,)),
            pltpu.SemaphoreType.DMA((9,)),
            pltpu.SemaphoreType.DMA((GROUP,)),
            pltpu.SemaphoreType.DMA((4, GROUP)),
            pltpu.SemaphoreType.DMA,
            pltpu.SemaphoreType.DMA((4, GROUP)),
            pltpu.SemaphoreType.DMA((8,)),
            pltpu.SemaphoreType.DMA((8,)),
            pltpu.SemaphoreType.DMA((2,)),
            pltpu.SemaphoreType.DMA((2,)),
            pltpu.SemaphoreType.DMA((len(OFFSETS),)),
            pltpu.SemaphoreType.REGULAR,
            pltpu.SemaphoreType.DMA((RING,)),
            pltpu.SemaphoreType.DMA((RING,)),
        ],
        compiler_params=pltpu.CompilerParams(
            collective_id=0, has_side_effects=True, vmem_limit_bytes=60 * 2**20
        ),
        name="wave_steps",
    )(*fields, samples, weights, gain.reshape(1, -1), *receivers)
    return pl.pallas_call(
        hand_over,
        out_shape=[jax.ShapeDtypeStruct(block, f32)] * 4,
        in_specs=[pl.BlockSpec(memory_space=pl.ANY)] * 4,
        out_specs=[pl.BlockSpec(memory_space=pltpu.HBM)] * 4,
        scratch_shapes=[pltpu.SemaphoreType.DMA((4,))],
        compiler_params=pltpu.CompilerParams(vmem_limit_bytes=2**20),
        name="hand_over",
    )(*outs)


def solution(mesh):
    sizes = tuple(mesh.shape[axis] for axis in ("inl", "xl", "gz"))
    cells = P("gz", "inl", "xl")
    traces = P(("inl", "xl", "gz"))
    return jax.shard_map(
        functools.partial(local, sizes),
        mesh=mesh,
        in_specs=(cells,) * 11 + (P(("inl", "xl", "gz"), None), P(), P(), traces, traces, traces),
        out_specs=(cells,) * 4,
        check_vma=False,
    )
```
